512 devices in a mesh: gz: 16 (over z), gy: 32 (over x, y, core).
Axes of the slice: x: 4, y: 4, z: 16, core: 2. Of those that a mesh axis runs over, the one named last changes fastest.
Arguments:
- source: float32 [2, 256, 512, 128], P(None, 'gz', 'gy'), may hold values from -6 to 6
- labels: int32 [256, 512, 128], P('gz', 'gy'), may hold values from 0 to 3
- phase_table: float32 [4, 4], replicated, may hold values from 0.1 to 3
Outputs:
- potential: float32 [2, 256, 512, 128], P(None, 'gz', 'gy')
The draws below stay inside these ranges and needn't reach their ends.
All inputs are finite; a program needn't handle non-finite values.
Results may differ from the reference program's by a relative error of at most 0.000065.
Values sent between devices are 32-bit elements; how exact they have to be, the bound alone decides.
No kernel may reach another device: no remote copies, remote signals or barrier semaphores. Data moves between devices by JAX's collectives and lax.ppermute only.
A program may use at most 128 MiB of HBM per device.

```python
import math
import jax
import jax.numpy as jnp
from jax import lax

PHASES = 4
LEVELS = 4
PRE = 2
POST = 2
COARSE_SWEEPS = 8
NZ = 256
NY = 512
NX = 128


def draw_labels(key, part):
    key = jax.random.fold_in(key, 11)
    block_key = jax.random.fold_in(key, 1)
    rough_key = jax.random.fold_in(key, 2)
    pick_key = jax.random.fold_in(key, 3)
    blocks = jax.random.randint(block_key, (NZ // 16, NY // 16, NX // 16), 0, PHASES, dtype=jnp.int32)
    blocks = jnp.repeat(jnp.repeat(jnp.repeat(blocks, 16, axis=0), 16, axis=1), 16, axis=2)
    rough = jax.random.randint(rough_key, (NZ, NY, NX), 0, PHASES, dtype=jnp.int32)
    picks = jax.random.randint(pick_key, (NZ, NY, NX), 0, 4, dtype=jnp.int32)
    labels = jnp.where(picks == 0, rough, blocks)
    labels = labels.at[0, 0, :PHASES].set(jnp.arange(PHASES, dtype=jnp.int32))
    return labels.astype(jnp.int32)


def level_of(own_key, shape, cuts, low, top_value):
    gain = 1.0
    for dim, blocks in cuts:
        draws = jax.random.uniform(jax.random.fold_in(jax.random.fold_in(own_key, 6), dim), (blocks,), jnp.float32, low / len(cuts), top_value / len(cuts))
        gain = gain * jnp.repeat(jnp.exp(draws), shape[dim] // blocks).reshape((-1,) + (1,) * (len(shape) - 1 - dim))
    return gain


def bell_draw(stream_key, shape, deviation, limit, pieces=(), held_as=jnp.bfloat16):
    drawn = jax.random.normal(stream_key, shape, jnp.float32) * deviation
    if len(pieces) > 0:
        drawn = level_of(stream_key, shape, pieces, -0.22, 0.18) * drawn
    return jnp.clip(drawn, min=-limit, max=limit).astype(held_as)


def setup_inputs(seed: int = 0) -> dict:
    splits = jax.random.split(jax.random.key(seed), 4)
    source = bell_draw(splits[0], (2, NZ, NY, NX), 1.0, 6.0, ((1, 16), (2, 32)), jnp.float32)
    labels = draw_labels(jax.random.fold_in(splits[3], 71), 0)
    phase_table = jnp.clip(jnp.exp(jax.random.uniform(splits[2], (PHASES, 4), jnp.float32, math.log(0.1), math.log(3.0))), 0.1, 3.0)
    return dict(source=source, labels=labels, phase_table=phase_table)


relax = 0.7
mass_scale = 0.01


def coefficients(labels, phase_table):
    scales = jnp.array([1.0, 1.0, mass_scale, mass_scale], jnp.float32)
    scaled = phase_table * scales[None, :]
    phase_ids = jnp.arange(PHASES, dtype=jnp.int32)
    onehot = (labels[None] == phase_ids[:, None, None, None]).astype(jnp.float32)
    return jnp.einsum("pzyx,pc->czyx", onehot, scaled, precision=lax.Precision.HIGHEST)


def neighbours(padded):
    center = padded[:, 1:-1, 1:-1, :]
    xpad = jnp.pad(center, ((0, 0), (0, 0), (0, 0), (1, 1)))
    return [padded[:, :-2, 1:-1, :], padded[:, 2:, 1:-1, :], padded[:, 1:-1, :-2, :], padded[:, 1:-1, 2:, :], xpad[..., :-2], xpad[..., 2:]]


def diagonal(sig_pad):
    center = sig_pad[:, 1:-1, 1:-1, :]
    diag_re = center[2]
    diag_im = center[3]
    for near in neighbours(sig_pad):
        diag_re = diag_re + 0.5 * (center[0] + near[0])
        diag_im = diag_im + 0.5 * (center[1] + near[1])
    return jnp.stack([diag_re, diag_im])


def apply_op(field_pad, sig_pad):
    center = sig_pad[:, 1:-1, 1:-1, :]
    value = field_pad[:, 1:-1, 1:-1, :]
    acc_re = center[2] * value[0] - center[3] * value[1]
    acc_im = center[2] * value[1] + center[3] * value[0]
    for near_s, near_v in zip(neighbours(sig_pad), neighbours(field_pad)):
        face_re = 0.5 * (center[0] + near_s[0])
        face_im = 0.5 * (center[1] + near_s[1])
        diff_re = value[0] - near_v[0]
        diff_im = value[1] - near_v[1]
        acc_re = acc_re + (face_re * diff_re - face_im * diff_im)
        acc_im = acc_im + (face_re * diff_im + face_im * diff_re)
    return jnp.stack([acc_re, acc_im])


def quotient(resid, diag):
    denom = diag[0] * diag[0] + diag[1] * diag[1]
    q_re = (resid[0] * diag[0] + resid[1] * diag[1]) / denom
    q_im = (resid[1] * diag[0] - resid[0] * diag[1]) / denom
    return relax * jnp.stack([q_re, q_im])


def block_sum(field):
    chans, zc, yc, xc = field.shape
    return field.reshape(chans, zc // 2, 2, yc // 2, 2, xc // 2, 2).sum(axis=(2, 4, 6))


def coarse_coeffs(sig):
    mean = block_sum(sig) * 0.125
    return jnp.concatenate([mean[:2], 4.0 * mean[2:]], 0)


def prolong(field):
    return jnp.repeat(jnp.repeat(jnp.repeat(field, 2, axis=1), 2, axis=2), 2, axis=3)


def pad_one(field):
    return jnp.pad(field, ((0, 0), (1, 1), (1, 1), (0, 0)))


def vcycle(level, rhs, sig):
    sig_pad = pad_one(sig)
    diag = diagonal(sig_pad)
    if level == LEVELS:
        guess = quotient(rhs, diag)
        for sweep in range(COARSE_SWEEPS - 1):
            guess = guess + quotient(rhs - apply_op(pad_one(guess), sig_pad), diag)
        return guess
    guess = quotient(rhs, diag)
    for sweep in range(PRE - 1):
        guess = guess + quotient(rhs - apply_op(pad_one(guess), sig_pad), diag)
    resid = rhs - apply_op(pad_one(guess), sig_pad)
    correction = vcycle(level + 1, 0.5 * block_sum(resid), coarse_coeffs(sig))
    guess = guess + prolong(correction)
    for sweep in range(POST):
        guess = guess + quotient(rhs - apply_op(pad_one(guess), sig_pad), diag)
    return guess


def reference(source, labels, phase_table):
    return vcycle(0, source, coefficients(labels, phase_table))
```

```python
import jax
import jax.numpy as jnp
from jax import lax
from jax.experimental import pallas as pl
from jax.experimental.pallas import tpu as pltpu
from jax.sharding import PartitionSpec as P

PHASES = 4
COARSE_SWEEPS = 8
LANES = 128
relax = 0.7
keep = 1.0 - relax
mass_scale = 0.01
F32 = jnp.float32
VMEM_BYTES = 40 * 1024 * 1024


def lanes(rows):
    return lax.broadcasted_iota(jnp.int32, (rows, LANES), 1)


def row_ids(rows):
    return lax.broadcasted_iota(jnp.int32, (rows, LANES), 0)


def ahead_x(q, k):
    return pltpu.roll(q, (-k) % LANES, 1)


def ahead_y(q, k):
    return pltpu.roll(q, (-k) % q.shape[0], 0)


def pair_x(q, k):
    return q + swap_x(q, k)


def swap_x(q, k):
    return jnp.where((lanes(q.shape[0]) & k) == 0, ahead_x(q, k), ahead_x(q, -k))


def interleave(re, im):
    return jnp.where((lanes(re.shape[0]) & 1) == 0, re, im)


def separate(q):
    even = (lanes(q.shape[0]) & 1) == 0
    return jnp.where(even, q, ahead_x(q, -1)), jnp.where(even, ahead_x(q, 1), q)


def each(lo, hi, body, step=2):
    full = (hi - lo) // step

    def run(i, carry):
        for j in range(step):
            body(lo + i * step + j)
        return carry

    lax.fori_loop(0, full, run, 0)
    for z in range(lo + full * step, hi):
        body(z)


def times(t, q):
    return t[0] * q[0] - t[1] * q[1], t[0] * q[1] + t[1] * q[0]


def pair(ref, z):
    return ref[0, z], ref[1, z]


def put(ref, z, q):
    ref[0, z] = q[0]
    ref[1, z] = q[1]


def add(*terms):
    return sum(t[0] for t in terms[1:]) + terms[0][0], sum(t[1] for t in terms[1:]) + terms[0][1]


def both(fn, q, k):
    return fn(q[0], k), fn(q[1], k)


def inside(rows, wrap, z, first_z, first_y, size_z, size_y, dead=()):
    r = row_ids(rows)
    y = jnp.where(r >= wrap, r - rows, r) + first_y
    ok = (y >= 0) & (y < size_y)
    plane = jnp.full((rows, LANES), first_z + z, jnp.int32)
    ok = ok & (plane >= 0) & (plane < size_z)
    if dead:
        ok = ok & ((r < dead[0]) | (r >= dead[1]))
    return ok


def make_faces(z, shift, ok, s, m, tz, ty, tx, w, g=None):
    lane = lanes(s.shape[2])
    last = lane >= LANES - shift
    initial = lane < shift
    diag = []
    for c in (0, 1):
        here = s[c, z]
        up = 0.5 * (here + s[c, z + 1])
        down = 0.5 * (here + s[c, z - 1])
        side = 0.5 * (here + ahead_y(here, 1))
        right = 0.5 * (here + jnp.where(last, 0.0, ahead_x(here, shift)))
        left = 0.5 * (here + jnp.where(initial, 0.0, ahead_x(here, -shift)))
        tz[c, z] = up
        ty[c, z] = side
        tx[c, z] = jnp.where(last, 0.0, right)
        diag.append(m[c, z] + (up + down) + (side + ahead_y(side, -1)) + (right + left))
    inv = jnp.where(ok, relax / (diag[0] * diag[0] + diag[1] * diag[1]), 0.0)
    q = (diag[0] * inv, -(diag[1] * inv))
    put(w, z, q)
    if g is not None:
        put(g, z, diag)
    return q


def inflow(z, shift, v, tz, ty, tx):
    here = pair(v, z)
    side, right = pair(ty, z), pair(tx, z)
    return add(
        times(pair(tz, z), pair(v, z + 1)),
        times(pair(tz, z - 1), pair(v, z - 1)),
        times(side, both(ahead_y, here, 1)),
        both(ahead_y, times(side, here), -1),
        times(right, both(ahead_x, here, shift)),
        both(ahead_x, times(right, here), -shift),
    )


def swept(z, shift, v, f, tz, ty, tx, w):
    here = pair(v, z)
    step = times(pair(w, z), add(pair(f, z), inflow(z, shift, v, tz, ty, tx)))
    return keep * here[0] + step[0], keep * here[1] + step[1]


def residual(z, shift, v, f, tz, ty, tx, g):
    out = times(pair(g, z), pair(v, z))
    gain = add(pair(f, z), inflow(z, shift, v, tz, ty, tx))
    return gain[0] - out[0], gain[1] - out[1]


def rows_paired(buf, at, start, count):
    plane = buf.at[at]
    return plane[pl.ds(start, count, stride=2), :] + plane[pl.ds(start + 1, count, stride=2), :]


def packed_row(stack):
    lane, row = lanes(8), row_ids(8)
    cells = jnp.take_along_axis(stack, 8 * (lane % 16), axis=1)
    return jnp.sum(jnp.where(lane // 16 == row, cells, 0.0), axis=0, keepdims=True)


def lookup(lab, table):
    out = []
    for c in range(4):
        scale = 1.0 if c < 2 else mass_scale
        val = [table[p, c] * F32(scale) for p in range(PHASES)]
        out.append(jnp.where(lab == 0, val[0], jnp.where(lab == 1, val[1], jnp.where(lab == 2, val[2], val[3]))))
    return out


def coeff_kernel(labels, table, near_out, far_out, buf, c1, c2, stack):
    for z in range(8):
        a, b = lookup(labels[2 * z], table), lookup(labels[2 * z + 1], table)
        for c in range(4):
            buf[c, z] = a[c] + b[c]
    for z in range(8):
        for c in range(4):
            c1[c, z] = pair_x(rows_paired(buf, (c, z), 0, 8), 1) * (0.125 if c < 2 else 0.5)
    for z in range(8):
        near_out[0, z] = interleave(c1[0, z], c1[1, z])
        near_out[1, z] = interleave(c1[2, z], c1[3, z])
    for c in range(4):
        scale = 0.125 if c < 2 else 0.5
        for z in range(4):
            buf[c, z, 0:8] = c1[c, 2 * z] + c1[c, 2 * z + 1]
        for z in range(4):
            c2[c, z] = pair_x(rows_paired(buf, (c, z), 0, 4), 2) * scale
        for z in range(2):
            buf[c, 4 + z, 0:4] = c2[c, 2 * z] + c2[c, 2 * z + 1]
        for z in range(2):
            stack[c // 2, (c % 2) * 4 + 2 * z : (c % 2) * 4 + 2 * z + 2] = (
                pair_x(rows_paired(buf, (c, 4 + z), 0, 2), 4) * scale
            )
    far_out[:, 0:LANES] = packed_row(stack[0])
    far_out[:, LANES : 2 * LANES] = packed_row(stack[1])


def fine_kernel(sizes, mid, left, right, table, rhs_out, v, f, tz, ty, tx, w, lab, s, m, g, first, buf):
    first_z = lax.axis_index("gz") * 16 - 4
    first_y = lax.axis_index("gy") * 16

    def load(z):
        for c, ref in ((0, f), (1, f), (2, None)):
            dst = lab.at[z] if ref is None else ref.at[c, z]
            dst[0:16] = mid[c, z]
            dst[16:20] = right[c, z]
            dst[20:24] = left[c, z]
        ok = inside(24, 20, z, first_z, first_y, *sizes)
        vals = lookup(lab[z], table)
        for c in (0, 1):
            s[c, z] = jnp.where(ok, vals[c], 0.0)
            m[c, z] = vals[2 + c]

    each(0, 24, load)

    def faces(z):
        ok = inside(24, 20, z, first_z, first_y, *sizes)
        put(first, z, times(make_faces(z, 1, ok, s, m, tz, ty, tx, w, g), pair(f, z)))

    each(1, 23, faces)
    each(2, 22, lambda z: put(v, z, swept(z, 1, first, f, tz, ty, tx, w)))

    def restrict(z):
        a = residual(2 * z + 4, 1, v, f, tz, ty, tx, g)
        b = residual(2 * z + 5, 1, v, f, tz, ty, tx, g)
        put(buf, z, add(a, b))

    each(0, 8, restrict, 1)

    def finish(z):
        re, im = (0.5 * pair_x(rows_paired(buf, (c, z), 0, 8), 1) for c in (0, 1))
        rhs_out[z] = interleave(re, im)

    each(0, 8, finish)


def middle_kernel(
    sizes, dmid, dleft, dright, bmid, bleft, bright,
    row_out, c_out, v, f, tz, ty, tx, w, tz2, ty2, tx2, w2,
    s, m, g, first, buf, s2, m2, f2, g2, first2, v2, buf2, stack,
):
    gz, gy = lax.axis_index("gz"), lax.axis_index("gy")

    def load(z):
        for lo, d, b in ((0, dmid, bmid), (8, dright, bright), (16, dleft, bleft)):
            for ref, q in ((s, d[0, z]), (m, d[1, z]), (f, b[z])):
                re, im = separate(q)
                ref[0, z, lo : lo + 8] = re
                ref[1, z, lo : lo + 8] = im

    each(0, 24, load)

    def faces(z):
        ok = inside(24, 16, z, gz * 8 - 8, gy * 8, *sizes[0])
        put(first, z, times(make_faces(z, 2, ok, s, m, tz, ty, tx, w, g), pair(f, z)))

    each(1, 23, faces)
    each(2, 22, lambda z: put(v, z, swept(z, 2, first, f, tz, ty, tx, w)))

    def coarser(dst, scale, z):
        for c in (0, 1):
            dst[c, z, 0:8] = scale * pair_x(rows_paired(buf, (c, z), 0, 8), 2)
            dst[c, z, 8:12] = jnp.zeros((4, LANES), F32)
            dst[c, z, 12:16] = scale * pair_x(rows_paired(buf, (c, z), 16, 4), 2)

    for src, dst, scale in ((s, s2, 0.125), (m, m2, 0.5)):
        each(0, 12, lambda z: put(buf, z, add(pair(src, 2 * z), pair(src, 2 * z + 1))))
        each(0, 12, lambda z: coarser(dst, scale, z))

    def restrict(z):
        put(buf, z, add(residual(2 * z, 2, v, f, tz, ty, tx, g), residual(2 * z + 1, 2, v, f, tz, ty, tx, g)))

    each(2, 10, restrict, 1)
    each(2, 10, lambda z: coarser(f2, 0.5, z))

    def faces2(z):
        ok = inside(16, 12, z, gz * 4 - 4, gy * 4, *sizes[1], dead=(8, 12))
        return make_faces(z, 4, ok, s2, m2, tz2, ty2, tx2, w2, g2)

    faces2(1)
    tz2[0, 0] = 0.5 * (s2[0, 0] + s2[0, 1])
    tz2[1, 0] = 0.5 * (s2[1, 0] + s2[1, 1])
    each(2, 10, lambda z: put(first2, z, times(faces2(z), pair(f2, z))))
    faces2(10)
    each(3, 9, lambda z: put(v2, z, swept(z, 4, first2, f2, tz2, ty2, tx2, w2)))
    which = lanes(4) & 3
    for z in range(4):
        a, b = pair(v2, z + 4), pair(f2, z + 4)
        c_out[z] = jnp.where(
            which < 2, jnp.where(which == 0, a[0][0:4], a[1][0:4]), jnp.where(which == 2, b[0][0:4], b[1][0:4])
        )
    for z in range(2):
        a = residual(2 * z + 4, 4, v2, f2, tz2, ty2, tx2, g2)
        b = residual(2 * z + 5, 4, v2, f2, tz2, ty2, tx2, g2)
        put(buf2, z, add(a, b))
    for z in range(2):
        for c in (0, 1):
            stack[4 * c + 2 * z : 4 * c + 2 * z + 2] = 0.5 * pair_x(rows_paired(buf2, (c, z), 0, 2), 4)
    row_out[...] = packed_row(stack[...])


def real_lanes(rows):
    return lanes(rows) < 64


def flip(q):
    return pltpu.roll(q, 64, 1)


def as_factors(q):
    real, other = real_lanes(q.shape[0]), flip(q)
    return jnp.where(real, q, other), jnp.where(real, -other, q)


def product(a, b, q):
    return a * q + b * flip(q)


def shifted_rows(q, k):
    edge = q.shape[0] - 1 if k > 0 else 0
    return jnp.where(row_ids(q.shape[0]) == edge, 0.0, ahead_y(q, k))


def near_level3(ref, p):
    q = ref[p]
    lane = lanes(q.shape[0])
    low_z, low_y, x = (lane & 32) == 0, (lane & 16) == 0, lane & 15
    qz, qy = swap_x(q, 32), swap_x(q, 16)
    return (
        jnp.where(low_z, qz, swap_x(ref[p + 1], 32)),
        jnp.where(low_z, swap_x(ref[p - 1], 32), qz),
        jnp.where(low_y, qy, shifted_rows(qy, 1)),
        jnp.where(low_y, shifted_rows(qy, -1), qy),
        jnp.where(x == 15, 0.0, ahead_x(q, 1)),
        jnp.where(x == 0, 0.0, ahead_x(q, -1)),
    )


def near_level4(ref, p):
    q = ref[p]
    x = lanes(q.shape[0]) & 15
    return (
        ref[p + 1],
        ref[p - 1],
        shifted_rows(q, 1),
        shifted_rows(q, -1),
        jnp.where(x >= 14, 0.0, ahead_x(q, 2)),
        jnp.where(x < 2, 0.0, ahead_x(q, -2)),
    )


def set_level(near, s, ps, m, t, w, g, p):
    here = s[ps]
    diag = m
    for i, other in enumerate(near(s, ps)):
        face = 0.5 * (here + other)
        diag = diag + face
        t[2 * i, p], t[2 * i + 1, p] = as_factors(face)
    real, other = real_lanes(here.shape[0]), flip(diag)
    inv = relax / (diag * diag + other * other)
    w[0, p] = jnp.where(real, diag, other) * inv
    w[1, p] = jnp.where(real, other, -diag) * inv
    if g is not None:
        g[0, p], g[1, p] = as_factors(diag)


def gathered_inflow(near, v, pv, t, p):
    total = None
    for i, q in enumerate(near(v, pv)):
        term = product(t[2 * i, p], t[2 * i + 1, p], q)
        total = term if total is None else total + term
    return total


def eightfold(q):
    return pair_x(pair_x(pair_x(q, 32), 16), 1)


def coarse_solve(counts, rhs, coef, s3, s4, t3, w3, g3, t4, w4, f4, va, vb, ea, eb, near_out):
    nz, ny = counts
    zero = jnp.zeros((ny, LANES), F32)
    for ref in (s3, s4, ea, eb):
        ref[0] = zero
        ref[nz + 1] = zero
    for ref in (va, vb):
        for p in (0, 1, 2, nz + 3, nz + 4, nz + 5):
            ref[p] = zero
    for p in (0, 1, nz + 2, nz + 3):
        for i in range(12):
            t3[i, p] = zero
        w3[0, p] = zero
        w3[1, p] = zero

    def load(p):
        q = coef[p, :, 0:LANES]
        s3[p + 1] = q
        s4[p + 1] = 0.125 * eightfold(q)

    each(0, nz, load)

    def setup(p):
        q = coef[p, :, LANES : 2 * LANES]
        set_level(near_level3, s3, p + 1, q, t3, w3, g3, p + 2)
        set_level(near_level4, s4, p + 1, 0.5 * eightfold(q), t4, w4, None, p)
        va[p + 3] = product(w3[0, p + 2], w3[1, p + 2], rhs[p])

    each(0, nz, setup, 1)

    def sweep3(src, p):
        gain = rhs[jnp.clip(p, 0, nz - 1)] + gathered_inflow(near_level3, src, p + 3, t3, p + 2)
        return keep * src[p + 3] + product(w3[0, p + 2], w3[1, p + 2], gain)

    def pre(p):
        vb[p + 3] = sweep3(va, p)

    each(0, nz, pre, 1)

    def restrict(p):
        gain = rhs[p] + gathered_inflow(near_level3, vb, p + 3, t3, p + 2)
        gain = 0.5 * eightfold(gain - product(g3[0, p + 2], g3[1, p + 2], vb[p + 3]))
        f4[p] = gain
        ea[p + 1] = product(w4[0, p], w4[1, p], gain)

    each(0, nz, restrict, 1)
    src, dst = ea, eb
    for sweep in range(COARSE_SWEEPS - 1):

        def relaxed(p, src=src, dst=dst):
            gain = f4[p] + gathered_inflow(near_level4, src, p + 1, t4, p)
            dst[p + 1] = keep * src[p + 1] + product(w4[0, p], w4[1, p], gain)

        each(0, nz, relaxed, 2)
        src, dst = dst, src

    def correct(p):
        vb[p + 3] = vb[p + 3] + src[p + 1]

    each(0, nz, correct)
    mine = lax.axis_index("gz")
    for d in range(-2, 3):
        va[mine + d + 3] = sweep3(vb, mine + d)
    for d in range(-1, 2):
        near_out[d + 1] = sweep3(va, mine + d)


def up_kernel(
    counts, rhs, coef, cmid, cleft, cright, tz2, ty2, tx2, w2, v1, f1, tz1, ty1, tx1, w1, v0, f0, tz0, ty0, tx0, w0, out,
    s3, s4, t3, w3, g3, t4, w4, f4, va, vb, ea, eb, near, a2, b2, f2, e1, a1, b1, e0, a0, b0,
):
    ny = counts[1]
    gy = lax.axis_index("gy")
    coarse_solve(counts, rhs, coef, s3, s4, t3, w3, g3, t4, w4, f4, va, vb, ea, eb, near)

    lane4, zero4 = lanes(4), jnp.zeros((4, LANES), F32)

    def unpack(z):
        for ref in (a2, f2):
            for c in (0, 1):
                ref[c, z, 8:12] = zero4
        for lo, src in ((0, cmid), (4, cright), (12, cleft)):
            q = src[z]
            turned = {k: ahead_x(q, k) if k else q for k in range(-3, 4)}
            for k, (ref, c) in enumerate(((a2, 0), (a2, 1), (f2, 0), (f2, 1))):
                val = turned[k]
                for i in range(1, 4):
                    val = jnp.where((lane4 & 3) == i, turned[k - i], val)
                ref[c, z, lo : lo + 4] = val

    each(0, 12, unpack)
    r16, l16 = row_ids(16), lanes(16)
    cell = 16 * ((r16 // 2) & 1) + l16 // 8
    for d in range(3):
        own = near[d, pl.ds(gy, 1), :]
        after = near[d, pl.ds(jnp.minimum(gy + 1, ny - 1), 1), :] * jnp.where(gy == ny - 1, 0.0, 1.0)
        before = near[d, pl.ds(jnp.maximum(gy - 1, 0), 1), :] * jnp.where(gy == 0, 0.0, 1.0)
        rows = jnp.where(r16 < 4, own, jnp.where(r16 < 8, after, jnp.where(r16 < 12, 0.0, before)))
        for c in (0, 1):
            for zz in (0, 1):
                corr = jnp.take_along_axis(rows, cell + (64 * c + 32 * zz), axis=1)
                for z in (4 * d + 2 * zz, 4 * d + 2 * zz + 1):
                    a2[c, z] = a2[c, z] + corr

    each(1, 11, lambda z: put(b2, z, swept(z, 4, a2, f2, tz2, ty2, tx2, w2)))
    each(2, 10, lambda z: put(a2, z, swept(z, 4, b2, f2, tz2, ty2, tx2, w2)))

    def widen1(z):
        for c in (0, 1):
            q = a2[c, z]
            for k in (0, 1):
                e1.at[c, z][pl.ds(k, 8, stride=2), :] = q[0:8]
                e1.at[c, z][pl.ds(16 + k, 4, stride=2), :] = q[12:16]

    each(2, 10, widen1)
    each(5, 19, lambda z: put(a1, z, add(pair(v1, z), pair(e1, z // 2))))
    each(6, 18, lambda z: put(b1, z, swept(z, 2, a1, f1, tz1, ty1, tx1, w1)))
    each(7, 17, lambda z: put(a1, z, swept(z, 2, b1, f1, tz1, ty1, tx1, w1)))

    def widen0(z):
        for c in (0, 1):
            q = a1[c, z]
            for k in (0, 1):
                e0.at[c, z][pl.ds(k, 8, stride=2), :] = q[0:8]
                e0.at[c, z][pl.ds(16 + k, 2, stride=2), :] = q[8:10]
                e0.at[c, z][pl.ds(20 + k, 2, stride=2), :] = q[22:24]

    each(7, 17, widen0)
    each(2, 22, lambda z: put(a0, z, add(pair(v0, z), pair(e0, z // 2 + 6))))
    each(3, 21, lambda z: put(b0, z, swept(z, 1, a0, f0, tz0, ty0, tx0, w0)))

    def last(z):
        q = swept(z, 1, b0, f0, tz0, ty0, tx0, w0)
        out[0, z - 4] = q[0][0:16]
        out[1, z - 4] = q[1][0:16]

    each(4, 20, last)


def spec_all(n, smem=()):
    return [pl.BlockSpec(memory_space=pltpu.SMEM if i in smem else pltpu.VMEM) for i in range(n)]


def run(kernel, name, args, outs, scratch, smem=()):
    shapes = [jax.ShapeDtypeStruct(s, F32) for s in outs]
    return pl.pallas_call(
        kernel,
        name=name,
        out_shape=shapes,
        in_specs=spec_all(len(args), smem),
        out_specs=spec_all(len(outs)),
        scratch_shapes=[pltpu.VMEM(s, F32) for s in scratch],
        compiler_params=pltpu.CompilerParams(vmem_limit_bytes=VMEM_BYTES),
    )(*args)


def shifts(axis):
    n = lax.axis_size(axis)
    up = [(i, i + 1) for i in range(n - 1)]
    return up, [(j, i) for i, j in up]


def around(block, axis, dim, width):
    up, down = shifts(axis)
    size = block.shape[dim]
    before = lax.ppermute(lax.slice_in_dim(block, size - width, size, axis=dim), axis, up)
    after = lax.ppermute(lax.slice_in_dim(block, 0, width, axis=dim), axis, down)
    return before, after


def window(block, dim, width):
    before, after = around(block, "gz", dim, width)
    mid = jnp.concatenate([before, block, after], axis=dim)
    left, right = around(mid, "gy", dim + 1, width)
    return mid, left, right


def body(source, labels, phase_table):
    nz, ny = lax.axis_size("gz"), lax.axis_size("gy")
    lab = labels.astype(jnp.int32)
    near_c, far_c = run(
        coeff_kernel, "coefficients", (lab, phase_table),
        [(2, 8, 8, LANES), (1, 2 * LANES)],
        [(4, 8, 16, LANES), (4, 8, 8, LANES), (4, 4, 4, LANES), (2, 8, LANES)], smem=(1,),
    )
    far_c = lax.all_gather(far_c, ("gz", "gy"), axis=0, tiled=True).reshape(nz, ny, 2 * LANES)
    fine = jnp.concatenate([source, labels.astype(F32)[None]], axis=0)
    coef1 = window(near_c, 1, 8)

    win = (2, 24, 24, LANES)
    rhs1, *state0 = run(
        lambda *refs: fine_kernel((16 * nz, 16 * ny), *refs), "fine_down", (*window(fine, 1, 4), phase_table),
        [(8, 8, LANES)] + [win] * 6,
        [(24, 24, LANES)] + [win] * 4 + [(2, 8, 24, LANES)], smem=(3,),
    )
    win2 = (2, 12, 16, LANES)
    row, c_own, *state = run(
        lambda *refs: middle_kernel(((8 * nz, 8 * ny), (4 * nz, 4 * ny)), *refs), "middle_down",
        (*coef1, *window(rhs1, 0, 8)),
        [(1, LANES), (4, 4, LANES)] + [win] * 6 + [win2] * 4,
        [win] * 4 + [(2, 12, 24, LANES)] + [win2] * 6 + [(2, 2, 16, LANES), (8, LANES)],
    )
    state1, state2 = state[:6], state[6:]
    rhs3 = lax.all_gather(row, ("gz", "gy"), axis=0, tiled=True).reshape(nz, ny, LANES)
    cwin = window(c_own, 0, 4)

    def whole(n, pad):
        return (n, nz + 2 * pad, ny, LANES)

    return run(
        lambda *refs: up_kernel((nz, ny), *refs), "coarse_and_up",
        (rhs3, far_c, *cwin, *state2, *state1, *state0),
        [(2, 16, 16, LANES)],
        [whole(1, 1)[1:]] * 2
        + [whole(12, 2), whole(2, 2), whole(2, 2), whole(12, 0), whole(2, 0), whole(1, 0)[1:]]
        + [whole(1, 3)[1:]] * 2 + [whole(1, 1)[1:]] * 2 + [(3, ny, LANES)]
        + [win2] * 3 + [(2, 12, 24, LANES), win, win, win, win, win],
    )[0]


def solution(mesh):
    in_specs = (P(None, "gz", "gy", None), P("gz", "gy", None), P())
    out_specs = P(None, "gz", "gy", None)
    return jax.shard_map(body, mesh=mesh, in_specs=in_specs, out_specs=out_specs, check_vma=False)
```

```python
import jax
import jax.numpy as jnp
from jax import lax
from jax.experimental import pallas as pl
from jax.experimental.pallas import tpu as pltpu
from jax.sharding import PartitionSpec as P

PHASES = 4
COARSE_SWEEPS = 8
LANES = 128
relax = 0.7
keep = 1.0 - relax
mass_scale = 0.01
F32 = jnp.float32
VMEM_BYTES = 40 * 1024 * 1024


def lanes(rows):
    return lax.broadcasted_iota(jnp.int32, (rows, LANES), 1)


def row_ids(rows):
    return lax.broadcasted_iota(jnp.int32, (rows, LANES), 0)


def ahead_x(q, k):
    return pltpu.roll(q, (-k) % LANES, 1)


def ahead_y(q, k):
    return pltpu.roll(q, (-k) % q.shape[0], 0)


def pair_x(q, k):
    return q + swap_x(q, k)


def swap_x(q, k):
    return jnp.where((lanes(q.shape[0]) & k) == 0, ahead_x(q, k), ahead_x(q, -k))


def interleave(re, im):
    return jnp.where((lanes(re.shape[0]) & 1) == 0, re, im)


def separate(q):
    even = (lanes(q.shape[0]) & 1) == 0
    return jnp.where(even, q, ahead_x(q, -1)), jnp.where(even, ahead_x(q, 1), q)


def each(lo, hi, body, step=4):
    full = (hi - lo) // step

    def run(i, carry):
        for j in range(step):
            body(lo + i * step + j)
        return carry

    lax.fori_loop(0, full, run, 0)
    for z in range(lo + full * step, hi):
        body(z)


def times(t, q):
    return t[0] * q[0] - t[1] * q[1], t[0] * q[1] + t[1] * q[0]


def pair(ref, z):
    return ref[0, z], ref[1, z]


def put(ref, z, q):
    ref[0, z] = q[0]
    ref[1, z] = q[1]


def add(*terms):
    return sum(t[0] for t in terms[1:]) + terms[0][0], sum(t[1] for t in terms[1:]) + terms[0][1]


def both(fn, q, k):
    return fn(q[0], k), fn(q[1], k)


def inside(rows, wrap, z, first_z, first_y, size_z, size_y, dead=()):
    r = row_ids(rows)
    y = jnp.where(r >= wrap, r - rows, r) + first_y
    ok = (y >= 0) & (y < size_y)
    plane = jnp.full((rows, LANES), first_z + z, jnp.int32)
    ok = ok & (plane >= 0) & (plane < size_z)
    if dead:
        ok = ok & ((r < dead[0]) | (r >= dead[1]))
    return ok


def make_faces(z, shift, ok, s, m, tz, ty, tx, w, g=None):
    lane = lanes(s.shape[2])
    last = lane >= LANES - shift
    initial = lane < shift
    diag = []
    for c in (0, 1):
        here = s[c, z]
        up = 0.5 * (here + s[c, z + 1])
        down = 0.5 * (here + s[c, z - 1])
        side = 0.5 * (here + ahead_y(here, 1))
        right = 0.5 * (here + jnp.where(last, 0.0, ahead_x(here, shift)))
        left = 0.5 * (here + jnp.where(initial, 0.0, ahead_x(here, -shift)))
        tz[c, z] = up
        ty[c, z] = side
        tx[c, z] = jnp.where(last, 0.0, right)
        diag.append(m[c, z] + (up + down) + (side + ahead_y(side, -1)) + (right + left))
    inv = jnp.where(ok, relax / (diag[0] * diag[0] + diag[1] * diag[1]), 0.0)
    q = (diag[0] * inv, -(diag[1] * inv))
    put(w, z, q)
    if g is not None:
        put(g, z, diag)
    return q


def inflow(z, shift, v, tz, ty, tx):
    here = pair(v, z)
    side, right = pair(ty, z), pair(tx, z)
    return add(
        times(pair(tz, z), pair(v, z + 1)),
        times(pair(tz, z - 1), pair(v, z - 1)),
        times(side, both(ahead_y, here, 1)),
        both(ahead_y, times(side, here), -1),
        times(right, both(ahead_x, here, shift)),
        both(ahead_x, times(right, here), -shift),
    )


def swept(z, shift, v, f, tz, ty, tx, w):
    here = pair(v, z)
    step = times(pair(w, z), add(pair(f, z), inflow(z, shift, v, tz, ty, tx)))
    return keep * here[0] + step[0], keep * here[1] + step[1]


def residual(z, shift, v, f, tz, ty, tx, g):
    out = times(pair(g, z), pair(v, z))
    gain = add(pair(f, z), inflow(z, shift, v, tz, ty, tx))
    return gain[0] - out[0], gain[1] - out[1]


def rows_paired(buf, at, start, count):
    plane = buf.at[at]
    return plane[pl.ds(start, count, stride=2), :] + plane[pl.ds(start + 1, count, stride=2), :]


def packed_row(stack):
    lane, row = lanes(8), row_ids(8)
    cells = jnp.take_along_axis(stack, 8 * (lane % 16), axis=1)
    return jnp.sum(jnp.where(lane // 16 == row, cells, 0.0), axis=0, keepdims=True)


def lookup(lab, table):
    out = []
    for c in range(4):
        scale = 1.0 if c < 2 else mass_scale
        val = [table[p, c] * F32(scale) for p in range(PHASES)]
        out.append(jnp.where(lab == 0, val[0], jnp.where(lab == 1, val[1], jnp.where(lab == 2, val[2], val[3]))))
    return out


def coeff_kernel(labels, table, near_out, far_out, buf, c1, c2, stack):
    for z in range(8):
        a, b = lookup(labels[2 * z], table), lookup(labels[2 * z + 1], table)
        for c in range(4):
            buf[c, z] = a[c] + b[c]
    for z in range(8):
        for c in range(4):
            c1[c, z] = pair_x(rows_paired(buf, (c, z), 0, 8), 1) * (0.125 if c < 2 else 0.5)
    for z in range(8):
        near_out[0, z] = interleave(c1[0, z], c1[1, z])
        near_out[1, z] = interleave(c1[2, z], c1[3, z])
    for c in range(4):
        scale = 0.125 if c < 2 else 0.5
        for z in range(4):
            buf[c, z, 0:8] = c1[c, 2 * z] + c1[c, 2 * z + 1]
        for z in range(4):
            c2[c, z] = pair_x(rows_paired(buf, (c, z), 0, 4), 2) * scale
        for z in range(2):
            buf[c, 4 + z, 0:4] = c2[c, 2 * z] + c2[c, 2 * z + 1]
        for z in range(2):
            stack[c // 2, (c % 2) * 4 + 2 * z : (c % 2) * 4 + 2 * z + 2] = (
                pair_x(rows_paired(buf, (c, 4 + z), 0, 2), 4) * scale
            )
    far_out[:, 0:LANES] = packed_row(stack[0])
    far_out[:, LANES : 2 * LANES] = packed_row(stack[1])


def fine_kernel(sizes, mid, left, right, table, near_c, msg_out, v, f, tz, ty, tx, w, lab, s, m, g, first, buf):
    first_z = lax.axis_index("gz") * 16 - 4
    first_y = lax.axis_index("gy") * 16

    def load(z):
        for c, ref in ((0, f), (1, f), (2, None)):
            dst = lab.at[z] if ref is None else ref.at[c, z]
            dst[0:16] = mid[c, z]
            dst[16:20] = right[c, z]
            dst[20:24] = left[c, z]
        ok = inside(24, 20, z, first_z, first_y, *sizes)
        vals = lookup(lab[z], table)
        for c in (0, 1):
            s[c, z] = jnp.where(ok, vals[c], 0.0)
            m[c, z] = vals[2 + c]

    each(0, 24, load)

    def faces(z):
        ok = inside(24, 20, z, first_z, first_y, *sizes)
        put(first, z, times(make_faces(z, 1, ok, s, m, tz, ty, tx, w, g), pair(f, z)))

    each(1, 23, faces)
    each(2, 22, lambda z: put(v, z, swept(z, 1, first, f, tz, ty, tx, w)))

    def restrict(z):
        a = residual(2 * z + 4, 1, v, f, tz, ty, tx, g)
        b = residual(2 * z + 5, 1, v, f, tz, ty, tx, g)
        put(buf, z, add(a, b))

    each(0, 8, restrict, 2)

    def finish(z):
        re, im = (0.5 * pair_x(rows_paired(buf, (c, z), 0, 8), 1) for c in (0, 1))
        msg_out[2, z] = interleave(re, im)
        msg_out[0, z] = near_c[0, z]
        msg_out[1, z] = near_c[1, z]

    each(0, 8, finish)


def middle_kernel(
    sizes, mid, left, right, far_c,
    row_out, c_out, v, f, tz, ty, tx, w, tz2, ty2, tx2, w2,
    s, m, g, first, buf, s2, m2, f2, g2, first2, v2, buf2, stack,
):
    gz, gy = lax.axis_index("gz"), lax.axis_index("gy")

    def load(z):
        for lo, src in ((0, mid), (8, right), (16, left)):
            for i, ref in enumerate((s, m, f)):
                re, im = separate(src[i, z])
                ref[0, z, lo : lo + 8] = re
                ref[1, z, lo : lo + 8] = im

    each(0, 24, load)

    def faces(z):
        ok = inside(24, 16, z, gz * 8 - 8, gy * 8, *sizes[0])
        put(first, z, times(make_faces(z, 2, ok, s, m, tz, ty, tx, w, g), pair(f, z)))

    each(1, 23, faces)
    each(2, 22, lambda z: put(v, z, swept(z, 2, first, f, tz, ty, tx, w)))

    def coarser(dst, scale, z):
        for c in (0, 1):
            dst[c, z, 0:8] = scale * pair_x(rows_paired(buf, (c, z), 0, 8), 2)
            dst[c, z, 8:12] = jnp.zeros((4, LANES), F32)
            dst[c, z, 12:16] = scale * pair_x(rows_paired(buf, (c, z), 16, 4), 2)

    for src, dst, scale in ((s, s2, 0.125), (m, m2, 0.5)):
        each(0, 12, lambda z: put(buf, z, add(pair(src, 2 * z), pair(src, 2 * z + 1))))
        each(0, 12, lambda z: coarser(dst, scale, z))

    def restrict(z):
        put(buf, z, add(residual(2 * z, 2, v, f, tz, ty, tx, g), residual(2 * z + 1, 2, v, f, tz, ty, tx, g)))

    each(2, 10, restrict, 2)
    each(2, 10, lambda z: coarser(f2, 0.5, z))

    def faces2(z):
        ok = inside(16, 12, z, gz * 4 - 4, gy * 4, *sizes[1], dead=(8, 12))
        return make_faces(z, 4, ok, s2, m2, tz2, ty2, tx2, w2, g2)

    faces2(1)
    tz2[0, 0] = 0.5 * (s2[0, 0] + s2[0, 1])
    tz2[1, 0] = 0.5 * (s2[1, 0] + s2[1, 1])
    each(2, 10, lambda z: put(first2, z, times(faces2(z), pair(f2, z))))
    faces2(10)
    each(3, 9, lambda z: put(v2, z, swept(z, 4, first2, f2, tz2, ty2, tx2, w2)))
    which = lanes(4) & 3
    for z in range(4):
        a, b = pair(v2, z + 4), pair(f2, z + 4)
        c_out[z] = jnp.where(
            which < 2, jnp.where(which == 0, a[0][0:4], a[1][0:4]), jnp.where(which == 2, b[0][0:4], b[1][0:4])
        )
    for z in range(2):
        a = residual(2 * z + 4, 4, v2, f2, tz2, ty2, tx2, g2)
        b = residual(2 * z + 5, 4, v2, f2, tz2, ty2, tx2, g2)
        put(buf2, z, add(a, b))
    for z in range(2):
        for c in (0, 1):
            stack[4 * c + 2 * z : 4 * c + 2 * z + 2] = 0.5 * pair_x(rows_paired(buf2, (c, z), 0, 2), 4)
    row_out[:, 0:LANES] = packed_row(stack[...])
    row_out[:, LANES : 3 * LANES] = far_c[...]


def real_lanes(rows):
    return lanes(rows) < 64


def flip(q):
    return pltpu.roll(q, 64, 1)


def as_factors(q):
    real, other = real_lanes(q.shape[0]), flip(q)
    return jnp.where(real, q, other), jnp.where(real, other, -q)


def product(t, q):
    return t[0] * q + flip(t[1] * q)


def inverse_factors(diag):
    real, other = real_lanes(diag.shape[0]), flip(diag)
    inv = relax / (diag * diag + other * other)
    return jnp.where(real, diag, other) * inv, jnp.where(real, -other, diag) * inv


def shifted_rows(q, k):
    edge = q.shape[0] - 1 if k > 0 else 0
    return jnp.where(row_ids(q.shape[0]) == edge, 0.0, ahead_y(q, k))


def near_level3(planes):
    n = planes[0].shape[0]
    lane = lanes(n)
    low_z, low_y, x = (lane & 32) == 0, (lane & 16) == 0, lane & 15
    turned = [swap_x(q, 16) for q in planes]
    out = []
    for i, q in enumerate(planes[1:-1]):
        qz = swap_x(q, 32)
        out.append(
            (
                jnp.where(low_y, turned[i + 1], turned[i + 2]),
                jnp.where(low_y, turned[i], turned[i + 1]),
                jnp.where(low_z, qz, shifted_rows(qz, 1)),
                jnp.where(low_z, shifted_rows(qz, -1), qz),
                jnp.where(x == 15, 0.0, ahead_x(q, 1)),
                jnp.where(x == 0, 0.0, ahead_x(q, -1)),
            )
        )
    return out


def slot_lanes(lane, slot):
    return (lane & 78) | ((slot & 4) << 3) | ((slot & 2) << 3) | (slot & 1)


def slot_of(lane):
    return ((lane >> 3) & 4) | ((lane >> 3) & 2) | (lane & 1)


def near_level4(groups):
    n = groups[0].shape[0]
    lane = lanes(n)
    slot, x = slot_of(lane), lane & 14
    nxt, prv = slot_lanes(lane, slot + 1), slot_lanes(lane, slot + 7)
    zero = jnp.zeros_like(groups[0])
    up = [jnp.take_along_axis(q, nxt, axis=1) for q in groups] + [zero]
    down = [zero] + [jnp.take_along_axis(q, prv, axis=1) for q in groups]
    return [
        (
            jnp.where(slot == 7, up[i + 1], up[i]),
            jnp.where(slot == 0, down[i], down[i + 1]),
            shifted_rows(q, 1),
            shifted_rows(q, -1),
            jnp.where(x == 14, 0.0, ahead_x(q, 2)),
            jnp.where(x == 0, 0.0, ahead_x(q, -2)),
        )
        for i, q in enumerate(groups)
    ]


def set_level(here, near, m, t, w, g, p):
    diag = m
    for i, other in enumerate(near):
        face = 0.5 * (here + other)
        diag = diag + face
        t[2 * i, p], t[2 * i + 1, p] = as_factors(face)
    w[0, p], w[1, p] = inverse_factors(diag)
    if g is not None:
        g[0, p], g[1, p] = as_factors(diag)


def gathered_inflow(near, t, p):
    a = sum(t[2 * i, p] * q for i, q in enumerate(near[1:], 1)) + t[0, p] * near[0]
    b = sum(t[2 * i + 1, p] * q for i, q in enumerate(near[1:], 1)) + t[1, p] * near[0]
    return a + flip(b)


def factors(ref, p):
    return ref[0, p], ref[1, p]


def eightfold(q):
    return pair_x(pair_x(pair_x(q, 32), 16), 1)


BATCH = 8


def batches(n, body):
    def run(i, carry):
        body(pl.multiple_of(i * BATCH, BATCH))
        return carry

    lax.fori_loop(0, n // BATCH, run, 0)


def coarse_solve(counts, cells, t3, w3, g3, t4, w4, s3, va, vb, ea, near_out):
    nz, ny = counts
    groups = ny // 8
    zero = jnp.zeros((nz, LANES), F32)
    slot = slot_of(lanes(nz))
    s3[0] = zero
    s3[ny + 1] = zero
    for ref in (va, vb):
        for p in (0, 1, 2, ny + 3, ny + 4, ny + 5):
            ref[p] = zero
    for p in (0, 1, ny + 2, ny + 3):
        for i in range(12):
            t3[i, p] = zero
        w3[0, p] = zero
        w3[1, p] = zero

    def rhs(p):
        return cells[p, :, 0:LANES]

    def compacted(planes):
        out = planes[0]
        for j in range(1, 8):
            out = jnp.where(slot == j, planes[j], out)
        return out

    def load(p0):
        for i in range(BATCH):
            s3[p0 + i + 1] = cells[p0 + i, :, LANES : 2 * LANES]

    batches(ny, load)

    def setup(p0):
        planes = [s3[p0 + i] for i in range(BATCH + 2)]
        for i, near in enumerate(near_level3(planes)):
            p = p0 + i
            set_level(planes[i + 1], near, cells[p, :, 2 * LANES : 3 * LANES], t3, w3, g3, p + 2)
            va[p + 3] = product(factors(w3, p + 2), rhs(p))

    batches(ny, setup)

    s4, m4 = [], []
    for k in range(groups):
        s4.append(0.125 * eightfold_compact([s3[8 * k + j + 1] for j in range(8)], compacted))
        m4.append(0.5 * eightfold_compact([cells[8 * k + j, :, 2 * LANES : 3 * LANES] for j in range(8)], compacted))
    for k, near in enumerate(near_level4(s4)):
        set_level(s4[k], near, m4[k], t4, w4, None, k)

    def sweep3(src, rows, p):
        near = near_level3([src[p + 2], src[p + 3], src[p + 4]])[0]
        gain = rows + gathered_inflow(near, t3, p + 2)
        return keep * src[p + 3] + product(factors(w3, p + 2), gain)

    def pre(p0):
        planes = [va[p0 + i + 2] for i in range(BATCH + 2)]
        for i, near in enumerate(near_level3(planes)):
            p = p0 + i
            gain = rhs(p) + gathered_inflow(near, t3, p + 2)
            vb[p + 3] = keep * planes[i + 1] + product(factors(w3, p + 2), gain)

    batches(ny, pre)

    def restrict(p0):
        planes = [vb[p0 + i + 2] for i in range(BATCH + 2)]
        gains = []
        for i, near in enumerate(near_level3(planes)):
            p = p0 + i
            gain = rhs(p) + gathered_inflow(near, t3, p + 2)
            gains.append(gain - product(factors(g3, p + 2), planes[i + 1]))
        ea[p0 // BATCH] = 0.5 * eightfold_compact(gains, compacted)

    batches(ny, restrict)
    f4 = [ea[k] for k in range(groups)]
    e4 = [product(factors(w4, k), f4[k]) for k in range(groups)]
    for sweep in range(COARSE_SWEEPS - 1):
        e4 = [
            keep * e4[k] + product(factors(w4, k), f4[k] + gathered_inflow(near, t4, k))
            for k, near in enumerate(near_level4(e4))
        ]
    for k in range(groups):
        ea[k] = e4[k]

    mine = lax.axis_index("gy")
    lane = lanes(nz)
    for d in range(-3, 4):
        p = mine + d
        on = jnp.where((p >= 0) & (p < ny), 1.0, 0.0)
        q = jnp.clip(p, 0, ny - 1)
        corr = jnp.take_along_axis(ea[q // 8], slot_lanes(lane, jnp.full((nz, LANES), q % 8, jnp.int32)), axis=1)
        vb[p + 3] = vb[p + 3] + on * corr
    for d in range(-2, 3):
        va[mine + d + 3] = sweep3(vb, rhs(jnp.clip(mine + d, 0, ny - 1)), mine + d)
    for d in range(-1, 2):
        near_out[d + 1] = sweep3(va, rhs(jnp.clip(mine + d, 0, ny - 1)), mine + d)


def eightfold_compact(planes, compacted):
    return compacted([eightfold(q) for q in planes])


def up_kernel(
    counts, cells, cmid, cleft, cright, tz2, ty2, tx2, w2, v1, f1, tz1, ty1, tx1, w1, v0, f0, tz0, ty0, tx0, w0, out,
    t3, w3, g3, t4, w4, s3, va, vb, ea, near, a2, b2, f2, e1, a1, b1, e0, a0, b0,
):
    nz = counts[0]
    gz = lax.axis_index("gz")
    coarse_solve(counts, cells, t3, w3, g3, t4, w4, s3, va, vb, ea, near)

    lane4, zero4 = lanes(4), jnp.zeros((4, LANES), F32)

    def unpack(z):
        for ref in (a2, f2):
            for c in (0, 1):
                ref[c, z, 8:12] = zero4
        for lo, src in ((0, cmid), (4, cright), (12, cleft)):
            q = src[z]
            turned = {k: ahead_x(q, k) if k else q for k in range(-3, 4)}
            for k, (ref, c) in enumerate(((a2, 0), (a2, 1), (f2, 0), (f2, 1))):
                val = turned[k]
                for i in range(1, 4):
                    val = jnp.where((lane4 & 3) == i, turned[k - i], val)
                ref[c, z, lo : lo + 4] = val

    each(0, 12, unpack)
    r16, l16 = row_ids(16), lanes(16)
    cell = l16 // 8
    for dz in (-1, 0, 1):
        row = jnp.clip(gz + dz, 0, nz - 1)
        on = jnp.where((gz + dz >= 0) & (gz + dz < nz), 1.0, 0.0)
        before, own, after = (near[d, pl.ds(row, 1), :] * on for d in range(3))
        rows = jnp.where(r16 < 4, own, jnp.where(r16 < 8, after, jnp.where(r16 < 12, 0.0, before)))
        for c in (0, 1):
            for zz in (0, 1):
                corr = jnp.take_along_axis(rows, cell + 16 * ((r16 // 2) & 1) + (64 * c + 32 * zz), axis=1)
                for z in (4 * dz + 4 + 2 * zz, 4 * dz + 5 + 2 * zz):
                    a2[c, z] = a2[c, z] + corr

    each(1, 11, lambda z: put(b2, z, swept(z, 4, a2, f2, tz2, ty2, tx2, w2)))
    each(2, 10, lambda z: put(a2, z, swept(z, 4, b2, f2, tz2, ty2, tx2, w2)))

    def widen1(z):
        for c in (0, 1):
            q = a2[c, z]
            for k in (0, 1):
                e1.at[c, z][pl.ds(k, 8, stride=2), :] = q[0:8]
                e1.at[c, z][pl.ds(16 + k, 4, stride=2), :] = q[12:16]

    each(2, 10, widen1)
    each(5, 19, lambda z: put(a1, z, add(pair(v1, z), pair(e1, z // 2))))
    each(6, 18, lambda z: put(b1, z, swept(z, 2, a1, f1, tz1, ty1, tx1, w1)))
    each(7, 17, lambda z: put(a1, z, swept(z, 2, b1, f1, tz1, ty1, tx1, w1)))

    def widen0(z):
        for c in (0, 1):
            q = a1[c, z]
            for k in (0, 1):
                e0.at[c, z][pl.ds(k, 8, stride=2), :] = q[0:8]
                e0.at[c, z][pl.ds(16 + k, 2, stride=2), :] = q[8:10]
                e0.at[c, z][pl.ds(20 + k, 2, stride=2), :] = q[22:24]

    each(7, 17, widen0)
    each(2, 22, lambda z: put(a0, z, add(pair(v0, z), pair(e0, z // 2 + 6))))
    each(3, 21, lambda z: put(b0, z, swept(z, 1, a0, f0, tz0, ty0, tx0, w0)))

    def last(z):
        q = swept(z, 1, b0, f0, tz0, ty0, tx0, w0)
        out[0, z - 4] = q[0][0:16]
        out[1, z - 4] = q[1][0:16]

    each(4, 20, last)


def spec_all(n, smem=()):
    return [pl.BlockSpec(memory_space=pltpu.SMEM if i in smem else pltpu.VMEM) for i in range(n)]


def run(kernel, name, args, outs, scratch, smem=()):
    shapes = [jax.ShapeDtypeStruct(s, F32) for s in outs]
    return pl.pallas_call(
        kernel,
        name=name,
        out_shape=shapes,
        in_specs=spec_all(len(args), smem),
        out_specs=spec_all(len(outs)),
        scratch_shapes=[pltpu.VMEM(s, F32) for s in scratch],
        compiler_params=pltpu.CompilerParams(vmem_limit_bytes=VMEM_BYTES),
    )(*args)


def shifts(axis):
    n = lax.axis_size(axis)
    up = [(i, i + 1) for i in range(n - 1)]
    return up, [(j, i) for i, j in up]


def around(block, axis, dim, width):
    up, down = shifts(axis)
    size = block.shape[dim]
    before = lax.ppermute(lax.slice_in_dim(block, size - width, size, axis=dim), axis, up)
    after = lax.ppermute(lax.slice_in_dim(block, 0, width, axis=dim), axis, down)
    return before, after


def window(block, dim, width):
    before, after = around(block, "gz", dim, width)
    mid = jnp.concatenate([before, block, after], axis=dim)
    left, right = around(mid, "gy", dim + 1, width)
    return mid, left, right


def shared(block, axis):
    n = lax.axis_size(axis)
    return lax.all_to_all(jnp.broadcast_to(block[None], (n, *block.shape)), axis, 0, 0)


def body(source, labels, phase_table):
    nz, ny = lax.axis_size("gz"), lax.axis_size("gy")
    near_c, far_c = run(
        coeff_kernel, "coefficients", (labels, phase_table),
        [(2, 8, 8, LANES), (1, 2 * LANES)],
        [(4, 8, 16, LANES), (4, 8, 8, LANES), (4, 4, 4, LANES), (2, 8, LANES)], smem=(1,),
    )
    fine = jnp.concatenate([source, labels.astype(F32)[None]], axis=0)

    win = (2, 24, 24, LANES)
    msg, *state0 = run(
        lambda *refs: fine_kernel((16 * nz, 16 * ny), *refs), "fine_down",
        (*window(fine, 1, 4), phase_table, near_c),
        [(3, 8, 8, LANES)] + [win] * 6,
        [(24, 24, LANES)] + [win] * 4 + [(2, 8, 24, LANES)], smem=(3,),
    )
    win2 = (2, 12, 16, LANES)
    row, c_own, *state = run(
        lambda *refs: middle_kernel(((8 * nz, 8 * ny), (4 * nz, 4 * ny)), *refs), "middle_down",
        (*window(msg, 1, 8), far_c),
        [(1, 3 * LANES), (4, 4, LANES)] + [win] * 6 + [win2] * 4,
        [win] * 4 + [(2, 12, 24, LANES)] + [win2] * 6 + [(2, 2, 16, LANES), (8, LANES)],
    )
    state1, state2 = state[:6], state[6:]
    column = shared(row[0], "gz")
    cells = shared(column, "gy")
    cwin = window(c_own, 0, 4)

    def whole(n, pad):
        return (n, ny + 2 * pad, nz, LANES)

    small = (ny // 8, nz, LANES)
    return run(
        lambda *refs: up_kernel((nz, ny), *refs), "coarse_and_up",
        (cells, *cwin, *state2, *state1, *state0),
        [(2, 16, 16, LANES)],
        [whole(12, 2), whole(2, 2), whole(2, 2), (12, *small), (2, *small)]
        + [whole(1, 1)[1:]] + [whole(1, 3)[1:]] * 2 + [small, (3, nz, LANES)]
        + [win2] * 3 + [(2, 12, 24, LANES), win, win, win, win, win],
    )[0]


def solution(mesh):
    in_specs = (P(None, "gz", "gy", None), P("gz", "gy", None), P())
    out_specs = P(None, "gz", "gy", None)
    return jax.shard_map(body, mesh=mesh, in_specs=in_specs, out_specs=out_specs, check_vma=False)
```

```python
import jax
import jax.numpy as jnp
from jax import lax
from jax.experimental import pallas as pl
from jax.experimental.pallas import tpu as pltpu
from jax.sharding import PartitionSpec as P

PHASES = 4
COARSE_SWEEPS = 8
LANES = 128
relax = 0.7
keep = 1.0 - relax
mass_scale = 0.01
F32 = jnp.float32
VMEM_BYTES = 40 * 1024 * 1024


def lanes(rows):
    return lax.broadcasted_iota(jnp.int32, (rows, LANES), 1)


def row_ids(rows):
    return lax.broadcasted_iota(jnp.int32, (rows, LANES), 0)


def ahead_x(q, k):
    return pltpu.roll(q, (-k) % LANES, 1)


def ahead_y(q, k):
    return pltpu.roll(q, (-k) % q.shape[0], 0)


def pair_x(q, k):
    return q + swap_x(q, k)


def swap_x(q, k):
    return jnp.where((lanes(q.shape[0]) & k) == 0, ahead_x(q, k), ahead_x(q, -k))


def interleave(re, im):
    return jnp.where((lanes(re.shape[0]) & 1) == 0, re, im)


def separate(q):
    even = (lanes(q.shape[0]) & 1) == 0
    return jnp.where(even, q, ahead_x(q, -1)), jnp.where(even, ahead_x(q, 1), q)


def each(lo, hi, body, most=11):
    n = hi - lo
    step = max(k for k in range(1, most + 1) if n % k == 0)
    if step == n:
        for z in range(lo, hi):
            body(z)
        return

    def run(i, carry):
        for j in range(step):
            body(lo + i * step + j)
        return carry

    lax.fori_loop(0, n // step, run, 0)


def sent(copies):
    for copy in copies:
        copy.start()
    return copies


def landed(copies):
    for copy in copies:
        copy.wait()


def times(t, q):
    return t[0] * q[0] - t[1] * q[1], t[0] * q[1] + t[1] * q[0]


def pair(ref, z):
    return ref[0, z], ref[1, z]


def put(ref, z, q):
    ref[0, z] = q[0]
    ref[1, z] = q[1]


def add(*terms):
    return sum(t[0] for t in terms[1:]) + terms[0][0], sum(t[1] for t in terms[1:]) + terms[0][1]


def both(fn, q, k):
    return fn(q[0], k), fn(q[1], k)


def inside(rows, wrap, z, first_z, first_y, size_z, size_y, dead=()):
    r = row_ids(rows)
    y = jnp.where(r >= wrap, r - rows, r) + first_y
    ok = (y >= 0) & (y < size_y)
    plane = jnp.full((rows, LANES), first_z + z, jnp.int32)
    ok = ok & (plane >= 0) & (plane < size_z)
    if dead:
        ok = ok & ((r < dead[0]) | (r >= dead[1]))
    return ok


def make_faces(z, shift, ok, s, m, tz, ty, tx, w, g=None):
    lane = lanes(s.shape[2])
    last = lane >= LANES - shift
    initial = lane < shift
    diag = []
    for c in (0, 1):
        here = s[c, z]
        up = 0.5 * (here + s[c, z + 1])
        down = 0.5 * (here + s[c, z - 1])
        side = 0.5 * (here + ahead_y(here, 1))
        right = 0.5 * (here + jnp.where(last, 0.0, ahead_x(here, shift)))
        left = 0.5 * (here + jnp.where(initial, 0.0, ahead_x(here, -shift)))
        tz[c, z] = up
        ty[c, z] = side
        tx[c, z] = jnp.where(last, 0.0, right)
        diag.append(m[c, z] + (up + down) + (side + ahead_y(side, -1)) + (right + left))
    inv = jnp.where(ok, relax / (diag[0] * diag[0] + diag[1] * diag[1]), 0.0)
    q = (diag[0] * inv, -(diag[1] * inv))
    put(w, z, q)
    if g is not None:
        put(g, z, diag)
    return q


def inflow(z, shift, v, tz, ty, tx):
    here = pair(v, z)
    side, right = pair(ty, z), pair(tx, z)
    return add(
        times(pair(tz, z), pair(v, z + 1)),
        times(pair(tz, z - 1), pair(v, z - 1)),
        times(side, both(ahead_y, here, 1)),
        both(ahead_y, times(side, here), -1),
        times(right, both(ahead_x, here, shift)),
        both(ahead_x, times(right, here), -shift),
    )


def swept(z, shift, v, f, tz, ty, tx, w):
    here = pair(v, z)
    step = times(pair(w, z), add(pair(f, z), inflow(z, shift, v, tz, ty, tx)))
    return keep * here[0] + step[0], keep * here[1] + step[1]


def residual(z, shift, v, f, tz, ty, tx, g):
    out = times(pair(g, z), pair(v, z))
    gain = add(pair(f, z), inflow(z, shift, v, tz, ty, tx))
    return gain[0] - out[0], gain[1] - out[1]


def rows_paired(buf, at, start, count):
    plane = buf.at[at]
    return plane[pl.ds(start, count, stride=2), :] + plane[pl.ds(start + 1, count, stride=2), :]


def packed_row(stack):
    lane, row = lanes(8), row_ids(8)
    cells = jnp.take_along_axis(stack, 8 * (lane % 16), axis=1)
    return jnp.sum(jnp.where(lane // 16 == row, cells, 0.0), axis=0, keepdims=True)


def lookup(lab, table):
    out = []
    for c in range(4):
        scale = 1.0 if c < 2 else mass_scale
        val = [table[p, c] * F32(scale) for p in range(PHASES)]
        out.append(jnp.where(lab == 0, val[0], jnp.where(lab == 1, val[1], jnp.where(lab == 2, val[2], val[3]))))
    return out


def coeff_kernel(labels, table, near_out, far_out, buf, c1, c2, stack):
    for z in range(8):
        a, b = lookup(labels[2 * z], table), lookup(labels[2 * z + 1], table)
        for c in range(4):
            buf[c, z] = a[c] + b[c]
    for z in range(8):
        for c in range(4):
            c1[c, z] = pair_x(rows_paired(buf, (c, z), 0, 8), 1) * (0.125 if c < 2 else 0.5)
    for z in range(8):
        near_out[0, z] = interleave(c1[0, z], c1[1, z])
        near_out[1, z] = interleave(c1[2, z], c1[3, z])
    for c in range(4):
        scale = 0.125 if c < 2 else 0.5
        for z in range(4):
            buf[c, z, 0:8] = c1[c, 2 * z] + c1[c, 2 * z + 1]
        for z in range(4):
            c2[c, z] = pair_x(rows_paired(buf, (c, z), 0, 4), 2) * scale
        for z in range(2):
            buf[c, 4 + z, 0:4] = c2[c, 2 * z] + c2[c, 2 * z + 1]
        for z in range(2):
            stack[c // 2, (c % 2) * 4 + 2 * z : (c % 2) * 4 + 2 * z + 2] = (
                pair_x(rows_paired(buf, (c, 4 + z), 0, 2), 4) * scale
            )
    far_out[:, 0:LANES] = packed_row(stack[0])
    far_out[:, LANES : 2 * LANES] = packed_row(stack[1])


KEPT0 = slice(2, 22)
KEPT1 = slice(5, 19)


def fine_kernel(
    sizes, source, labels, zb, za, left, right, table, near_c, msg_out, *rest
):
    keeps, (v, f, tz, ty, tx, w, lab, s, m, g, first, buf, sem) = rest[:6], rest[6:]
    first_z = lax.axis_index("gz") * 16 - 4
    first_y = lax.axis_index("gy") * 16

    def load(z, own):
        dst = (f.at[0, z], f.at[1, z], lab.at[z])
        for c in range(3):
            dst[c][0:16] = own[c]
            dst[c][16:20] = right[c, z].astype(dst[c].dtype)
            dst[c][20:24] = left[c, z].astype(dst[c].dtype)
        ok = inside(24, 20, z, first_z, first_y, *sizes)
        vals = lookup(lab[z], table)
        for c in (0, 1):
            s[c, z] = jnp.where(ok, vals[c], 0.0)
            m[c, z] = vals[2 + c]

    for z in range(4):
        load(z, (zb[0, z], zb[1, z], zb[2, z].astype(jnp.int32)))
        load(z + 20, (za[0, z], za[1, z], za[2, z].astype(jnp.int32)))
    each(0, 16, lambda z: load(z + 4, (source[0, z], source[1, z], labels[z])))

    def faces(z):
        ok = inside(24, 20, z, first_z, first_y, *sizes)
        put(first, z, times(make_faces(z, 1, ok, s, m, tz, ty, tx, w, g), pair(f, z)))

    each(1, 23, faces)

    def kept(i, ref):
        return pltpu.make_async_copy(ref.at[:, KEPT0], keeps[i], sem.at[i])

    copies = sent([kept(i, ref) for i, ref in enumerate((v, f, tz, ty, tx, w)) if i])
    each(2, 22, lambda z: put(v, z, swept(z, 1, first, f, tz, ty, tx, w)))
    copies += sent([kept(0, v)])

    def restrict(z):
        a = residual(2 * z + 4, 1, v, f, tz, ty, tx, g)
        b = residual(2 * z + 5, 1, v, f, tz, ty, tx, g)
        put(buf, z, add(a, b))

    each(0, 8, restrict, 4)

    def finish(z):
        re, im = (0.5 * pair_x(rows_paired(buf, (c, z), 0, 8), 1) for c in (0, 1))
        msg_out[2, z] = interleave(re, im)
        msg_out[0, z] = near_c[0, z]
        msg_out[1, z] = near_c[1, z]

    each(0, 8, finish)
    landed(copies)


def middle_kernel(
    sizes, mid, left, right, far_c,
    row_out, c_out, *rest
):
    keeps, rest = rest[:10], rest[10:]
    v, f, tz, ty, tx, w, tz2, ty2, tx2, w2, s, m, g, first, buf, s2, m2, f2, g2, first2, v2, buf2, stack, sem = rest
    gz, gy = lax.axis_index("gz"), lax.axis_index("gy")

    def load(z):
        for lo, src in ((0, mid), (8, right), (16, left)):
            for i, ref in enumerate((s, m, f)):
                re, im = separate(src[i, z])
                ref[0, z, lo : lo + 8] = re
                ref[1, z, lo : lo + 8] = im

    each(0, 24, load)

    def faces(z):
        ok = inside(24, 16, z, gz * 8 - 8, gy * 8, *sizes[0])
        put(first, z, times(make_faces(z, 2, ok, s, m, tz, ty, tx, w, g), pair(f, z)))

    each(1, 23, faces)

    def kept(i, ref):
        return pltpu.make_async_copy(ref.at[:, KEPT1], keeps[i], sem.at[i])

    copies = sent([kept(i, ref) for i, ref in enumerate((v, f, tz, ty, tx, w)) if i])
    each(2, 22, lambda z: put(v, z, swept(z, 2, first, f, tz, ty, tx, w)))
    copies += sent([kept(0, v)])

    def coarser(dst, scale, z):
        for c in (0, 1):
            dst[c, z, 0:8] = scale * pair_x(rows_paired(buf, (c, z), 0, 8), 2)
            dst[c, z, 8:12] = jnp.zeros((4, LANES), F32)
            dst[c, z, 12:16] = scale * pair_x(rows_paired(buf, (c, z), 16, 4), 2)

    for src, dst, scale in ((s, s2, 0.125), (m, m2, 0.5)):
        each(0, 12, lambda z: put(buf, z, add(pair(src, 2 * z), pair(src, 2 * z + 1))))
        each(0, 12, lambda z: coarser(dst, scale, z))

    def restrict(z):
        put(buf, z, add(residual(2 * z, 2, v, f, tz, ty, tx, g), residual(2 * z + 1, 2, v, f, tz, ty, tx, g)))

    each(2, 10, restrict, 4)
    each(2, 10, lambda z: coarser(f2, 0.5, z))

    def faces2(z):
        ok = inside(16, 12, z, gz * 4 - 4, gy * 4, *sizes[1], dead=(8, 12))
        return make_faces(z, 4, ok, s2, m2, tz2, ty2, tx2, w2, g2)

    faces2(1)
    tz2[0, 0] = 0.5 * (s2[0, 0] + s2[0, 1])
    tz2[1, 0] = 0.5 * (s2[1, 0] + s2[1, 1])
    each(2, 10, lambda z: put(first2, z, times(faces2(z), pair(f2, z))))
    faces2(10)
    copies += sent([pltpu.make_async_copy(ref, keeps[6 + i], sem.at[6 + i]) for i, ref in enumerate((tz2, ty2, tx2, w2))])
    each(3, 9, lambda z: put(v2, z, swept(z, 4, first2, f2, tz2, ty2, tx2, w2)))
    which = lanes(4) & 3
    for z in range(4):
        a, b = pair(v2, z + 4), pair(f2, z + 4)
        c_out[z] = jnp.where(
            which < 2, jnp.where(which == 0, a[0][0:4], a[1][0:4]), jnp.where(which == 2, b[0][0:4], b[1][0:4])
        )
    for z in range(2):
        a = residual(2 * z + 4, 4, v2, f2, tz2, ty2, tx2, g2)
        b = residual(2 * z + 5, 4, v2, f2, tz2, ty2, tx2, g2)
        put(buf2, z, add(a, b))
    for z in range(2):
        for c in (0, 1):
            stack[4 * c + 2 * z : 4 * c + 2 * z + 2] = 0.5 * pair_x(rows_paired(buf2, (c, z), 0, 2), 4)
    row_out[0:1] = packed_row(stack[...])
    row_out[1:2] = far_c[:, 0:LANES]
    row_out[2:3] = far_c[:, LANES : 2 * LANES]
    row_out[3:8] = jnp.zeros((5, LANES), F32)
    landed(copies)


def real_lanes(rows):
    return lanes(rows) < 64


def flip(q):
    return pltpu.roll(q, 64, 1)


def as_factors(q):
    real, other = real_lanes(q.shape[0]), flip(q)
    return jnp.where(real, q, other), jnp.where(real, other, -q)


def product(t, q):
    return t[0] * q + flip(t[1] * q)


def inverse_factors(diag):
    real, other = real_lanes(diag.shape[0]), flip(diag)
    inv = relax / (diag * diag + other * other)
    return jnp.where(real, diag, other) * inv, jnp.where(real, -other, diag) * inv


def shifted_rows(q, k):
    edge = q.shape[0] - 1 if k > 0 else 0
    return jnp.where(row_ids(q.shape[0]) == edge, 0.0, ahead_y(q, k))


def near_level3(planes):
    n = planes[0].shape[0]
    lane = lanes(n)
    low_z, low_y, x = (lane & 32) == 0, (lane & 16) == 0, lane & 15
    turned = [swap_x(q, 16) for q in planes]
    out = []
    for i, q in enumerate(planes[1:-1]):
        qz = swap_x(q, 32)
        out.append(
            (
                jnp.where(low_y, turned[i + 1], turned[i + 2]),
                jnp.where(low_y, turned[i], turned[i + 1]),
                jnp.where(low_z, qz, shifted_rows(qz, 1)),
                jnp.where(low_z, shifted_rows(qz, -1), qz),
                jnp.where(x == 15, 0.0, ahead_x(q, 1)),
                jnp.where(x == 0, 0.0, ahead_x(q, -1)),
            )
        )
    return out


def slot_lanes(lane, slot):
    return (lane & 78) | ((slot & 4) << 3) | ((slot & 2) << 3) | (slot & 1)


def slot_of(lane):
    return ((lane >> 3) & 4) | ((lane >> 3) & 2) | (lane & 1)


def near_level4(groups):
    n = groups[0].shape[0]
    lane = lanes(n)
    slot, x = slot_of(lane), lane & 14
    nxt, prv = slot_lanes(lane, slot + 1), slot_lanes(lane, slot + 7)
    zero = jnp.zeros_like(groups[0])
    up = [jnp.take_along_axis(q, nxt, axis=1) for q in groups] + [zero]
    down = [zero] + [jnp.take_along_axis(q, prv, axis=1) for q in groups]
    return [
        (
            jnp.where(slot == 7, up[i + 1], up[i]),
            jnp.where(slot == 0, down[i], down[i + 1]),
            shifted_rows(q, 1),
            shifted_rows(q, -1),
            jnp.where(x == 14, 0.0, ahead_x(q, 2)),
            jnp.where(x == 0, 0.0, ahead_x(q, -2)),
        )
        for i, q in enumerate(groups)
    ]


def set_level(here, near, m, t, w, g, p):
    diag = m
    for i, other in enumerate(near):
        face = 0.5 * (here + other)
        diag = diag + face
        t[2 * i, p], t[2 * i + 1, p] = as_factors(face)
    w[0, p], w[1, p] = inverse_factors(diag)
    if g is not None:
        g[0, p], g[1, p] = as_factors(diag)


def gathered_inflow(near, t, p):
    a = sum(t[2 * i, p] * q for i, q in enumerate(near[1:], 1)) + t[0, p] * near[0]
    b = sum(t[2 * i + 1, p] * q for i, q in enumerate(near[1:], 1)) + t[1, p] * near[0]
    return a + flip(b)


def factors(ref, p):
    return ref[0, p], ref[1, p]


def folded(planes):
    lane = lanes(planes[0].shape[0])
    for bit in (1, 16, 32):
        low = (lane & bit) == 0
        planes = [
            jnp.where(low, a, b) + swap_x(jnp.where(low, b, a), bit) for a, b in zip(planes[0::2], planes[1::2])
        ]
    return planes[0]


BATCH = 8


def batches(n, body):
    def run(i, carry):
        body(pl.multiple_of(i * BATCH, BATCH))
        return carry

    lax.fori_loop(0, n // BATCH, run, 0)


def level4(f4, s4, m4, t4):
    real = real_lanes(s4[0].shape[0])
    start = []
    for k, near in enumerate(near_level4(s4)):
        faces = [0.5 * (s4[k] + other) for other in near]
        fa = inverse_factors(sum(faces[1:]) + faces[0] + m4[k])
        start.append(product(fa, f4[k]))
        for i, face in enumerate(faces):
            q = product(fa, face)
            other = flip(q)
            t4[2 * i, k] = jnp.where(real, q, other)
            t4[2 * i + 1, k] = jnp.where(real, -other, q)
    turned = [flip(q) for q in start]
    e, o = start, turned
    for sweep in range(COARSE_SWEEPS - 1):
        pairs = list(zip(near_level4(e), near_level4(o)))
        e_next, o_next = [], []
        for k, (ne, no) in enumerate(pairs):
            ab = [(t4[2 * i, k], t4[2 * i + 1, k]) for i in range(6)]
            x = [a * p + b * q for (a, b), p, q in zip(ab, ne, no)]
            y = [a * q - b * p for (a, b), p, q in zip(ab, ne, no)]
            e_next.append((keep * e[k] + start[k] + x[0]) + (x[1] + x[2]) + (x[3] + x[4]) + x[5])
            o_next.append((keep * o[k] + turned[k] + y[0]) + (y[1] + y[2]) + (y[3] + y[4]) + y[5])
        e, o = e_next, o_next
    return e


def coarse_solve(counts, cells, t3, w3, g3, t4, s3, va, vb, ea):
    nz, ny = counts
    groups = ny // 8
    zero = jnp.zeros((nz, LANES), F32)
    s3[0] = zero
    s3[ny + 1] = zero
    for ref in (va, vb):
        for p in (0, 1, 2, ny + 3, ny + 4, ny + 5):
            ref[p] = zero
    for p in (0, 1, ny + 2, ny + 3):
        for i in range(12):
            t3[i, p] = zero
        w3[0, p] = zero
        w3[1, p] = zero

    def load(p0):
        for i in range(BATCH):
            s3[p0 + i + 1] = cells[p0 + i, 1]

    batches(ny, load)

    def setup(p0):
        planes = [s3[p0 + i] for i in range(BATCH + 2)]
        for i, near in enumerate(near_level3(planes)):
            p = p0 + i
            set_level(planes[i + 1], near, cells[p, 2], t3, w3, g3, p + 2)
            va[p + 3] = product(factors(w3, p + 2), cells[p, 0])

    batches(ny, setup)
    s4 = [0.125 * folded([cells[8 * k + j, 1] for j in range(8)]) for k in range(groups)]
    m4 = [0.5 * folded([cells[8 * k + j, 2] for j in range(8)]) for k in range(groups)]

    def swept3(here, near, p):
        gain = cells[jnp.clip(p, 0, ny - 1), 0] + gathered_inflow(near, t3, p + 2)
        return keep * here + product(factors(w3, p + 2), gain)

    def pre(p0):
        planes = [va[p0 + i + 2] for i in range(BATCH + 2)]
        for i, near in enumerate(near_level3(planes)):
            p = p0 + i
            gain = cells[p, 0] + gathered_inflow(near, t3, p + 2)
            vb[p + 3] = keep * planes[i + 1] + product(factors(w3, p + 2), gain)

    batches(ny, pre)

    def restrict(p0):
        planes = [vb[p0 + i + 2] for i in range(BATCH + 2)]
        gains = []
        for i, near in enumerate(near_level3(planes)):
            p = p0 + i
            gain = cells[p, 0] + gathered_inflow(near, t3, p + 2)
            gains.append(gain - product(factors(g3, p + 2), planes[i + 1]))
        ea[p0 // BATCH] = 0.5 * folded(gains)

    batches(ny, restrict)
    for k, q in enumerate(level4([ea[k] for k in range(groups)], s4, m4, t4)):
        ea[k] = q

    mine = lax.axis_index("gy")
    lane = lanes(nz)
    planes = []
    for d in range(-3, 4):
        p = mine + d
        on = jnp.where((p >= 0) & (p < ny), 1.0, 0.0)
        q = jnp.clip(p, 0, ny - 1)
        corr = jnp.take_along_axis(ea[q // 8], slot_lanes(lane, jnp.full((nz, LANES), q % 8, jnp.int32)), axis=1)
        planes.append(vb[p + 3] + on * corr)
    for reach in (2, 1):
        planes = [
            swept3(here, near, mine + d)
            for d, here, near in zip(range(-reach, reach + 1), planes[1:-1], near_level3(planes))
        ]
    return planes


def up_kernel(counts, cells, cmid, cleft, cright, *rest):
    keeps, out, rest = rest[:16], rest[16], rest[17:]
    tz2, ty2, tx2, w2, v1, f1, tz1, ty1, tx1, w1, v0, f0, tz0, ty0, tx0, w0 = rest[:16]
    t3, w3, g3, t4, s3, va, vb, ea, near, a2, b2, f2, e1, a1, b1, e0, a0, b0, sem = rest[16:]
    copies = []
    for i, dst in enumerate(rest[:16]):
        dst = dst if i < 4 else dst.at[:, KEPT1] if i < 10 else dst.at[:, KEPT0]
        copies.append(pltpu.make_async_copy(keeps[i], dst, sem.at[i]))
    sent(copies)
    nz = counts[0]
    gz = lax.axis_index("gz")
    for d, q in enumerate(coarse_solve(counts, cells, t3, w3, g3, t4, s3, va, vb, ea)):
        near[d] = q

    lane4, zero4 = lanes(4), jnp.zeros((4, LANES), F32)

    def unpack(z):
        for ref in (a2, f2):
            for c in (0, 1):
                ref[c, z, 8:12] = zero4
        for lo, src in ((0, cmid), (4, cright), (12, cleft)):
            q = src[z]
            turned = {k: ahead_x(q, k) if k else q for k in range(-3, 4)}
            for k, (ref, c) in enumerate(((a2, 0), (a2, 1), (f2, 0), (f2, 1))):
                val = turned[k]
                for i in range(1, 4):
                    val = jnp.where((lane4 & 3) == i, turned[k - i], val)
                ref[c, z, lo : lo + 4] = val

    each(0, 12, unpack)
    r16, l16 = row_ids(16), lanes(16)
    cell = l16 // 8
    for dz in (-1, 0, 1):
        row = jnp.clip(gz + dz, 0, nz - 1)
        on = jnp.where((gz + dz >= 0) & (gz + dz < nz), 1.0, 0.0)
        before, own, after = (near[d, pl.ds(row, 1), :] * on for d in range(3))
        rows = jnp.where(r16 < 4, own, jnp.where(r16 < 8, after, jnp.where(r16 < 12, 0.0, before)))
        for c in (0, 1):
            for zz in (0, 1):
                corr = jnp.take_along_axis(rows, cell + 16 * ((r16 // 2) & 1) + (64 * c + 32 * zz), axis=1)
                for z in (4 * dz + 4 + 2 * zz, 4 * dz + 5 + 2 * zz):
                    a2[c, z] = a2[c, z] + corr

    landed(copies)
    each(1, 11, lambda z: put(b2, z, swept(z, 4, a2, f2, tz2, ty2, tx2, w2)))
    each(2, 10, lambda z: put(a2, z, swept(z, 4, b2, f2, tz2, ty2, tx2, w2)))

    def widen1(z):
        for c in (0, 1):
            q = a2[c, z]
            for k in (0, 1):
                e1.at[c, z][pl.ds(k, 8, stride=2), :] = q[0:8]
                e1.at[c, z][pl.ds(16 + k, 4, stride=2), :] = q[12:16]

    each(2, 10, widen1)
    def correct1(z):
        e = pair(e1, z)
        for k in (2 * z, 2 * z + 1):
            put(a1, k, add(pair(v1, k), e))

    each(3, 9, correct1)
    for k, z in ((5, 2), (18, 9)):
        put(a1, k, add(pair(v1, k), pair(e1, z)))
    each(6, 18, lambda z: put(b1, z, swept(z, 2, a1, f1, tz1, ty1, tx1, w1)))
    each(7, 17, lambda z: put(a1, z, swept(z, 2, b1, f1, tz1, ty1, tx1, w1)))

    def widen0(z):
        for c in (0, 1):
            q = a1[c, z]
            for k in (0, 1):
                e0.at[c, z][pl.ds(k, 8, stride=2), :] = q[0:8]
                e0.at[c, z][pl.ds(16 + k, 2, stride=2), :] = q[8:10]
                e0.at[c, z][pl.ds(20 + k, 2, stride=2), :] = q[22:24]

    each(7, 17, widen0)
    def correct0(z):
        e = pair(e0, z)
        for k in (2 * z - 12, 2 * z - 11):
            put(a0, k, add(pair(v0, k), e))

    each(7, 17, correct0)
    each(3, 21, lambda z: put(b0, z, swept(z, 1, a0, f0, tz0, ty0, tx0, w0)))

    def last(z):
        q = swept(z, 1, b0, f0, tz0, ty0, tx0, w0)
        out[0, z - 4] = q[0][0:16]
        out[1, z - 4] = q[1][0:16]

    each(4, 20, last)


def run(kernel, name, args, outs, scratch, smem=(), far_in=(), far_out=(), copies=0):
    def specs(n, smem, far):
        spaces = [pltpu.SMEM if i in smem else pltpu.HBM if i in far else pltpu.VMEM for i in range(n)]
        return [pl.BlockSpec(memory_space=space) for space in spaces]

    return pl.pallas_call(
        kernel,
        name=name,
        out_shape=[jax.ShapeDtypeStruct(s, F32) for s in outs],
        in_specs=specs(len(args), smem, far_in),
        out_specs=specs(len(outs), (), far_out),
        scratch_shapes=[pltpu.VMEM(s, F32) if isinstance(s, tuple) else s for s in scratch]
        + ([pltpu.SemaphoreType.DMA((copies,))] if copies else []),
        compiler_params=pltpu.CompilerParams(vmem_limit_bytes=VMEM_BYTES),
    )(*args)


def shifts(axis):
    n = lax.axis_size(axis)
    up = [(i, i + 1) for i in range(n - 1)]
    return up, [(j, i) for i, j in up]


def around(block, axis, dim, width):
    up, down = shifts(axis)
    size = block.shape[dim]
    before = lax.ppermute(lax.slice_in_dim(block, size - width, size, axis=dim), axis, up)
    after = lax.ppermute(lax.slice_in_dim(block, 0, width, axis=dim), axis, down)
    return before, after


def window(block, dim, width):
    before, after = around(block, "gz", dim, width)
    mid = jnp.concatenate([before, block, after], axis=dim)
    left, right = around(mid, "gy", dim + 1, width)
    return mid, left, right


def shared(block, axis):
    n = lax.axis_size(axis)
    return lax.all_to_all(jnp.broadcast_to(block[None], (n, *block.shape)), axis, 0, 0)


def body(source, labels, phase_table):
    nz, ny = lax.axis_size("gz"), lax.axis_size("gy")

    def edge(lo, hi):
        return jnp.concatenate([source[:, lo:hi], labels[None, lo:hi].astype(F32)], axis=0)

    up, down = shifts("gz")
    zb = lax.ppermute(edge(12, 16), "gz", up)
    za = lax.ppermute(edge(0, 4), "gz", down)

    def side(lo, hi):
        own = jnp.concatenate([source[:, :, lo:hi], labels[None, :, lo:hi].astype(F32)], axis=0)
        return jnp.concatenate([zb[:, :, lo:hi], own, za[:, :, lo:hi]], axis=1)

    up, down = shifts("gy")
    left = lax.ppermute(side(12, 16), "gy", up)
    right = lax.ppermute(side(0, 4), "gy", down)

    near_c, far_c = run(
        coeff_kernel, "coefficients", (labels, phase_table),
        [(2, 8, 8, LANES), (1, 2 * LANES)],
        [(4, 8, 16, LANES), (4, 8, 8, LANES), (4, 4, 4, LANES), (2, 8, LANES)], smem=(1,),
    )
    win, win2 = (2, 24, 24, LANES), (2, 12, 16, LANES)
    win0 = (2, KEPT0.stop - KEPT0.start, 24, LANES)
    win1 = (2, KEPT1.stop - KEPT1.start, 24, LANES)
    msg, *state0 = run(
        lambda *refs: fine_kernel((16 * nz, 16 * ny), *refs), "fine_down",
        (source, labels, zb, za, left, right, phase_table, near_c),
        [(3, 8, 8, LANES)] + [win0] * 6,
        [win] * 6 + [pltpu.VMEM((24, 24, LANES), jnp.int32)] + [win] * 4 + [(2, 8, 24, LANES)],
        smem=(6,), far_out=range(1, 7), copies=6,
    )
    row, c_own, *state = run(
        lambda *refs: middle_kernel(((8 * nz, 8 * ny), (4 * nz, 4 * ny)), *refs), "middle_down",
        (*window(msg, 1, 8), far_c),
        [(8, LANES), (4, 4, LANES)] + [win1] * 6 + [win2] * 4,
        [win] * 6 + [win2] * 4 + [win] * 4 + [(2, 12, 24, LANES)] + [win2] * 6 + [(2, 2, 16, LANES), (8, LANES)],
        far_out=range(2, 12), copies=10,
    )
    state1, state2 = state[:6], state[6:]
    column = shared(row, "gz")[:, 0:3].transpose(1, 0, 2)
    cells = shared(column, "gy")
    cwin = window(c_own, 0, 4)

    def whole(n, pad):
        return (n, ny + 2 * pad, nz, LANES)

    small = (ny // 8, nz, LANES)
    return run(
        lambda *refs: up_kernel((nz, ny), *refs), "coarse_and_up",
        (cells, *cwin, *state2, *state1, *state0),
        [(2, 16, 16, LANES)],
        [win2] * 4 + [win] * 12
        + [whole(12, 2), whole(2, 2), whole(2, 2), (12, *small)]
        + [whole(1, 1)[1:]] + [whole(1, 3)[1:]] * 2 + [small, (3, nz, LANES)]
        + [win2] * 3 + [(2, 12, 24, LANES), win, win, win, win, win],
        far_in=range(4, 20), copies=16,
    )[0]


def solution(mesh):
    in_specs = (P(None, "gz", "gy", None), P("gz", "gy", None), P())
    out_specs = P(None, "gz", "gy", None)
    return jax.shard_map(body, mesh=mesh, in_specs=in_specs, out_specs=out_specs, check_vma=False)
```

```python
import jax
import jax.numpy as jnp
from jax import lax
from jax.experimental import pallas as pl
from jax.experimental.pallas import tpu as pltpu
from jax.sharding import PartitionSpec as P

PHASES = 4
COARSE_SWEEPS = 8
LANES = 128
relax = 0.7
keep = 1.0 - relax
mass_scale = 0.01
F32 = jnp.float32
MESSAGE = 24
MOST_VMEM = 60 * 1024 * 1024


def lanes(rows):
    return lax.broadcasted_iota(jnp.int32, (rows, LANES), 1)


def row_ids(rows):
    return lax.broadcasted_iota(jnp.int32, (rows, LANES), 0)


def ahead_x(q, k):
    return pltpu.roll(q, (-k) % LANES, 1)


def ahead_y(q, k):
    return pltpu.roll(q, (-k) % q.shape[0], 0)


def pair_x(q, k):
    return q + swap_x(q, k)


def swap_x(q, k):
    return jnp.where((lanes(q.shape[0]) & k) == 0, ahead_x(q, k), ahead_x(q, -k))


def interleave(re, im):
    return jnp.where((lanes(re.shape[0]) & 1) == 0, re, im)


def separate(q):
    even = (lanes(q.shape[0]) & 1) == 0
    return jnp.where(even, q, ahead_x(q, -1)), jnp.where(even, ahead_x(q, 1), q)


def each(lo, hi, body, step=4):
    full = (hi - lo) // step

    def run(i, carry):
        for j in range(step):
            body(lo + i * step + j)
        return carry

    lax.fori_loop(0, full, run, 0)
    for z in range(lo + full * step, hi):
        body(z)


def sent(copies):
    for copy in copies:
        copy.start()
    return copies


def landed(copies):
    for copy in copies:
        copy.wait()


def times(t, q):
    return t[0] * q[0] - t[1] * q[1], t[0] * q[1] + t[1] * q[0]


def pair(ref, z):
    return ref[0, z], ref[1, z]


def put(ref, z, q):
    ref[0, z] = q[0]
    ref[1, z] = q[1]


def add(*terms):
    return sum(t[0] for t in terms[1:]) + terms[0][0], sum(t[1] for t in terms[1:]) + terms[0][1]


def both(fn, q, k):
    return fn(q[0], k), fn(q[1], k)


def inside(rows, wrap, z, first_z, first_y, size_z, size_y, dead=()):
    r = row_ids(rows)
    y = jnp.where(r >= wrap, r - rows, r) + first_y
    ok = (y >= 0) & (y < size_y)
    plane = jnp.full((rows, LANES), first_z + z, jnp.int32)
    ok = ok & (plane >= 0) & (plane < size_z)
    if dead:
        ok = ok & ((r < dead[0]) | (r >= dead[1]))
    return ok


def make_faces(z, shift, ok, s, m, tz, ty, tx, w, g=None):
    lane = lanes(s.shape[2])
    last = lane >= LANES - shift
    initial = lane < shift
    diag = []
    for c in (0, 1):
        here = s[c, z]
        up = 0.5 * (here + s[c, z + 1])
        down = 0.5 * (here + s[c, z - 1])
        side = 0.5 * (here + ahead_y(here, 1))
        right = 0.5 * (here + jnp.where(last, 0.0, ahead_x(here, shift)))
        left = 0.5 * (here + jnp.where(initial, 0.0, ahead_x(here, -shift)))
        tz[c, z] = up
        ty[c, z] = side
        tx[c, z] = jnp.where(last, 0.0, right)
        diag.append(m[c, z] + (up + down) + (side + ahead_y(side, -1)) + (right + left))
    inv = jnp.where(ok, relax / (diag[0] * diag[0] + diag[1] * diag[1]), 0.0)
    q = (diag[0] * inv, -(diag[1] * inv))
    put(w, z, q)
    if g is not None:
        put(g, z, diag)
    return q


def inflow(z, shift, v, tz, ty, tx):
    here = pair(v, z)
    side, right = pair(ty, z), pair(tx, z)
    return add(
        times(pair(tz, z), pair(v, z + 1)),
        times(pair(tz, z - 1), pair(v, z - 1)),
        times(side, both(ahead_y, here, 1)),
        both(ahead_y, times(side, here), -1),
        times(right, both(ahead_x, here, shift)),
        both(ahead_x, times(right, here), -shift),
    )


def swept(z, shift, v, f, tz, ty, tx, w):
    here = pair(v, z)
    step = times(pair(w, z), add(pair(f, z), inflow(z, shift, v, tz, ty, tx)))
    return keep * here[0] + step[0], keep * here[1] + step[1]


def residual(z, shift, v, f, tz, ty, tx, g):
    out = times(pair(g, z), pair(v, z))
    gain = add(pair(f, z), inflow(z, shift, v, tz, ty, tx))
    return gain[0] - out[0], gain[1] - out[1]


def rows_paired(buf, at, start, count):
    plane = buf.at[at]
    return plane[pl.ds(start, count, stride=2), :] + plane[pl.ds(start + 1, count, stride=2), :]


def packed_row(stack):
    lane, row = lanes(8), row_ids(8)
    cells = jnp.take_along_axis(stack, 8 * (lane % 16), axis=1)
    return jnp.sum(jnp.where(lane // 16 == row, cells, 0.0), axis=0, keepdims=True)


def lookup(lab, table):
    out = []
    for c in range(4):
        scale = 1.0 if c < 2 else mass_scale
        val = [table[p, c] * F32(scale) for p in range(PHASES)]
        out.append(jnp.where(lab == 0, val[0], jnp.where(lab == 1, val[1], jnp.where(lab == 2, val[2], val[3]))))
    return out


def coeff_kernel(labels, table, near_out, far_out, buf, c1, c2, stack):
    for z in range(8):
        a, b = lookup(labels[2 * z], table), lookup(labels[2 * z + 1], table)
        for c in range(4):
            buf[c, z] = a[c] + b[c]
    for z in range(8):
        for c in range(4):
            c1[c, z] = pair_x(rows_paired(buf, (c, z), 0, 8), 1) * (0.125 if c < 2 else 0.5)
    for z in range(8):
        near_out[0, z] = interleave(c1[0, z], c1[1, z])
        near_out[1, z] = interleave(c1[2, z], c1[3, z])
    for c in range(4):
        scale = 0.125 if c < 2 else 0.5
        for z in range(4):
            buf[c, z, 0:8] = c1[c, 2 * z] + c1[c, 2 * z + 1]
        for z in range(4):
            c2[c, z] = pair_x(rows_paired(buf, (c, z), 0, 4), 2) * scale
        for z in range(2):
            buf[c, 4 + z, 0:4] = c2[c, 2 * z] + c2[c, 2 * z + 1]
        for z in range(2):
            stack[c // 2, (c % 2) * 4 + 2 * z : (c % 2) * 4 + 2 * z + 2] = (
                pair_x(rows_paired(buf, (c, 4 + z), 0, 2), 4) * scale
            )
    far_out[:, 0:LANES] = packed_row(stack[0])
    far_out[:, LANES : 2 * LANES] = packed_row(stack[1])


KEPT0 = slice(2, 22)
KEPT1 = slice(5, 19)


def fine_kernel(
    sizes, source, labels, zb, za, left, right, table, near_c, msg_out, *rest
):
    keeps, v, f, tz, ty, tx, w, lab, s, m, g, first, buf, sem = rest
    first_z = lax.axis_index("gz") * 16 - 4
    first_y = lax.axis_index("gy") * 16

    def load(z, own):
        dst = (f.at[0, z], f.at[1, z], lab.at[z])
        for c in range(3):
            dst[c][0:16] = own[c]
            dst[c][16:20] = right[c, z].astype(dst[c].dtype)
            dst[c][20:24] = left[c, z].astype(dst[c].dtype)
        ok = inside(24, 20, z, first_z, first_y, *sizes)
        vals = lookup(lab[z], table)
        for c in (0, 1):
            s[c, z] = jnp.where(ok, vals[c], 0.0)
            m[c, z] = vals[2 + c]

    for z in range(4):
        load(z, (zb[0, z], zb[1, z], zb[2, z].astype(jnp.int32)))
        load(z + 20, (za[0, z], za[1, z], za[2, z].astype(jnp.int32)))
    each(0, 16, lambda z: load(z + 4, (source[0, z], source[1, z], labels[z])))

    def faces(z):
        ok = inside(24, 20, z, first_z, first_y, *sizes)
        put(first, z, times(make_faces(z, 1, ok, s, m, tz, ty, tx, w, g), pair(f, z)))

    each(1, 23, faces)

    def kept(i, ref):
        return pltpu.make_async_copy(ref.at[:, KEPT0], keeps.at[i], sem.at[i])

    copies = sent([kept(i, ref) for i, ref in enumerate((v, f, tz, ty, tx, w)) if i])
    each(2, 22, lambda z: put(v, z, swept(z, 1, first, f, tz, ty, tx, w)))
    copies += sent([kept(0, v)])

    def restrict(z):
        a = residual(2 * z + 4, 1, v, f, tz, ty, tx, g)
        b = residual(2 * z + 5, 1, v, f, tz, ty, tx, g)
        put(buf, z, add(a, b))

    each(0, 8, restrict, 4)

    def finish(z):
        re, im = (0.5 * pair_x(rows_paired(buf, (c, z), 0, 8), 1) for c in (0, 1))
        msg_out[2, z] = interleave(re, im)
        msg_out[0, z] = near_c[0, z]
        msg_out[1, z] = near_c[1, z]

    each(0, 8, finish)
    landed(copies)


def middle_kernel(
    sizes, mid, left, right, far_c,
    msg_out, *rest
):
    keeps, rest = rest[0], rest[1:]
    v, f, tz, ty, tx, w, tz2, ty2, tx2, w2, s, m, g, first, buf, s2, m2, f2, g2, first2, v2, buf2, stack, sem = rest
    gz, gy = lax.axis_index("gz"), lax.axis_index("gy")

    def load(z):
        for lo, src in ((0, mid), (8, right), (16, left)):
            for i, ref in enumerate((s, m, f)):
                re, im = separate(src[i, z])
                ref[0, z, lo : lo + 8] = re
                ref[1, z, lo : lo + 8] = im

    each(0, 24, load)

    def faces(z):
        ok = inside(24, 16, z, gz * 8 - 8, gy * 8, *sizes[0])
        put(first, z, times(make_faces(z, 2, ok, s, m, tz, ty, tx, w, g), pair(f, z)))

    each(1, 23, faces)

    def kept(i, ref):
        return pltpu.make_async_copy(ref.at[:, KEPT1], keeps.at[i], sem.at[i])

    copies = sent([kept(i, ref) for i, ref in enumerate((v, f, tz, ty, tx, w)) if i])
    each(2, 22, lambda z: put(v, z, swept(z, 2, first, f, tz, ty, tx, w)))
    copies += sent([kept(0, v)])

    def coarser(dst, scale, z):
        for c in (0, 1):
            dst[c, z, 0:8] = scale * pair_x(rows_paired(buf, (c, z), 0, 8), 2)
            dst[c, z, 8:12] = jnp.zeros((4, LANES), F32)
            dst[c, z, 12:16] = scale * pair_x(rows_paired(buf, (c, z), 16, 4), 2)

    for src, dst, scale in ((s, s2, 0.125), (m, m2, 0.5)):
        each(0, 12, lambda z: put(buf, z, add(pair(src, 2 * z), pair(src, 2 * z + 1))))
        each(0, 12, lambda z: coarser(dst, scale, z))

    def restrict(z):
        put(buf, z, add(residual(2 * z, 2, v, f, tz, ty, tx, g), residual(2 * z + 1, 2, v, f, tz, ty, tx, g)))

    each(2, 10, restrict, 4)
    each(2, 10, lambda z: coarser(f2, 0.5, z))

    def faces2(z):
        ok = inside(16, 12, z, gz * 4 - 4, gy * 4, *sizes[1], dead=(8, 12))
        return make_faces(z, 4, ok, s2, m2, tz2, ty2, tx2, w2, g2)

    faces2(1)
    tz2[0, 0] = 0.5 * (s2[0, 0] + s2[0, 1])
    tz2[1, 0] = 0.5 * (s2[1, 0] + s2[1, 1])
    each(2, 10, lambda z: put(first2, z, times(faces2(z), pair(f2, z))))
    faces2(10)
    copies += sent([pltpu.make_async_copy(ref, keeps.at[6 + i, :, 0:12, 0:16], sem.at[6 + i]) for i, ref in enumerate((tz2, ty2, tx2, w2))])
    each(3, 9, lambda z: put(v2, z, swept(z, 4, first2, f2, tz2, ty2, tx2, w2)))
    which = lanes(4) & 3
    for z in range(4):
        a, b = pair(v2, z + 4), pair(f2, z + 4)
        msg_out[8 + 4 * z : 12 + 4 * z] = jnp.where(
            which < 2, jnp.where(which == 0, a[0][0:4], a[1][0:4]), jnp.where(which == 2, b[0][0:4], b[1][0:4])
        )
    for z in range(2):
        a = residual(2 * z + 4, 4, v2, f2, tz2, ty2, tx2, g2)
        b = residual(2 * z + 5, 4, v2, f2, tz2, ty2, tx2, g2)
        put(buf2, z, add(a, b))
    for z in range(2):
        for c in (0, 1):
            stack[4 * c + 2 * z : 4 * c + 2 * z + 2] = 0.5 * pair_x(rows_paired(buf2, (c, z), 0, 2), 4)
    msg_out[0:1] = packed_row(stack[...])
    msg_out[1:2] = far_c[:, 0:LANES]
    msg_out[2:3] = far_c[:, LANES : 2 * LANES]
    msg_out[3:8] = jnp.zeros((5, LANES), F32)
    landed(copies)


def spread_kernel(column, cells, near):
    ny, _, nz, _ = cells.shape
    for k in range(3):
        q = column[pl.ds(k, nz, stride=MESSAGE), :]
        for p in range(ny):
            cells[p, k] = q
    mine = lax.axis_index("gz")
    for d in (-1, 0, 1):
        p = jnp.clip(mine + d, 0, nz - 1)
        on = jnp.where((mine + d >= 0) & (mine + d < nz), 1.0, 0.0)
        q = on * column[pl.ds(pl.multiple_of(p * MESSAGE + 8, 8), 16), :]
        for z in range(4):
            near[4 * d + 4 + z] = q[4 * z : 4 * z + 4]


def real_lanes(rows):
    return lanes(rows) < 64


def flip(q):
    return pltpu.roll(q, 64, 1)


def as_factors(q):
    real, other = real_lanes(q.shape[0]), flip(q)
    return jnp.where(real, q, other), jnp.where(real, other, -q)


def product(t, q):
    return t[0] * q + flip(t[1] * q)


def inverse_factors(diag):
    real, other = real_lanes(diag.shape[0]), flip(diag)
    inv = relax / (diag * diag + other * other)
    return jnp.where(real, diag, other) * inv, jnp.where(real, -other, diag) * inv


def shifted_rows(q, k):
    edge = q.shape[0] - 1 if k > 0 else 0
    return jnp.where(row_ids(q.shape[0]) == edge, 0.0, ahead_y(q, k))


def near_level3(planes):
    n = planes[0].shape[0]
    lane = lanes(n)
    low_z, low_y, x = (lane & 32) == 0, (lane & 16) == 0, lane & 15
    turned = [swap_x(q, 16) for q in planes]
    out = []
    for i, q in enumerate(planes[1:-1]):
        qz = swap_x(q, 32)
        out.append(
            (
                jnp.where(low_y, turned[i + 1], turned[i + 2]),
                jnp.where(low_y, turned[i], turned[i + 1]),
                jnp.where(low_z, qz, shifted_rows(qz, 1)),
                jnp.where(low_z, shifted_rows(qz, -1), qz),
                jnp.where(x == 15, 0.0, ahead_x(q, 1)),
                jnp.where(x == 0, 0.0, ahead_x(q, -1)),
            )
        )
    return out


def slot_lanes(lane, slot):
    return (lane & 78) | ((slot & 4) << 3) | ((slot & 2) << 3) | (slot & 1)


def slot_of(lane):
    return ((lane >> 3) & 4) | ((lane >> 3) & 2) | (lane & 1)


def near_level4(groups):
    n = groups[0].shape[0]
    lane = lanes(n)
    slot, x = slot_of(lane), lane & 14
    nxt, prv = slot_lanes(lane, slot + 1), slot_lanes(lane, slot + 7)
    zero = jnp.zeros_like(groups[0])
    up = [jnp.take_along_axis(q, nxt, axis=1) for q in groups] + [zero]
    down = [zero] + [jnp.take_along_axis(q, prv, axis=1) for q in groups]
    return [
        (
            jnp.where(slot == 7, up[i + 1], up[i]),
            jnp.where(slot == 0, down[i], down[i + 1]),
            shifted_rows(q, 1),
            shifted_rows(q, -1),
            jnp.where(x == 14, 0.0, ahead_x(q, 2)),
            jnp.where(x == 0, 0.0, ahead_x(q, -2)),
        )
        for i, q in enumerate(groups)
    ]


def set_level(here, near, m, t, w, g, p):
    diag = m
    for i, other in enumerate(near):
        face = 0.5 * (here + other)
        diag = diag + face
        t[2 * i, p], t[2 * i + 1, p] = as_factors(face)
    w[0, p], w[1, p] = inverse_factors(diag)
    if g is not None:
        g[0, p], g[1, p] = as_factors(diag)


def gathered_inflow(near, t, p):
    a = sum(t[2 * i, p] * q for i, q in enumerate(near[1:], 1)) + t[0, p] * near[0]
    b = sum(t[2 * i + 1, p] * q for i, q in enumerate(near[1:], 1)) + t[1, p] * near[0]
    return a + flip(b)


def factors(ref, p):
    return ref[0, p], ref[1, p]


def folded(planes):
    lane = lanes(planes[0].shape[0])
    for bit in (1, 16, 32):
        low = (lane & bit) == 0
        planes = [
            jnp.where(low, a, b) + swap_x(jnp.where(low, b, a), bit) for a, b in zip(planes[0::2], planes[1::2])
        ]
    return planes[0]


BATCH = 8


def batches(n, body):
    def run(i, carry):
        body(pl.multiple_of(i * BATCH, BATCH))
        return carry

    lax.fori_loop(0, n // BATCH, run, 0)


def level4(f4, s4, m4, t4):
    real = real_lanes(s4[0].shape[0])
    start = []
    for k, near in enumerate(near_level4(s4)):
        faces = [0.5 * (s4[k] + other) for other in near]
        fa = inverse_factors(sum(faces[1:]) + faces[0] + m4[k])
        start.append(product(fa, f4[k]))
        for i, face in enumerate(faces):
            q = product(fa, face)
            other = flip(q)
            t4[2 * i, k] = jnp.where(real, q, other)
            t4[2 * i + 1, k] = jnp.where(real, -other, q)
    turned = [flip(q) for q in start]
    e, o = start, turned
    for sweep in range(COARSE_SWEEPS - 1):
        pairs = list(zip(near_level4(e), near_level4(o)))
        e_next, o_next = [], []
        for k, (ne, no) in enumerate(pairs):
            ab = [(t4[2 * i, k], t4[2 * i + 1, k]) for i in range(6)]
            x = [a * p + b * q for (a, b), p, q in zip(ab, ne, no)]
            y = [a * q - b * p for (a, b), p, q in zip(ab, ne, no)]
            e_next.append((keep * e[k] + start[k] + x[0]) + (x[1] + x[2]) + (x[3] + x[4]) + x[5])
            o_next.append((keep * o[k] + turned[k] + y[0]) + (y[1] + y[2]) + (y[3] + y[4]) + y[5])
        e, o = e_next, o_next
    return e


def coarse_solve(counts, cells, t3, w3, g3, t4, s3, va, vb, ea):
    nz, ny = counts
    groups = ny // 8
    zero = jnp.zeros((nz, LANES), F32)
    s3[0] = zero
    s3[ny + 1] = zero
    for ref in (va, vb):
        for p in (0, 1, 2, ny + 3, ny + 4, ny + 5):
            ref[p] = zero
    for p in (0, 1, ny + 2, ny + 3):
        for i in range(12):
            t3[i, p] = zero
        w3[0, p] = zero
        w3[1, p] = zero

    def load(p0):
        for i in range(BATCH):
            s3[p0 + i + 1] = cells[p0 + i, 1]

    batches(ny, load)

    def setup(p0):
        planes = [s3[p0 + i] for i in range(BATCH + 2)]
        for i, near in enumerate(near_level3(planes)):
            p = p0 + i
            set_level(planes[i + 1], near, cells[p, 2], t3, w3, g3, p + 2)
            va[p + 3] = product(factors(w3, p + 2), cells[p, 0])

    batches(ny, setup)
    s4 = [0.125 * folded([cells[8 * k + j, 1] for j in range(8)]) for k in range(groups)]
    m4 = [0.5 * folded([cells[8 * k + j, 2] for j in range(8)]) for k in range(groups)]

    def swept3(here, near, p):
        gain = cells[jnp.clip(p, 0, ny - 1), 0] + gathered_inflow(near, t3, p + 2)
        return keep * here + product(factors(w3, p + 2), gain)

    def pre(p0):
        planes = [va[p0 + i + 2] for i in range(BATCH + 2)]
        for i, near in enumerate(near_level3(planes)):
            p = p0 + i
            gain = cells[p, 0] + gathered_inflow(near, t3, p + 2)
            vb[p + 3] = keep * planes[i + 1] + product(factors(w3, p + 2), gain)

    batches(ny, pre)

    def restrict(p0):
        planes = [vb[p0 + i + 2] for i in range(BATCH + 2)]
        gains = []
        for i, near in enumerate(near_level3(planes)):
            p = p0 + i
            gain = cells[p, 0] + gathered_inflow(near, t3, p + 2)
            gains.append(gain - product(factors(g3, p + 2), planes[i + 1]))
        ea[p0 // BATCH] = 0.5 * folded(gains)

    batches(ny, restrict)
    for k, q in enumerate(level4([ea[k] for k in range(groups)], s4, m4, t4)):
        ea[k] = q

    mine = lax.axis_index("gy")
    lane = lanes(nz)
    planes = []
    for d in range(-3, 4):
        p = mine + d
        on = jnp.where((p >= 0) & (p < ny), 1.0, 0.0)
        q = jnp.clip(p, 0, ny - 1)
        corr = jnp.take_along_axis(ea[q // 8], slot_lanes(lane, jnp.full((nz, LANES), q % 8, jnp.int32)), axis=1)
        planes.append(vb[p + 3] + on * corr)
    for reach in (2, 1):
        planes = [
            swept3(here, near, mine + d)
            for d, here, near in zip(range(-reach, reach + 1), planes[1:-1], near_level3(planes))
        ]
    return planes


def up_kernel(counts, cells, cmid, cleft, cright, *rest):
    kept1, kept0, out, rest = rest[0], rest[1], rest[2], rest[3:]
    tz2, ty2, tx2, w2, v1, f1, tz1, ty1, tx1, w1, v0, f0, tz0, ty0, tx0, w0 = rest[:16]
    t3, w3, g3, t4, s3, va, vb, ea, near, a2, b2, f2, e1, a1, b1, e0, a0, b0, sem = rest[16:]
    copies = []
    for i, dst in enumerate(rest[:16]):
        src, dst = (
            (kept1.at[6 + i, :, 0:12, 0:16], dst) if i < 4
            else (kept1.at[i - 4], dst.at[:, KEPT1]) if i < 10
            else (kept0.at[i - 10], dst.at[:, KEPT0])
        )
        copies.append(pltpu.make_async_copy(src, dst, sem.at[i]))
    sent(copies)
    nz = counts[0]
    gz = lax.axis_index("gz")
    for d, q in enumerate(coarse_solve(counts, cells, t3, w3, g3, t4, s3, va, vb, ea)):
        near[d] = q

    lane4, zero4 = lanes(4), jnp.zeros((4, LANES), F32)

    def unpack(z):
        for ref in (a2, f2):
            for c in (0, 1):
                ref[c, z, 8:12] = zero4
        for lo, src in ((0, cmid), (4, cright), (12, cleft)):
            q = src[z]
            turned = {k: ahead_x(q, k) if k else q for k in range(-3, 4)}
            for k, (ref, c) in enumerate(((a2, 0), (a2, 1), (f2, 0), (f2, 1))):
                val = turned[k]
                for i in range(1, 4):
                    val = jnp.where((lane4 & 3) == i, turned[k - i], val)
                ref[c, z, lo : lo + 4] = val

    each(0, 12, unpack)
    r16, l16 = row_ids(16), lanes(16)
    cell = l16 // 8
    for dz in (-1, 0, 1):
        row = jnp.clip(gz + dz, 0, nz - 1)
        on = jnp.where((gz + dz >= 0) & (gz + dz < nz), 1.0, 0.0)
        before, own, after = (near[d, pl.ds(row, 1), :] * on for d in range(3))
        rows = jnp.where(r16 < 4, own, jnp.where(r16 < 8, after, jnp.where(r16 < 12, 0.0, before)))
        for c in (0, 1):
            for zz in (0, 1):
                corr = jnp.take_along_axis(rows, cell + 16 * ((r16 // 2) & 1) + (64 * c + 32 * zz), axis=1)
                for z in (4 * dz + 4 + 2 * zz, 4 * dz + 5 + 2 * zz):
                    a2[c, z] = a2[c, z] + corr

    landed(copies)
    each(1, 11, lambda z: put(b2, z, swept(z, 4, a2, f2, tz2, ty2, tx2, w2)))
    each(2, 10, lambda z: put(a2, z, swept(z, 4, b2, f2, tz2, ty2, tx2, w2)))

    def widen1(z):
        for c in (0, 1):
            q = a2[c, z]
            for k in (0, 1):
                e1.at[c, z][pl.ds(k, 8, stride=2), :] = q[0:8]
                e1.at[c, z][pl.ds(16 + k, 4, stride=2), :] = q[12:16]

    each(2, 10, widen1)
    def correct1(z):
        e = pair(e1, z)
        for k in (2 * z, 2 * z + 1):
            put(a1, k, add(pair(v1, k), e))

    each(3, 9, correct1)
    for k, z in ((5, 2), (18, 9)):
        put(a1, k, add(pair(v1, k), pair(e1, z)))
    each(6, 18, lambda z: put(b1, z, swept(z, 2, a1, f1, tz1, ty1, tx1, w1)))
    each(7, 17, lambda z: put(a1, z, swept(z, 2, b1, f1, tz1, ty1, tx1, w1)))

    def widen0(z):
        for c in (0, 1):
            q = a1[c, z]
            for k in (0, 1):
                e0.at[c, z][pl.ds(k, 8, stride=2), :] = q[0:8]
                e0.at[c, z][pl.ds(16 + k, 2, stride=2), :] = q[8:10]
                e0.at[c, z][pl.ds(20 + k, 2, stride=2), :] = q[22:24]

    each(7, 17, widen0)
    def correct0(z):
        e = pair(e0, z)
        for k in (2 * z - 12, 2 * z - 11):
            put(a0, k, add(pair(v0, k), e))

    each(7, 17, correct0)
    each(3, 21, lambda z: put(b0, z, swept(z, 1, a0, f0, tz0, ty0, tx0, w0)))

    def last(z):
        q = swept(z, 1, b0, f0, tz0, ty0, tx0, w0)
        out[0, z - 4] = q[0][0:16]
        out[1, z - 4] = q[1][0:16]

    each(4, 20, last)


def run(kernel, name, args, outs, scratch, smem=(), far_in=(), far_out=(), copies=0, vmem=32 * 1024 * 1024):
    def specs(n, smem, far):
        spaces = [pltpu.SMEM if i in smem else pltpu.HBM if i in far else pltpu.VMEM for i in range(n)]
        return [pl.BlockSpec(memory_space=space) for space in spaces]

    return pl.pallas_call(
        kernel,
        name=name,
        out_shape=[jax.ShapeDtypeStruct(s, F32) for s in outs],
        in_specs=specs(len(args), smem, far_in),
        out_specs=specs(len(outs), (), far_out),
        scratch_shapes=[pltpu.VMEM(s, F32) if isinstance(s, tuple) else s for s in scratch]
        + ([pltpu.SemaphoreType.DMA((copies,))] if copies else []),
        compiler_params=pltpu.CompilerParams(vmem_limit_bytes=vmem),
    )(*args)


def shifts(axis):
    n = lax.axis_size(axis)
    up = [(i, i + 1) for i in range(n - 1)]
    return up, [(j, i) for i, j in up]


def around(block, axis, dim, width):
    up, down = shifts(axis)
    size = block.shape[dim]
    before = lax.ppermute(lax.slice_in_dim(block, size - width, size, axis=dim), axis, up)
    after = lax.ppermute(lax.slice_in_dim(block, 0, width, axis=dim), axis, down)
    return before, after


def window(block, dim, width):
    before, after = around(block, "gz", dim, width)
    mid = jnp.concatenate([before, block, after], axis=dim)
    left, right = around(mid, "gy", dim + 1, width)
    return mid, left, right


def body(source, labels, phase_table):
    nz, ny = lax.axis_size("gz"), lax.axis_size("gy")

    marks = lax.optimization_barrier(labels.astype(F32))[None]

    def edge(lo, hi):
        return jnp.concatenate([source[:, lo:hi], marks[:, lo:hi]], axis=0)

    up, down = shifts("gz")
    zb = lax.ppermute(edge(12, 16), "gz", up)
    za = lax.ppermute(edge(0, 4), "gz", down)

    def side(lo, hi):
        own = jnp.concatenate([source[:, :, lo:hi], marks[:, :, lo:hi]], axis=0)
        return jnp.concatenate([zb[:, :, lo:hi], own, za[:, :, lo:hi]], axis=1)

    up, down = shifts("gy")
    left = lax.ppermute(side(12, 16), "gy", up)
    right = lax.ppermute(side(0, 4), "gy", down)

    near_c, far_c = run(
        coeff_kernel, "coefficients", (labels, phase_table),
        [(2, 8, 8, LANES), (1, 2 * LANES)],
        [(4, 8, 16, LANES), (4, 8, 8, LANES), (4, 4, 4, LANES), (2, 8, LANES)], smem=(1,),
    )
    win, win2 = (2, 24, 24, LANES), (2, 12, 16, LANES)
    win0 = (2, KEPT0.stop - KEPT0.start, 24, LANES)
    win1 = (2, KEPT1.stop - KEPT1.start, 24, LANES)
    msg, state0 = run(
        lambda *refs: fine_kernel((16 * nz, 16 * ny), *refs), "fine_down",
        (source, labels, zb, za, left, right, phase_table, near_c),
        [(3, 8, 8, LANES), (12, *win0)],
        [win] * 6 + [pltpu.VMEM((24, 24, LANES), jnp.int32)] + [win] * 4 + [(2, 8, 24, LANES)],
        smem=(6,), far_out=(1,), copies=6, vmem=MOST_VMEM,
    )
    msg, state1 = run(
        lambda *refs: middle_kernel(((8 * nz, 8 * ny), (4 * nz, 4 * ny)), *refs), "middle_down",
        (*window(msg, 1, 8), far_c),
        [(MESSAGE, LANES), (20, *win1)],
        [win] * 6 + [win2] * 4 + [win] * 4 + [(2, 12, 24, LANES)] + [win2] * 6 + [(2, 2, 16, LANES), (8, LANES)],
        far_out=(1,), copies=10, vmem=MOST_VMEM,
    )
    column = lax.all_to_all(jnp.broadcast_to(msg[None], (nz, MESSAGE, LANES)), "gz", 0, 0)
    cells, cmid = run(
        spread_kernel, "spread", (column.reshape(nz * MESSAGE, LANES),), [(ny, 3, nz, LANES), (12, 4, LANES)], [],
    )
    cells = lax.all_to_all(cells, "gy", 0, 0)
    cwin = (cmid, *around(cmid, "gy", 1, 4))

    def whole(n, pad):
        return (n, ny + 2 * pad, nz, LANES)

    small = (ny // 8, nz, LANES)
    return run(
        lambda *refs: up_kernel((nz, ny), *refs), "coarse_and_up",
        (cells, *cwin, state1, state0),
        [(2, 16, 16, LANES)],
        [win2] * 4 + [win] * 12
        + [whole(12, 2), whole(2, 2), whole(2, 2), (12, *small)]
        + [whole(1, 1)[1:]] + [whole(1, 3)[1:]] * 2 + [small, (3, nz, LANES)]
        + [win2] * 3 + [(2, 12, 24, LANES), win, win, win, win, win],
        far_in=(4, 5), copies=16, vmem=MOST_VMEM,
    )[0]


def solution(mesh):
    in_specs = (P(None, "gz", "gy", None), P("gz", "gy", None), P())
    out_specs = P(None, "gz", "gy", None)
    return jax.shard_map(body, mesh=mesh, in_specs=in_specs, out_specs=out_specs, check_vma=False)
```

```python
import jax
import jax.numpy as jnp
from jax import lax
from jax.experimental import pallas as pl
from jax.experimental.pallas import tpu as pltpu
from jax.sharding import PartitionSpec as P

PHASES = 4
COARSE_SWEEPS = 8
LANES = 128
relax = 0.7
keep = 1.0 - relax
mass_scale = 0.01
F32 = jnp.float32
MESSAGE = 24
MOST_VMEM = 51 * 1024 * 1024


def lanes(rows):
    return lax.broadcasted_iota(jnp.int32, (rows, LANES), 1)


def row_ids(rows):
    return lax.broadcasted_iota(jnp.int32, (rows, LANES), 0)


def ahead_x(q, k):
    return pltpu.roll(q, (-k) % LANES, 1)


def ahead_y(q, k):
    return pltpu.roll(q, (-k) % q.shape[0], 0)


def pair_x(q, k):
    return q + swap_x(q, k)


def swap_x(q, k):
    return jnp.where((lanes(q.shape[0]) & k) == 0, ahead_x(q, k), ahead_x(q, -k))


def interleave(re, im):
    return jnp.where((lanes(re.shape[0]) & 1) == 0, re, im)


def separate(q):
    even = (lanes(q.shape[0]) & 1) == 0
    return jnp.where(even, q, ahead_x(q, -1)), jnp.where(even, ahead_x(q, 1), q)


def each(lo, hi, body, step=4):
    full = (hi - lo) // step

    def run(i, carry):
        for j in range(step):
            body(lo + i * step + j)
        return carry

    lax.fori_loop(0, full, run, 0)
    for z in range(lo + full * step, hi):
        body(z)


def sent(copies):
    for copy in copies:
        copy.start()
    return copies


def landed(copies):
    for copy in copies:
        copy.wait()


def times(t, q):
    return t[0] * q[0] - t[1] * q[1], t[0] * q[1] + t[1] * q[0]


def pair(ref, z):
    return ref[0, z], ref[1, z]


def put(ref, z, q):
    ref[0, z] = q[0]
    ref[1, z] = q[1]


def add(*terms):
    return sum(t[0] for t in terms[1:]) + terms[0][0], sum(t[1] for t in terms[1:]) + terms[0][1]


def both(fn, q, k):
    return fn(q[0], k), fn(q[1], k)


def inside(rows, wrap, z, first_z, first_y, size_z, size_y, dead=()):
    r = row_ids(rows)
    y = jnp.where(r >= wrap, r - rows, r) + first_y
    ok = (y >= 0) & (y < size_y)
    plane = jnp.full((rows, LANES), first_z + z, jnp.int32)
    ok = ok & (plane >= 0) & (plane < size_z)
    if dead:
        ok = ok & ((r < dead[0]) | (r >= dead[1]))
    return ok


def make_faces(z, shift, ok, s, m, tz, ty, tx, w, g=None):
    lane = lanes(s.shape[2])
    last = lane >= LANES - shift
    initial = lane < shift
    diag = []
    for c in (0, 1):
        here = s[c, z]
        up = 0.5 * (here + s[c, z + 1])
        down = 0.5 * (here + s[c, z - 1])
        side = 0.5 * (here + ahead_y(here, 1))
        right = 0.5 * (here + jnp.where(last, 0.0, ahead_x(here, shift)))
        left = 0.5 * (here + jnp.where(initial, 0.0, ahead_x(here, -shift)))
        tz[c, z] = up
        ty[c, z] = side
        tx[c, z] = jnp.where(last, 0.0, right)
        diag.append(m[c, z] + (up + down) + (side + ahead_y(side, -1)) + (right + left))
    inv = jnp.where(ok, relax / (diag[0] * diag[0] + diag[1] * diag[1]), 0.0)
    q = (diag[0] * inv, -(diag[1] * inv))
    put(w, z, q)
    if g is not None:
        put(g, z, diag)
    return q


def inflow(z, shift, v, tz, ty, tx):
    here = pair(v, z)
    side, right = pair(ty, z), pair(tx, z)
    return add(
        times(pair(tz, z), pair(v, z + 1)),
        times(pair(tz, z - 1), pair(v, z - 1)),
        times(side, both(ahead_y, here, 1)),
        both(ahead_y, times(side, here), -1),
        times(right, both(ahead_x, here, shift)),
        both(ahead_x, times(right, here), -shift),
    )


def swept(z, shift, v, f, tz, ty, tx, w):
    here = pair(v, z)
    step = times(pair(w, z), add(pair(f, z), inflow(z, shift, v, tz, ty, tx)))
    return keep * here[0] + step[0], keep * here[1] + step[1]


def residual(z, shift, v, f, tz, ty, tx, g):
    out = times(pair(g, z), pair(v, z))
    gain = add(pair(f, z), inflow(z, shift, v, tz, ty, tx))
    return gain[0] - out[0], gain[1] - out[1]


def rows_paired(buf, at, start, count):
    plane = buf.at[at]
    return plane[pl.ds(start, count, stride=2), :] + plane[pl.ds(start + 1, count, stride=2), :]


def packed_row(stack):
    lane, row = lanes(8), row_ids(8)
    cells = jnp.take_along_axis(stack, 8 * (lane % 16), axis=1)
    return jnp.sum(jnp.where(lane // 16 == row, cells, 0.0), axis=0, keepdims=True)


def lookup(lab, table):
    out = []
    for c in range(4):
        scale = 1.0 if c < 2 else mass_scale
        val = [table[p, c] * F32(scale) for p in range(PHASES)]
        out.append(jnp.where(lab == 0, val[0], jnp.where(lab == 1, val[1], jnp.where(lab == 2, val[2], val[3]))))
    return out


def coeff_kernel(labels, table, near_out, far_out, buf, c1, c2, stack):
    for z in range(8):
        a, b = lookup(labels[2 * z], table), lookup(labels[2 * z + 1], table)
        for c in range(4):
            buf[c, z] = a[c] + b[c]
    for z in range(8):
        for c in range(4):
            c1[c, z] = pair_x(rows_paired(buf, (c, z), 0, 8), 1) * (0.125 if c < 2 else 0.5)
    for z in range(8):
        near_out[0, z] = interleave(c1[0, z], c1[1, z])
        near_out[1, z] = interleave(c1[2, z], c1[3, z])
    for c in range(4):
        scale = 0.125 if c < 2 else 0.5
        for z in range(4):
            buf[c, z, 0:8] = c1[c, 2 * z] + c1[c, 2 * z + 1]
        for z in range(4):
            c2[c, z] = pair_x(rows_paired(buf, (c, z), 0, 4), 2) * scale
        for z in range(2):
            buf[c, 4 + z, 0:4] = c2[c, 2 * z] + c2[c, 2 * z + 1]
        for z in range(2):
            stack[c // 2, (c % 2) * 4 + 2 * z : (c % 2) * 4 + 2 * z + 2] = (
                pair_x(rows_paired(buf, (c, 4 + z), 0, 2), 4) * scale
            )
    far_out[:, 0:LANES] = packed_row(stack[0])
    far_out[:, LANES : 2 * LANES] = packed_row(stack[1])


KEPT0 = slice(2, 22)
KEPT1 = slice(5, 19)


def fine_kernel(
    sizes, source, labels, zb, za, left, right, table, near_c, msg_out, *rest
):
    keeps, v, f, tz, ty, tx, w, lab, s, m, g, first, buf, sem = rest
    first_z = lax.axis_index("gz") * 16 - 4
    first_y = lax.axis_index("gy") * 16

    def load(z, own):
        dst = (f.at[0, z], f.at[1, z], lab.at[z])
        for c in range(3):
            dst[c][0:16] = own[c]
            dst[c][16:20] = right[c, z].astype(dst[c].dtype)
            dst[c][20:24] = left[c, z].astype(dst[c].dtype)
        ok = inside(24, 20, z, first_z, first_y, *sizes)
        vals = lookup(lab[z], table)
        for c in (0, 1):
            s[c, z] = jnp.where(ok, vals[c], 0.0)
            m[c, z] = vals[2 + c]

    for z in range(4):
        load(z, (zb[0, z], zb[1, z], zb[2, z].astype(jnp.int32)))
        load(z + 20, (za[0, z], za[1, z], za[2, z].astype(jnp.int32)))
    each(0, 16, lambda z: load(z + 4, (source[0, z], source[1, z], labels[z])))

    def faces(z):
        ok = inside(24, 20, z, first_z, first_y, *sizes)
        put(first, z, times(make_faces(z, 1, ok, s, m, tz, ty, tx, w, g), pair(f, z)))

    each(1, 23, faces)

    def kept(i, ref):
        return pltpu.make_async_copy(ref.at[:, KEPT0], keeps.at[i], sem.at[i])

    copies = sent([kept(i, ref) for i, ref in enumerate((v, f, tz, ty, tx, w)) if i])
    each(2, 22, lambda z: put(v, z, swept(z, 1, first, f, tz, ty, tx, w)))
    copies += sent([kept(0, v)])

    def restrict(z):
        a = residual(2 * z + 4, 1, v, f, tz, ty, tx, g)
        b = residual(2 * z + 5, 1, v, f, tz, ty, tx, g)
        put(buf, z, add(a, b))

    each(0, 8, restrict, 4)

    def finish(z):
        re, im = (0.5 * pair_x(rows_paired(buf, (c, z), 0, 8), 1) for c in (0, 1))
        msg_out[2, z] = interleave(re, im)
        msg_out[0, z] = near_c[0, z]
        msg_out[1, z] = near_c[1, z]

    each(0, 8, finish)
    landed(copies)


def middle_kernel(
    sizes, mid, left, right, far_c,
    msg_out, *rest
):
    keeps, rest = rest[0], rest[1:]
    v, f, tz, ty, tx, w, tz2, ty2, tx2, w2, s, m, g, first, buf, s2, m2, f2, g2, first2, v2, buf2, stack, sem = rest
    gz, gy = lax.axis_index("gz"), lax.axis_index("gy")

    def load(z):
        for lo, src in ((0, mid), (8, right), (16, left)):
            for i, ref in enumerate((s, m, f)):
                re, im = separate(src[i, z])
                ref[0, z, lo : lo + 8] = re
                ref[1, z, lo : lo + 8] = im

    each(0, 24, load)

    def faces(z):
        ok = inside(24, 16, z, gz * 8 - 8, gy * 8, *sizes[0])
        put(first, z, times(make_faces(z, 2, ok, s, m, tz, ty, tx, w, g), pair(f, z)))

    each(1, 23, faces)

    def kept(i, ref):
        return pltpu.make_async_copy(ref.at[:, KEPT1], keeps.at[i], sem.at[i])

    copies = sent([kept(i, ref) for i, ref in enumerate((v, f, tz, ty, tx, w)) if i])
    each(2, 22, lambda z: put(v, z, swept(z, 2, first, f, tz, ty, tx, w)))
    copies += sent([kept(0, v)])

    def coarser(dst, scale, z):
        for c in (0, 1):
            dst[c, z, 0:8] = scale * pair_x(rows_paired(buf, (c, z), 0, 8), 2)
            dst[c, z, 8:12] = jnp.zeros((4, LANES), F32)
            dst[c, z, 12:16] = scale * pair_x(rows_paired(buf, (c, z), 16, 4), 2)

    for src, dst, scale in ((s, s2, 0.125), (m, m2, 0.5)):
        each(0, 12, lambda z: put(buf, z, add(pair(src, 2 * z), pair(src, 2 * z + 1))))
        each(0, 12, lambda z: coarser(dst, scale, z))

    def restrict(z):
        put(buf, z, add(residual(2 * z, 2, v, f, tz, ty, tx, g), residual(2 * z + 1, 2, v, f, tz, ty, tx, g)))

    each(2, 10, restrict, 4)
    each(2, 10, lambda z: coarser(f2, 0.5, z))

    def faces2(z):
        ok = inside(16, 12, z, gz * 4 - 4, gy * 4, *sizes[1], dead=(8, 12))
        return make_faces(z, 4, ok, s2, m2, tz2, ty2, tx2, w2, g2)

    faces2(1)
    tz2[0, 0] = 0.5 * (s2[0, 0] + s2[0, 1])
    tz2[1, 0] = 0.5 * (s2[1, 0] + s2[1, 1])
    each(2, 10, lambda z: put(first2, z, times(faces2(z), pair(f2, z))))
    faces2(10)
    copies += sent([pltpu.make_async_copy(ref, keeps.at[6 + i, :, 0:12, 0:16], sem.at[6 + i]) for i, ref in enumerate((tz2, ty2, tx2, w2))])
    each(3, 9, lambda z: put(v2, z, swept(z, 4, first2, f2, tz2, ty2, tx2, w2)))
    which = lanes(4) & 3
    for z in range(4):
        a, b = pair(v2, z + 4), pair(f2, z + 4)
        msg_out[0, 8 + 4 * z : 12 + 4 * z] = jnp.where(
            which < 2, jnp.where(which == 0, a[0][0:4], a[1][0:4]), jnp.where(which == 2, b[0][0:4], b[1][0:4])
        )
    for z in range(2):
        a = residual(2 * z + 4, 4, v2, f2, tz2, ty2, tx2, g2)
        b = residual(2 * z + 5, 4, v2, f2, tz2, ty2, tx2, g2)
        put(buf2, z, add(a, b))
    for z in range(2):
        for c in (0, 1):
            stack[4 * c + 2 * z : 4 * c + 2 * z + 2] = 0.5 * pair_x(rows_paired(buf2, (c, z), 0, 2), 4)
    msg_out[0, 0:1] = packed_row(stack[...])
    msg_out[0, 1:2] = far_c[:, 0:LANES]
    msg_out[0, 2:3] = far_c[:, LANES : 2 * LANES]
    msg_out[0, 3:8] = jnp.zeros((5, LANES), F32)
    message = msg_out[0]
    for g in range(1, msg_out.shape[0]):
        msg_out[g] = message
    landed(copies)


def spread_kernel(column, cells, near):
    ny, _, nz, _ = cells.shape
    for k in range(3):
        q = column[pl.ds(k, nz, stride=MESSAGE), :]
        for p in range(ny):
            cells[p, k] = q
    mine = lax.axis_index("gz")
    for d in (-1, 0, 1):
        p = jnp.clip(mine + d, 0, nz - 1)
        on = jnp.where((mine + d >= 0) & (mine + d < nz), 1.0, 0.0)
        q = on * column[pl.ds(pl.multiple_of(p * MESSAGE + 8, 8), 16), :]
        for z in range(4):
            near[4 * d + 4 + z] = q[4 * z : 4 * z + 4]


def real_lanes(rows):
    return lanes(rows) < 64


def flip(q):
    return pltpu.roll(q, 64, 1)


def as_factors(q):
    real, other = real_lanes(q.shape[0]), flip(q)
    return jnp.where(real, q, other), jnp.where(real, other, -q)


def product(t, q):
    return t[0] * q + flip(t[1] * q)


def inverse_factors(diag):
    real, other = real_lanes(diag.shape[0]), flip(diag)
    inv = relax / (diag * diag + other * other)
    return jnp.where(real, diag, other) * inv, jnp.where(real, -other, diag) * inv


def shifted_rows(q, k):
    edge = q.shape[0] - 1 if k > 0 else 0
    return jnp.where(row_ids(q.shape[0]) == edge, 0.0, ahead_y(q, k))


def near_level3(planes):
    n = planes[0].shape[0]
    lane = lanes(n)
    low_z, low_y, x = (lane & 32) == 0, (lane & 16) == 0, lane & 15
    turned = [swap_x(q, 16) for q in planes]
    out = []
    for i, q in enumerate(planes[1:-1]):
        qz = swap_x(q, 32)
        out.append(
            (
                jnp.where(low_y, turned[i + 1], turned[i + 2]),
                jnp.where(low_y, turned[i], turned[i + 1]),
                jnp.where(low_z, qz, shifted_rows(qz, 1)),
                jnp.where(low_z, shifted_rows(qz, -1), qz),
                jnp.where(x == 15, 0.0, ahead_x(q, 1)),
                jnp.where(x == 0, 0.0, ahead_x(q, -1)),
            )
        )
    return out


def slot_lanes(lane, slot):
    return (lane & 78) | ((slot & 4) << 3) | ((slot & 2) << 3) | (slot & 1)


def slot_of(lane):
    return ((lane >> 3) & 4) | ((lane >> 3) & 2) | (lane & 1)


def near_level4(groups):
    n = groups[0].shape[0]
    lane = lanes(n)
    slot, x = slot_of(lane), lane & 14
    nxt, prv = slot_lanes(lane, slot + 1), slot_lanes(lane, slot + 7)
    zero = jnp.zeros_like(groups[0])
    up = [jnp.take_along_axis(q, nxt, axis=1) for q in groups] + [zero]
    down = [zero] + [jnp.take_along_axis(q, prv, axis=1) for q in groups]
    return [
        (
            jnp.where(slot == 7, up[i + 1], up[i]),
            jnp.where(slot == 0, down[i], down[i + 1]),
            shifted_rows(q, 1),
            shifted_rows(q, -1),
            jnp.where(x == 14, 0.0, ahead_x(q, 2)),
            jnp.where(x == 0, 0.0, ahead_x(q, -2)),
        )
        for i, q in enumerate(groups)
    ]


def set_level(here, near, m, t, w, g, p):
    diag = m
    for i, other in enumerate(near):
        face = 0.5 * (here + other)
        diag = diag + face
        t[2 * i, p], t[2 * i + 1, p] = as_factors(face)
    w[0, p], w[1, p] = inverse_factors(diag)
    if g is not None:
        g[0, p], g[1, p] = as_factors(diag)


def gathered_inflow(near, t, p):
    a = sum(t[2 * i, p] * q for i, q in enumerate(near[1:], 1)) + t[0, p] * near[0]
    b = sum(t[2 * i + 1, p] * q for i, q in enumerate(near[1:], 1)) + t[1, p] * near[0]
    return a + flip(b)


def factors(ref, p):
    return ref[0, p], ref[1, p]


def folded(planes):
    lane = lanes(planes[0].shape[0])
    for bit in (1, 16, 32):
        low = (lane & bit) == 0
        planes = [
            jnp.where(low, a, b) + swap_x(jnp.where(low, b, a), bit) for a, b in zip(planes[0::2], planes[1::2])
        ]
    return planes[0]


BATCH = 8


def batches(n, body):
    def run(i, carry):
        body(pl.multiple_of(i * BATCH, BATCH))
        return carry

    lax.fori_loop(0, n // BATCH, run, 0)


def level4(f4, s4, m4, t4):
    real = real_lanes(s4[0].shape[0])
    start = []
    for k, near in enumerate(near_level4(s4)):
        faces = [0.5 * (s4[k] + other) for other in near]
        fa = inverse_factors(sum(faces[1:]) + faces[0] + m4[k])
        start.append(product(fa, f4[k]))
        for i, face in enumerate(faces):
            q = product(fa, face)
            other = flip(q)
            t4[2 * i, k] = jnp.where(real, q, other)
            t4[2 * i + 1, k] = jnp.where(real, -other, q)
    turned = [flip(q) for q in start]
    e, o = start, turned
    for sweep in range(COARSE_SWEEPS - 1):
        pairs = list(zip(near_level4(e), near_level4(o)))
        e_next, o_next = [], []
        for k, (ne, no) in enumerate(pairs):
            ab = [(t4[2 * i, k], t4[2 * i + 1, k]) for i in range(6)]
            x = [a * p + b * q for (a, b), p, q in zip(ab, ne, no)]
            y = [a * q - b * p for (a, b), p, q in zip(ab, ne, no)]
            e_next.append((keep * e[k] + start[k] + x[0]) + (x[1] + x[2]) + (x[3] + x[4]) + x[5])
            o_next.append((keep * o[k] + turned[k] + y[0]) + (y[1] + y[2]) + (y[3] + y[4]) + y[5])
        e, o = e_next, o_next
    return e


def coarse_solve(counts, cells, t3, w3, g3, t4, s3, va, vb, ea):
    nz, ny = counts
    groups = ny // 8
    zero = jnp.zeros((nz, LANES), F32)
    s3[0] = zero
    s3[ny + 1] = zero
    for ref in (va, vb):
        for p in (0, 1, 2, ny + 3, ny + 4, ny + 5):
            ref[p] = zero
    for p in (0, 1, ny + 2, ny + 3):
        for i in range(12):
            t3[i, p] = zero
        w3[0, p] = zero
        w3[1, p] = zero

    def load(p0):
        for i in range(BATCH):
            s3[p0 + i + 1] = cells[p0 + i, 1]

    batches(ny, load)

    def setup(p0):
        planes = [s3[p0 + i] for i in range(BATCH + 2)]
        for i, near in enumerate(near_level3(planes)):
            p = p0 + i
            set_level(planes[i + 1], near, cells[p, 2], t3, w3, g3, p + 2)
            va[p + 3] = product(factors(w3, p + 2), cells[p, 0])

    batches(ny, setup)
    s4 = [0.125 * folded([cells[8 * k + j, 1] for j in range(8)]) for k in range(groups)]
    m4 = [0.5 * folded([cells[8 * k + j, 2] for j in range(8)]) for k in range(groups)]

    def swept3(here, near, p):
        gain = cells[jnp.clip(p, 0, ny - 1), 0] + gathered_inflow(near, t3, p + 2)
        return keep * here + product(factors(w3, p + 2), gain)

    def pre(p0):
        planes = [va[p0 + i + 2] for i in range(BATCH + 2)]
        for i, near in enumerate(near_level3(planes)):
            p = p0 + i
            gain = cells[p, 0] + gathered_inflow(near, t3, p + 2)
            vb[p + 3] = keep * planes[i + 1] + product(factors(w3, p + 2), gain)

    batches(ny, pre)

    def restrict(p0):
        planes = [vb[p0 + i + 2] for i in range(BATCH + 2)]
        gains = []
        for i, near in enumerate(near_level3(planes)):
            p = p0 + i
            gain = cells[p, 0] + gathered_inflow(near, t3, p + 2)
            gains.append(gain - product(factors(g3, p + 2), planes[i + 1]))
        ea[p0 // BATCH] = 0.5 * folded(gains)

    batches(ny, restrict)
    for k, q in enumerate(level4([ea[k] for k in range(groups)], s4, m4, t4)):
        ea[k] = q

    mine = lax.axis_index("gy")
    lane = lanes(nz)
    planes = []
    for d in range(-3, 4):
        p = mine + d
        on = jnp.where((p >= 0) & (p < ny), 1.0, 0.0)
        q = jnp.clip(p, 0, ny - 1)
        corr = jnp.take_along_axis(ea[q // 8], slot_lanes(lane, jnp.full((nz, LANES), q % 8, jnp.int32)), axis=1)
        planes.append(vb[p + 3] + on * corr)
    for reach in (2, 1):
        planes = [
            swept3(here, near, mine + d)
            for d, here, near in zip(range(-reach, reach + 1), planes[1:-1], near_level3(planes))
        ]
    return planes


def up_kernel(counts, cells, cmid, cleft, cright, *rest):
    kept1, kept0, out, rest = rest[0], rest[1], rest[2], rest[3:]
    tz2, ty2, tx2, w2, v1, f1, tz1, ty1, tx1, w1, v0, f0, tz0, ty0, tx0, w0 = rest[:16]
    t3, w3, g3, t4, s3, va, vb, ea, near, a2, b2, f2, e1, a1, b1, e0, a0, b0, done, sem = rest[16:]
    copies = []
    for i, dst in enumerate(rest[:16]):
        src, dst = (
            (kept1.at[6 + i, :, 0:12, 0:16], dst) if i < 4
            else (kept1.at[i - 4], dst.at[:, KEPT1]) if i < 10
            else (kept0.at[i - 10], dst.at[:, KEPT0])
        )
        copies.append(pltpu.make_async_copy(src, dst, sem.at[i]))
    sent(copies)
    nz = counts[0]
    gz = lax.axis_index("gz")
    for d, q in enumerate(coarse_solve(counts, cells, t3, w3, g3, t4, s3, va, vb, ea)):
        near[d] = q

    lane4, zero4 = lanes(4), jnp.zeros((4, LANES), F32)

    def unpack(z):
        for ref in (a2, f2):
            for c in (0, 1):
                ref[c, z, 8:12] = zero4
        for lo, src in ((0, cmid), (4, cright), (12, cleft)):
            q = src[z]
            turned = {k: ahead_x(q, k) if k else q for k in range(-3, 4)}
            for k, (ref, c) in enumerate(((a2, 0), (a2, 1), (f2, 0), (f2, 1))):
                val = turned[k]
                for i in range(1, 4):
                    val = jnp.where((lane4 & 3) == i, turned[k - i], val)
                ref[c, z, lo : lo + 4] = val

    each(0, 12, unpack)
    r16, l16 = row_ids(16), lanes(16)
    cell = l16 // 8
    for dz in (-1, 0, 1):
        row = jnp.clip(gz + dz, 0, nz - 1)
        on = jnp.where((gz + dz >= 0) & (gz + dz < nz), 1.0, 0.0)
        before, own, after = (near[d, pl.ds(row, 1), :] * on for d in range(3))
        rows = jnp.where(r16 < 4, own, jnp.where(r16 < 8, after, jnp.where(r16 < 12, 0.0, before)))
        for c in (0, 1):
            for zz in (0, 1):
                corr = jnp.take_along_axis(rows, cell + 16 * ((r16 // 2) & 1) + (64 * c + 32 * zz), axis=1)
                for z in (4 * dz + 4 + 2 * zz, 4 * dz + 5 + 2 * zz):
                    a2[c, z] = a2[c, z] + corr

    landed(copies)
    each(1, 11, lambda z: put(b2, z, swept(z, 4, a2, f2, tz2, ty2, tx2, w2)))
    each(2, 10, lambda z: put(a2, z, swept(z, 4, b2, f2, tz2, ty2, tx2, w2)))

    def widen1(z):
        for c in (0, 1):
            q = a2[c, z]
            for k in (0, 1):
                e1.at[c, z][pl.ds(k, 8, stride=2), :] = q[0:8]
                e1.at[c, z][pl.ds(16 + k, 4, stride=2), :] = q[12:16]

    each(2, 10, widen1)
    def correct1(z):
        e = pair(e1, z)
        for k in (2 * z, 2 * z + 1):
            put(a1, k, add(pair(v1, k), e))

    each(3, 9, correct1)
    for k, z in ((5, 2), (18, 9)):
        put(a1, k, add(pair(v1, k), pair(e1, z)))
    each(6, 18, lambda z: put(b1, z, swept(z, 2, a1, f1, tz1, ty1, tx1, w1)))
    each(7, 17, lambda z: put(a1, z, swept(z, 2, b1, f1, tz1, ty1, tx1, w1)))

    def widen0(z):
        for c in (0, 1):
            q = a1[c, z]
            for k in (0, 1):
                e0.at[c, z][pl.ds(k, 8, stride=2), :] = q[0:8]
                e0.at[c, z][pl.ds(16 + k, 2, stride=2), :] = q[8:10]
                e0.at[c, z][pl.ds(20 + k, 2, stride=2), :] = q[22:24]

    each(7, 17, widen0)
    def correct0(z):
        e = pair(e0, z)
        for k in (2 * z - 12, 2 * z - 11):
            put(a0, k, add(pair(v0, k), e))

    each(7, 17, correct0)
    each(3, 21, lambda z: put(b0, z, swept(z, 1, a0, f0, tz0, ty0, tx0, w0)))

    def last(z):
        q = swept(z, 1, b0, f0, tz0, ty0, tx0, w0)
        done[0, z - 4] = q[0][0:16]
        done[1, z - 4] = q[1][0:16]

    copies = []
    for i in range(4):
        part = slice(4 * i, 4 * i + 4)
        for z in range(4):
            last(4 * i + z + 4)
        copies += sent([pltpu.make_async_copy(done.at[:, part], out.at[:, part], sem.at[16 + i])])
    landed(copies)


def run(kernel, name, args, outs, scratch, smem=(), far_in=(), far_out=(), copies=0, vmem=32 * 1024 * 1024):
    def specs(n, smem, far):
        spaces = [pltpu.SMEM if i in smem else pltpu.HBM if i in far else pltpu.VMEM for i in range(n)]
        return [pl.BlockSpec(memory_space=space) for space in spaces]

    return pl.pallas_call(
        kernel,
        name=name,
        out_shape=[jax.ShapeDtypeStruct(s, F32) for s in outs],
        in_specs=specs(len(args), smem, far_in),
        out_specs=specs(len(outs), (), far_out),
        scratch_shapes=[pltpu.VMEM(s, F32) if isinstance(s, tuple) else s for s in scratch]
        + ([pltpu.SemaphoreType.DMA((copies,))] if copies else []),
        compiler_params=pltpu.CompilerParams(vmem_limit_bytes=vmem),
    )(*args)


def shifts(axis):
    n = lax.axis_size(axis)
    up = [(i, i + 1) for i in range(n - 1)]
    return up, [(j, i) for i, j in up]


def around(block, axis, dim, width):
    up, down = shifts(axis)
    size = block.shape[dim]
    before = lax.ppermute(lax.slice_in_dim(block, size - width, size, axis=dim), axis, up)
    after = lax.ppermute(lax.slice_in_dim(block, 0, width, axis=dim), axis, down)
    return before, after


def window(block, dim, width):
    before, after = around(block, "gz", dim, width)
    mid = jnp.concatenate([before, block, after], axis=dim)
    left, right = around(mid, "gy", dim + 1, width)
    return mid, left, right


def body(source, labels, phase_table):
    nz, ny = lax.axis_size("gz"), lax.axis_size("gy")

    marks = lax.optimization_barrier(labels.astype(F32))[None]

    def edge(lo, hi):
        return jnp.concatenate([source[:, lo:hi], marks[:, lo:hi]], axis=0)

    up, down = shifts("gz")
    zb = lax.ppermute(edge(12, 16), "gz", up)
    za = lax.ppermute(edge(0, 4), "gz", down)

    def side(lo, hi):
        own = jnp.concatenate([source[:, :, lo:hi], marks[:, :, lo:hi]], axis=0)
        return jnp.concatenate([zb[:, :, lo:hi], own, za[:, :, lo:hi]], axis=1)

    up, down = shifts("gy")
    left = lax.ppermute(side(12, 16), "gy", up)
    right = lax.ppermute(side(0, 4), "gy", down)

    near_c, far_c = run(
        coeff_kernel, "coefficients", (labels, phase_table),
        [(2, 8, 8, LANES), (1, 2 * LANES)],
        [(4, 8, 16, LANES), (4, 8, 8, LANES), (4, 4, 4, LANES), (2, 8, LANES)], smem=(1,),
    )
    win, win2 = (2, 24, 24, LANES), (2, 12, 16, LANES)
    win0 = (2, KEPT0.stop - KEPT0.start, 24, LANES)
    win1 = (2, KEPT1.stop - KEPT1.start, 24, LANES)
    msg, state0 = run(
        lambda *refs: fine_kernel((16 * nz, 16 * ny), *refs), "fine_down",
        (source, labels, zb, za, left, right, phase_table, near_c),
        [(3, 8, 8, LANES), (20, *win0)],
        [win] * 6 + [pltpu.VMEM((24, 24, LANES), jnp.int32)] + [win] * 4 + [(2, 8, 24, LANES)],
        smem=(6,), far_out=(1,), copies=6, vmem=MOST_VMEM,
    )
    msg, state1 = run(
        lambda *refs: middle_kernel(((8 * nz, 8 * ny), (4 * nz, 4 * ny)), *refs), "middle_down",
        (*window(msg, 1, 8), far_c),
        [(nz, MESSAGE, LANES), (32, *win1)],
        [win] * 6 + [win2] * 4 + [win] * 4 + [(2, 12, 24, LANES)] + [win2] * 6 + [(2, 2, 16, LANES), (8, LANES)],
        far_out=(1,), copies=10, vmem=MOST_VMEM,
    )
    column = lax.all_to_all(msg, "gz", 0, 0)
    cells, cmid = run(
        spread_kernel, "spread", (column.reshape(nz * MESSAGE, LANES),), [(ny, 3, nz, LANES), (12, 4, LANES)], [],
    )
    cells = lax.all_to_all(cells, "gy", 0, 0)
    cwin = (cmid, *around(cmid, "gy", 1, 4))

    def whole(n, pad):
        return (n, ny + 2 * pad, nz, LANES)

    small = (ny // 8, nz, LANES)
    return run(
        lambda *refs: up_kernel((nz, ny), *refs), "coarse_and_up",
        (cells, *cwin, state1, state0),
        [(2, 16, 16, LANES)],
        [win2] * 4 + [win] * 12
        + [whole(12, 2), whole(2, 2), whole(2, 2), (12, *small)]
        + [whole(1, 1)[1:]] + [whole(1, 3)[1:]] * 2 + [small, (3, nz, LANES)]
        + [win2] * 3 + [(2, 12, 24, LANES), win, win, win, win, win, (2, 16, 16, LANES)],
        far_in=(4, 5), far_out=(0,), copies=20, vmem=MOST_VMEM,
    )[0]


def solution(mesh):
    in_specs = (P(None, "gz", "gy", None), P("gz", "gy", None), P())
    out_specs = P(None, "gz", "gy", None)
    return jax.shard_map(body, mesh=mesh, in_specs=in_specs, out_specs=out_specs, check_vma=False)
```

```python
import jax
import jax.numpy as jnp
from jax import lax
from jax.experimental import pallas as pl
from jax.experimental.pallas import tpu as pltpu
from jax.sharding import PartitionSpec as P

PHASES = 4
COARSE_SWEEPS = 8
LANES = 128
relax = 0.7
keep = 1.0 - relax
mass_scale = 0.01
F32 = jnp.float32
MESSAGE = 24
MOST_VMEM = 51 * 1024 * 1024


def lanes(rows):
    return lax.broadcasted_iota(jnp.int32, (rows, LANES), 1)


def row_ids(rows):
    return lax.broadcasted_iota(jnp.int32, (rows, LANES), 0)


def ahead_x(q, k):
    return pltpu.roll(q, (-k) % LANES, 1)


def ahead_y(q, k):
    return pltpu.roll(q, (-k) % q.shape[0], 0)


def pair_x(q, k):
    return q + swap_x(q, k)


def swap_x(q, k):
    return jnp.where((lanes(q.shape[0]) & k) == 0, ahead_x(q, k), ahead_x(q, -k))


def interleave(re, im):
    return jnp.where((lanes(re.shape[0]) & 1) == 0, re, im)


def separate(q):
    even = (lanes(q.shape[0]) & 1) == 0
    return jnp.where(even, q, ahead_x(q, -1)), jnp.where(even, ahead_x(q, 1), q)


def each(lo, hi, body, step=4):
    full = (hi - lo) // step

    def run(i, carry):
        for j in range(step):
            body(lo + i * step + j)
        return carry

    lax.fori_loop(0, full, run, 0)
    for z in range(lo + full * step, hi):
        body(z)


def sent(copies):
    for copy in copies:
        copy.start()
    return copies


def landed(copies):
    for copy in copies:
        copy.wait()


def times(t, q):
    return t[0] * q[0] - t[1] * q[1], t[0] * q[1] + t[1] * q[0]


def pair(ref, z):
    return ref[0, z], ref[1, z]


def put(ref, z, q):
    ref[0, z] = q[0]
    ref[1, z] = q[1]


def add(*terms):
    return sum(t[0] for t in terms[1:]) + terms[0][0], sum(t[1] for t in terms[1:]) + terms[0][1]


def both(fn, q, k):
    return fn(q[0], k), fn(q[1], k)


def inside(rows, wrap, z, first_z, first_y, size_z, size_y, dead=()):
    r = row_ids(rows)
    y = jnp.where(r >= wrap, r - rows, r) + first_y
    ok = (y >= 0) & (y < size_y)
    plane = jnp.full((rows, LANES), first_z + z, jnp.int32)
    ok = ok & (plane >= 0) & (plane < size_z)
    if dead:
        ok = ok & ((r < dead[0]) | (r >= dead[1]))
    return ok


def make_faces(z, shift, ok, s, m, tz, ty, tx, w, g=None):
    lane = lanes(s.shape[2])
    last = lane >= LANES - shift
    initial = lane < shift
    diag = []
    for c in (0, 1):
        here = s[c, z]
        up = 0.5 * (here + s[c, z + 1])
        down = 0.5 * (here + s[c, z - 1])
        side = 0.5 * (here + ahead_y(here, 1))
        right = 0.5 * (here + jnp.where(last, 0.0, ahead_x(here, shift)))
        left = 0.5 * (here + jnp.where(initial, 0.0, ahead_x(here, -shift)))
        tz[c, z] = up
        ty[c, z] = side
        tx[c, z] = jnp.where(last, 0.0, right)
        diag.append(m[c, z] + (up + down) + (side + ahead_y(side, -1)) + (right + left))
    inv = jnp.where(ok, relax / (diag[0] * diag[0] + diag[1] * diag[1]), 0.0)
    q = (diag[0] * inv, -(diag[1] * inv))
    put(w, z, q)
    if g is not None:
        put(g, z, diag)
    return q


def inflow(z, shift, v, tz, ty, tx):
    here = pair(v, z)
    side, right = pair(ty, z), pair(tx, z)
    return add(
        times(pair(tz, z), pair(v, z + 1)),
        times(pair(tz, z - 1), pair(v, z - 1)),
        times(side, both(ahead_y, here, 1)),
        both(ahead_y, times(side, here), -1),
        times(right, both(ahead_x, here, shift)),
        both(ahead_x, times(right, here), -shift),
    )


def swept(z, shift, v, f, tz, ty, tx, w):
    here = pair(v, z)
    step = times(pair(w, z), add(pair(f, z), inflow(z, shift, v, tz, ty, tx)))
    return keep * here[0] + step[0], keep * here[1] + step[1]


def residual(z, shift, v, f, tz, ty, tx, g):
    out = times(pair(g, z), pair(v, z))
    gain = add(pair(f, z), inflow(z, shift, v, tz, ty, tx))
    return gain[0] - out[0], gain[1] - out[1]


def rows_paired(buf, at, start, count):
    plane = buf.at[at]
    return plane[pl.ds(start, count, stride=2), :] + plane[pl.ds(start + 1, count, stride=2), :]


def packed_row(stack):
    lane, row = lanes(8), row_ids(8)
    cells = jnp.take_along_axis(stack, 8 * (lane % 16), axis=1)
    return jnp.sum(jnp.where(lane // 16 == row, cells, 0.0), axis=0, keepdims=True)


def lookup(lab, val):
    return [
        jnp.where(lab == 0, val[0][c], jnp.where(lab == 1, val[1][c], jnp.where(lab == 2, val[2][c], val[3][c])))
        for c in range(4)
    ]


def coeff_kernel(base, table, near_out, far_out, values_out, buf, c1, c2, stack):
    val = [[table[p, c] * F32(1.0 if c < 2 else mass_scale) for c in range(4)] for p in range(PHASES)]
    for p in range(PHASES):
        for c in range(4):
            values_out[p, c] = jnp.full((8, LANES), val[p][c], F32)
    for z in range(8):
        a, b = lookup(base[2, 2 * z], val), lookup(base[2, 2 * z + 1], val)
        for c in range(4):
            buf[c, z] = a[c] + b[c]
    for z in range(8):
        for c in range(4):
            c1[c, z] = pair_x(rows_paired(buf, (c, z), 0, 8), 1) * (0.125 if c < 2 else 0.5)
    for z in range(8):
        near_out[0, z] = interleave(c1[0, z], c1[1, z])
        near_out[1, z] = interleave(c1[2, z], c1[3, z])
    for c in range(4):
        scale = 0.125 if c < 2 else 0.5
        for z in range(4):
            buf[c, z, 0:8] = c1[c, 2 * z] + c1[c, 2 * z + 1]
        for z in range(4):
            c2[c, z] = pair_x(rows_paired(buf, (c, z), 0, 4), 2) * scale
        for z in range(2):
            buf[c, 4 + z, 0:4] = c2[c, 2 * z] + c2[c, 2 * z + 1]
        for z in range(2):
            stack[c // 2, (c % 2) * 4 + 2 * z : (c % 2) * 4 + 2 * z + 2] = (
                pair_x(rows_paired(buf, (c, 4 + z), 0, 2), 4) * scale
            )
    far_out[:, 0:LANES] = packed_row(stack[0])
    far_out[:, LANES : 2 * LANES] = packed_row(stack[1])


KEPT0 = slice(2, 22)
KEPT1 = slice(5, 19)


def fine_kernel(
    sizes, base, zb, za, left, right, values, near_c, msg_out, *rest
):
    keeps, v, f, tz, ty, tx, w, lab, s, m, g, first, buf, sem = rest
    first_z = lax.axis_index("gz") * 16 - 4
    first_y = lax.axis_index("gy") * 16

    def load(z, own, k):
        for c, dst in enumerate((f.at[0, z], f.at[1, z], lab.at[z])):
            dst[0:16] = own[c, k]
            dst[16:20] = right[c, z]
            dst[20:24] = left[c, z]
        ok = inside(24, 20, z, first_z, first_y, *sizes)
        val = [[values[p, c] for c in range(4)] for p in range(PHASES)]
        for r in (slice(0, 8), slice(8, 16), slice(16, 24)):
            got = lookup(lab[z, r], val)
            for c in (0, 1):
                s[c, z, r] = jnp.where(ok[r], got[c], 0.0)
                m[c, z, r] = got[2 + c]

    for z in range(4):
        load(z, zb, z)
        load(z + 20, za, z)
    each(0, 16, lambda z: load(z + 4, base, z))

    def faces(z):
        ok = inside(24, 20, z, first_z, first_y, *sizes)
        put(first, z, times(make_faces(z, 1, ok, s, m, tz, ty, tx, w, g), pair(f, z)))

    each(1, 23, faces)

    def kept(i, ref):
        return pltpu.make_async_copy(ref.at[:, KEPT0], keeps.at[i], sem.at[i])

    copies = sent([kept(i, ref) for i, ref in enumerate((v, f, tz, ty, tx, w)) if i])
    each(2, 22, lambda z: put(v, z, swept(z, 1, first, f, tz, ty, tx, w)))
    copies += sent([kept(0, v)])

    def restrict(z):
        a = residual(2 * z + 4, 1, v, f, tz, ty, tx, g)
        b = residual(2 * z + 5, 1, v, f, tz, ty, tx, g)
        put(buf, z, add(a, b))

    each(0, 8, restrict, 4)

    def finish(z):
        re, im = (0.5 * pair_x(rows_paired(buf, (c, z), 0, 8), 1) for c in (0, 1))
        msg_out[2, z] = interleave(re, im)
        msg_out[0, z] = near_c[0, z]
        msg_out[1, z] = near_c[1, z]

    each(0, 8, finish)
    landed(copies)


def middle_kernel(
    sizes, mid, left, right, far_c,
    msg_out, *rest
):
    keeps, rest = rest[0], rest[1:]
    v, f, tz, ty, tx, w, tz2, ty2, tx2, w2, s, m, g, first, buf, s2, m2, f2, g2, first2, v2, buf2, stack, sem = rest
    gz, gy = lax.axis_index("gz"), lax.axis_index("gy")

    def load(z):
        for lo, src in ((0, mid), (8, right), (16, left)):
            for i, ref in enumerate((s, m, f)):
                re, im = separate(src[i, z])
                ref[0, z, lo : lo + 8] = re
                ref[1, z, lo : lo + 8] = im

    each(0, 24, load)

    def faces(z):
        ok = inside(24, 16, z, gz * 8 - 8, gy * 8, *sizes[0])
        put(first, z, times(make_faces(z, 2, ok, s, m, tz, ty, tx, w, g), pair(f, z)))

    each(1, 23, faces)

    def kept(i, ref):
        return pltpu.make_async_copy(ref.at[:, KEPT1], keeps.at[i], sem.at[i])

    copies = sent([kept(i, ref) for i, ref in enumerate((v, f, tz, ty, tx, w)) if i])
    each(2, 22, lambda z: put(v, z, swept(z, 2, first, f, tz, ty, tx, w)))
    copies += sent([kept(0, v)])

    def coarser(dst, scale, z):
        for c in (0, 1):
            dst[c, z, 0:8] = scale * pair_x(rows_paired(buf, (c, z), 0, 8), 2)
            dst[c, z, 8:12] = jnp.zeros((4, LANES), F32)
            dst[c, z, 12:16] = scale * pair_x(rows_paired(buf, (c, z), 16, 4), 2)

    for src, dst, scale in ((s, s2, 0.125), (m, m2, 0.5)):
        each(0, 12, lambda z: put(buf, z, add(pair(src, 2 * z), pair(src, 2 * z + 1))))
        each(0, 12, lambda z: coarser(dst, scale, z))

    def restrict(z):
        put(buf, z, add(residual(2 * z, 2, v, f, tz, ty, tx, g), residual(2 * z + 1, 2, v, f, tz, ty, tx, g)))

    each(2, 10, restrict, 4)
    each(2, 10, lambda z: coarser(f2, 0.5, z))

    def faces2(z):
        ok = inside(16, 12, z, gz * 4 - 4, gy * 4, *sizes[1], dead=(8, 12))
        return make_faces(z, 4, ok, s2, m2, tz2, ty2, tx2, w2, g2)

    faces2(1)
    tz2[0, 0] = 0.5 * (s2[0, 0] + s2[0, 1])
    tz2[1, 0] = 0.5 * (s2[1, 0] + s2[1, 1])
    each(2, 10, lambda z: put(first2, z, times(faces2(z), pair(f2, z))))
    faces2(10)
    copies += sent([pltpu.make_async_copy(ref, keeps.at[6 + i, :, 0:12, 0:16], sem.at[6 + i]) for i, ref in enumerate((tz2, ty2, tx2, w2))])
    each(3, 9, lambda z: put(v2, z, swept(z, 4, first2, f2, tz2, ty2, tx2, w2)))
    which = lanes(4) & 3
    for z in range(4):
        a, b = pair(v2, z + 4), pair(f2, z + 4)
        msg_out[0, 8 + 4 * z : 12 + 4 * z] = jnp.where(
            which < 2, jnp.where(which == 0, a[0][0:4], a[1][0:4]), jnp.where(which == 2, b[0][0:4], b[1][0:4])
        )
    for z in range(2):
        a = residual(2 * z + 4, 4, v2, f2, tz2, ty2, tx2, g2)
        b = residual(2 * z + 5, 4, v2, f2, tz2, ty2, tx2, g2)
        put(buf2, z, add(a, b))
    for z in range(2):
        for c in (0, 1):
            stack[4 * c + 2 * z : 4 * c + 2 * z + 2] = 0.5 * pair_x(rows_paired(buf2, (c, z), 0, 2), 4)
    msg_out[0, 0:1] = packed_row(stack[...])
    msg_out[0, 1:2] = far_c[:, 0:LANES]
    msg_out[0, 2:3] = far_c[:, LANES : 2 * LANES]
    msg_out[0, 3:8] = jnp.zeros((5, LANES), F32)
    message = msg_out[0]
    for g in range(1, msg_out.shape[0]):
        msg_out[g] = message
    landed(copies)


def spread_kernel(column, cells, near):
    ny, _, nz, _ = cells.shape
    for k in range(3):
        q = column[pl.ds(k, nz, stride=MESSAGE), :]
        for p in range(ny):
            cells[p, k] = q
    mine = lax.axis_index("gz")
    for d in (-1, 0, 1):
        p = jnp.clip(mine + d, 0, nz - 1)
        on = jnp.where((mine + d >= 0) & (mine + d < nz), 1.0, 0.0)
        q = on * column[pl.ds(pl.multiple_of(p * MESSAGE + 8, 8), 16), :]
        for z in range(4):
            near[4 * d + 4 + z] = q[4 * z : 4 * z + 4]


def real_lanes(rows):
    return lanes(rows) < 64


def flip(q):
    return pltpu.roll(q, 64, 1)


def as_factors(q):
    real, other = real_lanes(q.shape[0]), flip(q)
    return jnp.where(real, q, other), jnp.where(real, other, -q)


def product(t, q):
    return t[0] * q + flip(t[1] * q)


def inverse_factors(diag):
    real, other = real_lanes(diag.shape[0]), flip(diag)
    inv = relax / (diag * diag + other * other)
    return jnp.where(real, diag, other) * inv, jnp.where(real, -other, diag) * inv


def shifted_rows(q, k):
    edge = q.shape[0] - 1 if k > 0 else 0
    return jnp.where(row_ids(q.shape[0]) == edge, 0.0, ahead_y(q, k))


def near_level3(planes):
    n = planes[0].shape[0]
    lane = lanes(n)
    low_z, low_y, x = (lane & 32) == 0, (lane & 16) == 0, lane & 15
    turned = [swap_x(q, 16) for q in planes]
    out = []
    for i, q in enumerate(planes[1:-1]):
        qz = swap_x(q, 32)
        out.append(
            (
                jnp.where(low_y, turned[i + 1], turned[i + 2]),
                jnp.where(low_y, turned[i], turned[i + 1]),
                jnp.where(low_z, qz, shifted_rows(qz, 1)),
                jnp.where(low_z, shifted_rows(qz, -1), qz),
                jnp.where(x == 15, 0.0, ahead_x(q, 1)),
                jnp.where(x == 0, 0.0, ahead_x(q, -1)),
            )
        )
    return out


def slot_lanes(lane, slot):
    return (lane & 78) | ((slot & 4) << 3) | ((slot & 2) << 3) | (slot & 1)


def slot_of(lane):
    return ((lane >> 3) & 4) | ((lane >> 3) & 2) | (lane & 1)


def near_level4(groups):
    n = groups[0].shape[0]
    lane = lanes(n)
    slot, x = slot_of(lane), lane & 14
    nxt, prv = slot_lanes(lane, slot + 1), slot_lanes(lane, slot + 7)
    zero = jnp.zeros_like(groups[0])
    up = [jnp.take_along_axis(q, nxt, axis=1) for q in groups] + [zero]
    down = [zero] + [jnp.take_along_axis(q, prv, axis=1) for q in groups]
    return [
        (
            jnp.where(slot == 7, up[i + 1], up[i]),
            jnp.where(slot == 0, down[i], down[i + 1]),
            shifted_rows(q, 1),
            shifted_rows(q, -1),
            jnp.where(x == 14, 0.0, ahead_x(q, 2)),
            jnp.where(x == 0, 0.0, ahead_x(q, -2)),
        )
        for i, q in enumerate(groups)
    ]


def set_level(here, near, m, t, w, g, p):
    diag = m
    for i, other in enumerate(near):
        face = 0.5 * (here + other)
        diag = diag + face
        t[2 * i, p], t[2 * i + 1, p] = as_factors(face)
    w[0, p], w[1, p] = inverse_factors(diag)
    if g is not None:
        g[0, p], g[1, p] = as_factors(diag)


def gathered_inflow(near, t, p):
    a = sum(t[2 * i, p] * q for i, q in enumerate(near[1:], 1)) + t[0, p] * near[0]
    b = sum(t[2 * i + 1, p] * q for i, q in enumerate(near[1:], 1)) + t[1, p] * near[0]
    return a + flip(b)


def factors(ref, p):
    return ref[0, p], ref[1, p]


def folded(planes):
    lane = lanes(planes[0].shape[0])
    for bit in (1, 16, 32):
        low = (lane & bit) == 0
        planes = [
            jnp.where(low, a, b) + swap_x(jnp.where(low, b, a), bit) for a, b in zip(planes[0::2], planes[1::2])
        ]
    return planes[0]


BATCH = 8


def batches(n, body):
    def run(i, carry):
        body(pl.multiple_of(i * BATCH, BATCH))
        return carry

    lax.fori_loop(0, n // BATCH, run, 0)


def level4(f4, s4, m4, t4):
    real = real_lanes(s4[0].shape[0])
    start = []
    for k, near in enumerate(near_level4(s4)):
        faces = [0.5 * (s4[k] + other) for other in near]
        fa = inverse_factors(sum(faces[1:]) + faces[0] + m4[k])
        start.append(product(fa, f4[k]))
        for i, face in enumerate(faces):
            q = product(fa, face)
            other = flip(q)
            t4[2 * i, k] = jnp.where(real, q, other)
            t4[2 * i + 1, k] = jnp.where(real, -other, q)
    turned = [flip(q) for q in start]
    e, o = start, turned
    for sweep in range(COARSE_SWEEPS - 1):
        pairs = list(zip(near_level4(e), near_level4(o)))
        e_next, o_next = [], []
        for k, (ne, no) in enumerate(pairs):
            ab = [(t4[2 * i, k], t4[2 * i + 1, k]) for i in range(6)]
            x = [a * p + b * q for (a, b), p, q in zip(ab, ne, no)]
            y = [a * q - b * p for (a, b), p, q in zip(ab, ne, no)]
            e_next.append((keep * e[k] + start[k] + x[0]) + (x[1] + x[2]) + (x[3] + x[4]) + x[5])
            o_next.append((keep * o[k] + turned[k] + y[0]) + (y[1] + y[2]) + (y[3] + y[4]) + y[5])
        e, o = e_next, o_next
    return e


def coarse_solve(counts, cells, t3, w3, g3, t4, s3, va, vb, ea):
    nz, ny = counts
    groups = ny // 8
    zero = jnp.zeros((nz, LANES), F32)
    s3[0] = zero
    s3[ny + 1] = zero
    for ref in (va, vb):
        for p in (0, 1, 2, ny + 3, ny + 4, ny + 5):
            ref[p] = zero
    for p in (0, 1, ny + 2, ny + 3):
        for i in range(12):
            t3[i, p] = zero
        w3[0, p] = zero
        w3[1, p] = zero

    def load(p0):
        for i in range(BATCH):
            s3[p0 + i + 1] = cells[p0 + i, 1]

    batches(ny, load)

    def setup(p0):
        planes = [s3[p0 + i] for i in range(BATCH + 2)]
        for i, near in enumerate(near_level3(planes)):
            p = p0 + i
            set_level(planes[i + 1], near, cells[p, 2], t3, w3, g3, p + 2)
            va[p + 3] = product(factors(w3, p + 2), cells[p, 0])

    batches(ny, setup)
    s4 = [0.125 * folded([cells[8 * k + j, 1] for j in range(8)]) for k in range(groups)]
    m4 = [0.5 * folded([cells[8 * k + j, 2] for j in range(8)]) for k in range(groups)]

    def swept3(here, near, p):
        gain = cells[jnp.clip(p, 0, ny - 1), 0] + gathered_inflow(near, t3, p + 2)
        return keep * here + product(factors(w3, p + 2), gain)

    def pre(p0):
        planes = [va[p0 + i + 2] for i in range(BATCH + 2)]
        for i, near in enumerate(near_level3(planes)):
            p = p0 + i
            gain = cells[p, 0] + gathered_inflow(near, t3, p + 2)
            vb[p + 3] = keep * planes[i + 1] + product(factors(w3, p + 2), gain)

    batches(ny, pre)

    def restrict(p0):
        planes = [vb[p0 + i + 2] for i in range(BATCH + 2)]
        gains = []
        for i, near in enumerate(near_level3(planes)):
            p = p0 + i
            gain = cells[p, 0] + gathered_inflow(near, t3, p + 2)
            gains.append(gain - product(factors(g3, p + 2), planes[i + 1]))
        ea[p0 // BATCH] = 0.5 * folded(gains)

    batches(ny, restrict)
    for k, q in enumerate(level4([ea[k] for k in range(groups)], s4, m4, t4)):
        ea[k] = q

    mine = lax.axis_index("gy")
    lane = lanes(nz)
    planes = []
    for d in range(-3, 4):
        p = mine + d
        on = jnp.where((p >= 0) & (p < ny), 1.0, 0.0)
        q = jnp.clip(p, 0, ny - 1)
        corr = jnp.take_along_axis(ea[q // 8], slot_lanes(lane, jnp.full((nz, LANES), q % 8, jnp.int32)), axis=1)
        planes.append(vb[p + 3] + on * corr)
    for reach in (2, 1):
        planes = [
            swept3(here, near, mine + d)
            for d, here, near in zip(range(-reach, reach + 1), planes[1:-1], near_level3(planes))
        ]
    return planes


def up_kernel(counts, cells, cmid, cleft, cright, *rest):
    kept1, kept0, out, rest = rest[0], rest[1], rest[2], rest[3:]
    tz2, ty2, tx2, w2, v1, f1, tz1, ty1, tx1, w1, v0, f0, tz0, ty0, tx0, w0 = rest[:16]
    t3, w3, g3, t4, s3, va, vb, ea, near, a2, b2, f2, e1, a1, b1, e0, a0, b0, done, sem = rest[16:]
    copies = []
    for i, dst in enumerate(rest[:16]):
        src, dst = (
            (kept1.at[6 + i, :, 0:12, 0:16], dst) if i < 4
            else (kept1.at[i - 4], dst.at[:, KEPT1]) if i < 10
            else (kept0.at[i - 10], dst.at[:, KEPT0])
        )
        copies.append(pltpu.make_async_copy(src, dst, sem.at[i]))
    sent(copies)
    nz = counts[0]
    gz = lax.axis_index("gz")
    for d, q in enumerate(coarse_solve(counts, cells, t3, w3, g3, t4, s3, va, vb, ea)):
        near[d] = q

    lane4, zero4 = lanes(4), jnp.zeros((4, LANES), F32)

    def unpack(z):
        for ref in (a2, f2):
            for c in (0, 1):
                ref[c, z, 8:12] = zero4
        for lo, src in ((0, cmid), (4, cright), (12, cleft)):
            q = src[z]
            turned = {k: ahead_x(q, k) if k else q for k in range(-3, 4)}
            for k, (ref, c) in enumerate(((a2, 0), (a2, 1), (f2, 0), (f2, 1))):
                val = turned[k]
                for i in range(1, 4):
                    val = jnp.where((lane4 & 3) == i, turned[k - i], val)
                ref[c, z, lo : lo + 4] = val

    each(0, 12, unpack)
    r16, l16 = row_ids(16), lanes(16)
    cell = l16 // 8
    for dz in (-1, 0, 1):
        row = jnp.clip(gz + dz, 0, nz - 1)
        on = jnp.where((gz + dz >= 0) & (gz + dz < nz), 1.0, 0.0)
        before, own, after = (near[d, pl.ds(row, 1), :] * on for d in range(3))
        rows = jnp.where(r16 < 4, own, jnp.where(r16 < 8, after, jnp.where(r16 < 12, 0.0, before)))
        for c in (0, 1):
            for zz in (0, 1):
                corr = jnp.take_along_axis(rows, cell + 16 * ((r16 // 2) & 1) + (64 * c + 32 * zz), axis=1)
                for z in (4 * dz + 4 + 2 * zz, 4 * dz + 5 + 2 * zz):
                    a2[c, z] = a2[c, z] + corr

    landed(copies)
    each(1, 11, lambda z: put(b2, z, swept(z, 4, a2, f2, tz2, ty2, tx2, w2)))
    each(2, 10, lambda z: put(a2, z, swept(z, 4, b2, f2, tz2, ty2, tx2, w2)))

    def widen1(z):
        for c in (0, 1):
            q = a2[c, z]
            for k in (0, 1):
                e1.at[c, z][pl.ds(k, 8, stride=2), :] = q[0:8]
                e1.at[c, z][pl.ds(16 + k, 4, stride=2), :] = q[12:16]

    each(2, 10, widen1)
    def correct1(z):
        e = pair(e1, z)
        for k in (2 * z, 2 * z + 1):
            put(a1, k, add(pair(v1, k), e))

    each(3, 9, correct1)
    for k, z in ((5, 2), (18, 9)):
        put(a1, k, add(pair(v1, k), pair(e1, z)))
    each(6, 18, lambda z: put(b1, z, swept(z, 2, a1, f1, tz1, ty1, tx1, w1)))
    each(7, 17, lambda z: put(a1, z, swept(z, 2, b1, f1, tz1, ty1, tx1, w1)))

    def widen0(z):
        for c in (0, 1):
            q = a1[c, z]
            for k in (0, 1):
                e0.at[c, z][pl.ds(k, 8, stride=2), :] = q[0:8]
                e0.at[c, z][pl.ds(16 + k, 2, stride=2), :] = q[8:10]
                e0.at[c, z][pl.ds(20 + k, 2, stride=2), :] = q[22:24]

    each(7, 17, widen0)
    def correct0(z):
        e = pair(e0, z)
        for k in (2 * z - 12, 2 * z - 11):
            put(a0, k, add(pair(v0, k), e))

    each(7, 17, correct0)
    each(3, 21, lambda z: put(b0, z, swept(z, 1, a0, f0, tz0, ty0, tx0, w0)))

    def last(z):
        q = swept(z, 1, b0, f0, tz0, ty0, tx0, w0)
        done[0, z - 4] = q[0][0:16]
        done[1, z - 4] = q[1][0:16]

    copies = []
    for i in range(4):
        part = slice(4 * i, 4 * i + 4)
        for z in range(4):
            last(4 * i + z + 4)
        copies += sent([pltpu.make_async_copy(done.at[:, part], out.at[:, part], sem.at[16 + i])])
    landed(copies)


def run(kernel, name, args, outs, scratch, smem=(), far_in=(), far_out=(), copies=0, vmem=32 * 1024 * 1024):
    def specs(n, smem, far):
        spaces = [pltpu.SMEM if i in smem else pltpu.HBM if i in far else pltpu.VMEM for i in range(n)]
        return [pl.BlockSpec(memory_space=space) for space in spaces]

    return pl.pallas_call(
        kernel,
        name=name,
        out_shape=[jax.ShapeDtypeStruct(s, F32) for s in outs],
        in_specs=specs(len(args), smem, far_in),
        out_specs=specs(len(outs), (), far_out),
        scratch_shapes=[pltpu.VMEM(s, F32) if isinstance(s, tuple) else s for s in scratch]
        + ([pltpu.SemaphoreType.DMA((copies,))] if copies else []),
        compiler_params=pltpu.CompilerParams(vmem_limit_bytes=vmem),
    )(*args)


def traded(axis, top, bottom):
    n = lax.axis_size(axis)
    even = lax.axis_index(axis) % 2 == 0
    far = [(i, j) for k in range(2, n, 2) for i, j in ((k - 1, k), (k, k - 1))]
    close = [(i, i ^ 1) for i in range(n) if i ^ 1 < n]
    same = top is bottom
    to_far = top if same else jnp.where(even, bottom, top)
    to_close = top if same else jnp.where(even, top, bottom)
    from_far = lax.ppermute(to_far, axis, far)
    from_close = lax.ppermute(to_close, axis, close)
    return jnp.where(even, from_far, from_close), jnp.where(even, from_close, from_far)


def around(block, axis, dim, width):
    size = block.shape[dim]
    if width == size:
        return traded(axis, block, block)
    return traded(
        axis,
        lax.slice_in_dim(block, size - width, size, axis=dim),
        lax.slice_in_dim(block, 0, width, axis=dim),
    )


def window(block, dim, width):
    before, after = around(block, "gz", dim, width)
    mid = jnp.concatenate([before, block, after], axis=dim)
    left, right = around(mid, "gy", dim + 1, width)
    return mid, left, right


def body(source, labels, phase_table):
    nz, ny = lax.axis_size("gz"), lax.axis_size("gy")

    base = lax.optimization_barrier(jnp.concatenate([source, labels.astype(F32)[None]], axis=0))
    zb, za = around(base, "gz", 1, 4)
    left, right = around(jnp.concatenate([zb, base, za], axis=1), "gy", 2, 4)

    near_c, far_c, values = run(
        coeff_kernel, "coefficients", (base, phase_table),
        [(2, 8, 8, LANES), (1, 2 * LANES), (PHASES, 4, 8, LANES)],
        [(4, 8, 16, LANES), (4, 8, 8, LANES), (4, 4, 4, LANES), (2, 8, LANES)], smem=(1,),
    )
    win, win2 = (2, 24, 24, LANES), (2, 12, 16, LANES)
    win0 = (2, KEPT0.stop - KEPT0.start, 24, LANES)
    win1 = (2, KEPT1.stop - KEPT1.start, 24, LANES)
    msg, state0 = run(
        lambda *refs: fine_kernel((16 * nz, 16 * ny), *refs), "fine_down",
        (base, zb, za, left, right, values, near_c),
        [(3, 8, 8, LANES), (20, *win0)],
        [win] * 6 + [(24, 24, LANES)] + [win] * 4 + [(2, 8, 24, LANES)],
        far_out=(1,), copies=6, vmem=MOST_VMEM,
    )
    msg, state1 = run(
        lambda *refs: middle_kernel(((8 * nz, 8 * ny), (4 * nz, 4 * ny)), *refs), "middle_down",
        (*window(msg, 1, 8), far_c),
        [(nz, MESSAGE, LANES), (32, *win1)],
        [win] * 6 + [win2] * 4 + [win] * 4 + [(2, 12, 24, LANES)] + [win2] * 6 + [(2, 2, 16, LANES), (8, LANES)],
        far_out=(1,), copies=10, vmem=MOST_VMEM,
    )
    column = lax.all_to_all(msg, "gz", 0, 0)
    cells, cmid = run(
        spread_kernel, "spread", (column.reshape(nz * MESSAGE, LANES),), [(ny, 3, nz, LANES), (12, 4, LANES)], [],
    )
    cells = lax.all_to_all(cells, "gy", 0, 0)
    cwin = (cmid, *around(cmid, "gy", 1, 4))

    def whole(n, pad):
        return (n, ny + 2 * pad, nz, LANES)

    small = (ny // 8, nz, LANES)
    return run(
        lambda *refs: up_kernel((nz, ny), *refs), "coarse_and_up",
        (cells, *cwin, state1, state0),
        [(2, 16, 16, LANES)],
        [win2] * 4 + [win] * 12
        + [whole(12, 2), whole(2, 2), whole(2, 2), (12, *small)]
        + [whole(1, 1)[1:]] + [whole(1, 3)[1:]] * 2 + [small, (3, nz, LANES)]
        + [win2] * 3 + [(2, 12, 24, LANES), win, win, win, win, win, (2, 16, 16, LANES)],
        far_in=(4, 5), far_out=(0,), copies=20, vmem=MOST_VMEM,
    )[0]


def solution(mesh):
    in_specs = (P(None, "gz", "gy", None), P("gz", "gy", None), P())
    out_specs = P(None, "gz", "gy", None)
    return jax.shard_map(body, mesh=mesh, in_specs=in_specs, out_specs=out_specs, check_vma=False)
```

```python
import jax
import jax.numpy as jnp
from jax import lax
from jax.experimental import pallas as pl
from jax.experimental.pallas import tpu as pltpu
from jax.sharding import PartitionSpec as P

PHASES = 4
COARSE_SWEEPS = 8
LANES = 128
relax = 0.7
keep = 1.0 - relax
mass_scale = 0.01
F32 = jnp.float32
MESSAGE = (5, 4, LANES)
MOST_VMEM = 51 * 1024 * 1024


def lanes(rows):
    return lax.broadcasted_iota(jnp.int32, (rows, LANES), 1)


def row_ids(rows):
    return lax.broadcasted_iota(jnp.int32, (rows, LANES), 0)


def ahead_x(q, k):
    return pltpu.roll(q, (-k) % LANES, 1)


def ahead_y(q, k):
    return pltpu.roll(q, (-k) % q.shape[0], 0)


def pair_x(q, k):
    return q + swap_x(q, k)


def swap_x(q, k):
    return jnp.where((lanes(q.shape[0]) & k) == 0, ahead_x(q, k), ahead_x(q, -k))


def interleave(re, im):
    return jnp.where((lanes(re.shape[0]) & 1) == 0, re, im)


def separate(q):
    even = (lanes(q.shape[0]) & 1) == 0
    return jnp.where(even, q, ahead_x(q, -1)), jnp.where(even, ahead_x(q, 1), q)


def each(lo, hi, body, step=4):
    full = (hi - lo) // step

    def run(i, carry):
        for j in range(step):
            body(lo + i * step + j)
        return carry

    lax.fori_loop(0, full, run, 0)
    for z in range(lo + full * step, hi):
        body(z)


def sent(copies):
    for copy in copies:
        copy.start()
    return copies


def landed(copies):
    for copy in copies:
        copy.wait()


def times(t, q):
    return t[0] * q[0] - t[1] * q[1], t[0] * q[1] + t[1] * q[0]


def pair(ref, z):
    return ref[0, z], ref[1, z]


def put(ref, z, q):
    ref[0, z] = q[0]
    ref[1, z] = q[1]


def add(*terms):
    return sum(t[0] for t in terms[1:]) + terms[0][0], sum(t[1] for t in terms[1:]) + terms[0][1]


def both(fn, q, k):
    return fn(q[0], k), fn(q[1], k)


def inside(rows, wrap, z, first_z, first_y, size_z, size_y, dead=()):
    r = row_ids(rows)
    y = jnp.where(r >= wrap, r - rows, r) + first_y
    ok = (y >= 0) & (y < size_y)
    plane = jnp.full((rows, LANES), first_z + z, jnp.int32)
    ok = ok & (plane >= 0) & (plane < size_z)
    if dead:
        ok = ok & ((r < dead[0]) | (r >= dead[1]))
    return ok


def make_faces(z, shift, ok, s, m, tz, ty, tx, w, g=None):
    lane = lanes(s.shape[2])
    last = lane >= LANES - shift
    initial = lane < shift
    diag = []
    for c in (0, 1):
        here = s[c, z]
        up = 0.5 * (here + s[c, z + 1])
        down = 0.5 * (here + s[c, z - 1])
        side = 0.5 * (here + ahead_y(here, 1))
        right = 0.5 * (here + jnp.where(last, 0.0, ahead_x(here, shift)))
        left = 0.5 * (here + jnp.where(initial, 0.0, ahead_x(here, -shift)))
        tz[c, z] = up
        ty[c, z] = side
        tx[c, z] = jnp.where(last, 0.0, right)
        diag.append(m[c, z] + (up + down) + (side + ahead_y(side, -1)) + (right + left))
    inv = jnp.where(ok, relax / (diag[0] * diag[0] + diag[1] * diag[1]), 0.0)
    q = (diag[0] * inv, -(diag[1] * inv))
    put(w, z, q)
    if g is not None:
        put(g, z, diag)
    return q


def inflow(z, shift, v, tz, ty, tx):
    here = pair(v, z)
    side, right = pair(ty, z), pair(tx, z)
    return add(
        times(pair(tz, z), pair(v, z + 1)),
        times(pair(tz, z - 1), pair(v, z - 1)),
        times(side, both(ahead_y, here, 1)),
        both(ahead_y, times(side, here), -1),
        times(right, both(ahead_x, here, shift)),
        both(ahead_x, times(right, here), -shift),
    )


def swept(z, shift, v, f, tz, ty, tx, w):
    here = pair(v, z)
    step = times(pair(w, z), add(pair(f, z), inflow(z, shift, v, tz, ty, tx)))
    return keep * here[0] + step[0], keep * here[1] + step[1]


def residual(z, shift, v, f, tz, ty, tx, g):
    out = times(pair(g, z), pair(v, z))
    gain = add(pair(f, z), inflow(z, shift, v, tz, ty, tx))
    return gain[0] - out[0], gain[1] - out[1]


def rows_paired(buf, at, start, count):
    plane = buf.at[at]
    return plane[pl.ds(start, count, stride=2), :] + plane[pl.ds(start + 1, count, stride=2), :]


def packed_row(stack):
    lane, row = lanes(8), row_ids(8)
    cells = jnp.take_along_axis(stack, 8 * (lane % 16), axis=1)
    return jnp.sum(jnp.where(lane // 16 == row, cells, 0.0), axis=0, keepdims=True)


def lookup(lab, val):
    return [
        jnp.where(lab == 0, val[0][c], jnp.where(lab == 1, val[1][c], jnp.where(lab == 2, val[2][c], val[3][c])))
        for c in range(4)
    ]


def coeff_kernel(base, table, near_out, far_out, values_out, buf, c1, c2, stack):
    val = [[table[p, c] * F32(1.0 if c < 2 else mass_scale) for c in range(4)] for p in range(PHASES)]
    for p in range(PHASES):
        for c in range(4):
            values_out[p, c] = jnp.full((8, LANES), val[p][c], F32)
    for z in range(8):
        a, b = lookup(base[2, 2 * z], val), lookup(base[2, 2 * z + 1], val)
        for c in range(4):
            buf[c, z] = a[c] + b[c]
    for z in range(8):
        for c in range(4):
            c1[c, z] = pair_x(rows_paired(buf, (c, z), 0, 8), 1) * (0.125 if c < 2 else 0.5)
    for z in range(8):
        near_out[0, z] = interleave(c1[0, z], c1[1, z])
        near_out[1, z] = interleave(c1[2, z], c1[3, z])
    for c in range(4):
        scale = 0.125 if c < 2 else 0.5
        for z in range(4):
            buf[c, z, 0:8] = c1[c, 2 * z] + c1[c, 2 * z + 1]
        for z in range(4):
            c2[c, z] = pair_x(rows_paired(buf, (c, z), 0, 4), 2) * scale
        for z in range(2):
            buf[c, 4 + z, 0:4] = c2[c, 2 * z] + c2[c, 2 * z + 1]
        for z in range(2):
            stack[c // 2, (c % 2) * 4 + 2 * z : (c % 2) * 4 + 2 * z + 2] = (
                pair_x(rows_paired(buf, (c, 4 + z), 0, 2), 4) * scale
            )
    far_out[:, 0:LANES] = packed_row(stack[0])
    far_out[:, LANES : 2 * LANES] = packed_row(stack[1])


KEPT0 = slice(2, 22)
KEPT1 = slice(5, 19)


def fine_kernel(
    sizes, base, zb, za, left, right, values, near_c, msg_out, *rest
):
    keeps, v, f, tz, ty, tx, w, lab, s, m, g, first, buf, sem = rest
    first_z = lax.axis_index("gz") * 16 - 4
    first_y = lax.axis_index("gy") * 16

    def load(z, own, k):
        for c, dst in enumerate((f.at[0, z], f.at[1, z], lab.at[z])):
            dst[0:16] = own[c, k]
            dst[16:20] = right[c, z]
            dst[20:24] = left[c, z]
        ok = inside(24, 20, z, first_z, first_y, *sizes)
        val = [[values[p, c] for c in range(4)] for p in range(PHASES)]
        for r in (slice(0, 8), slice(8, 16), slice(16, 24)):
            got = lookup(lab[z, r], val)
            for c in (0, 1):
                s[c, z, r] = jnp.where(ok[r], got[c], 0.0)
                m[c, z, r] = got[2 + c]

    for z in range(4):
        load(z, zb, z)
        load(z + 20, za, z)
    each(0, 16, lambda z: load(z + 4, base, z))

    def faces(z):
        ok = inside(24, 20, z, first_z, first_y, *sizes)
        put(first, z, times(make_faces(z, 1, ok, s, m, tz, ty, tx, w, g), pair(f, z)))

    each(1, 23, faces)

    def kept(i, ref):
        return pltpu.make_async_copy(ref.at[:, KEPT0], keeps.at[i], sem.at[i])

    copies = sent([kept(i, ref) for i, ref in enumerate((v, f, tz, ty, tx, w)) if i])
    each(2, 22, lambda z: put(v, z, swept(z, 1, first, f, tz, ty, tx, w)))
    copies += sent([kept(0, v)])

    def restrict(z):
        a = residual(2 * z + 4, 1, v, f, tz, ty, tx, g)
        b = residual(2 * z + 5, 1, v, f, tz, ty, tx, g)
        put(buf, z, add(a, b))

    each(0, 8, restrict, 4)

    def finish(z):
        re, im = (0.5 * pair_x(rows_paired(buf, (c, z), 0, 8), 1) for c in (0, 1))
        msg_out[2, z] = interleave(re, im)
        msg_out[0, z] = near_c[0, z]
        msg_out[1, z] = near_c[1, z]

    each(0, 8, finish)
    landed(copies)


def middle_kernel(
    sizes, mid, left, right, far_c,
    msg_out, *rest
):
    keeps, rest = rest[0], rest[1:]
    v, f, tz, ty, tx, w, tz2, ty2, tx2, w2, s, m, g, first, buf, s2, m2, f2, g2, first2, v2, buf2, stack, sem = rest
    gz, gy = lax.axis_index("gz"), lax.axis_index("gy")

    def load(z):
        for lo, src in ((0, mid), (8, right), (16, left)):
            for i, ref in enumerate((s, m, f)):
                re, im = separate(src[i, z])
                ref[0, z, lo : lo + 8] = re
                ref[1, z, lo : lo + 8] = im

    each(0, 24, load)

    def faces(z):
        ok = inside(24, 16, z, gz * 8 - 8, gy * 8, *sizes[0])
        put(first, z, times(make_faces(z, 2, ok, s, m, tz, ty, tx, w, g), pair(f, z)))

    each(2, 22, faces)

    def kept(i, ref):
        return pltpu.make_async_copy(ref.at[:, KEPT1], keeps.at[i], sem.at[i])

    copies = sent([kept(i, ref) for i, ref in enumerate((v, f, tz, ty, tx, w)) if i])
    each(3, 21, lambda z: put(v, z, swept(z, 2, first, f, tz, ty, tx, w)))
    copies += sent([kept(0, v)])

    def coarser(dst, scale, z):
        for c in (0, 1):
            dst[c, z, 0:8] = scale * pair_x(rows_paired(buf, (c, z), 0, 8), 2)
            dst[c, z, 8:12] = jnp.zeros((4, LANES), F32)
            dst[c, z, 12:16] = scale * pair_x(rows_paired(buf, (c, z), 16, 4), 2)

    for src, dst, scale in ((s, s2, 0.125), (m, m2, 0.5)):
        each(0, 12, lambda z: put(buf, z, add(pair(src, 2 * z), pair(src, 2 * z + 1))))
        each(0, 12, lambda z: coarser(dst, scale, z))

    def restrict(z):
        put(buf, z, add(residual(2 * z, 2, v, f, tz, ty, tx, g), residual(2 * z + 1, 2, v, f, tz, ty, tx, g)))

    each(2, 10, restrict, 4)
    each(2, 10, lambda z: coarser(f2, 0.5, z))

    def faces2(z):
        ok = inside(16, 12, z, gz * 4 - 4, gy * 4, *sizes[1], dead=(8, 12))
        return make_faces(z, 4, ok, s2, m2, tz2, ty2, tx2, w2, g2)

    faces2(1)
    tz2[0, 0] = 0.5 * (s2[0, 0] + s2[0, 1])
    tz2[1, 0] = 0.5 * (s2[1, 0] + s2[1, 1])
    each(2, 10, lambda z: put(first2, z, times(faces2(z), pair(f2, z))))
    faces2(10)
    copies += sent([pltpu.make_async_copy(ref, keeps.at[6 + i, :, 0:12, 0:16], sem.at[6 + i]) for i, ref in enumerate((tz2, ty2, tx2, w2))])
    each(3, 9, lambda z: put(v2, z, swept(z, 4, first2, f2, tz2, ty2, tx2, w2)))
    which = lanes(4) & 3
    for z in range(4):
        a, b = pair(v2, z + 4), pair(f2, z + 4)
        msg_out[0, z + 1] = jnp.where(
            which < 2, jnp.where(which == 0, a[0][0:4], a[1][0:4]), jnp.where(which == 2, b[0][0:4], b[1][0:4])
        )
    for z in range(2):
        a = residual(2 * z + 4, 4, v2, f2, tz2, ty2, tx2, g2)
        b = residual(2 * z + 5, 4, v2, f2, tz2, ty2, tx2, g2)
        put(buf2, z, add(a, b))
    for z in range(2):
        for c in (0, 1):
            stack[4 * c + 2 * z : 4 * c + 2 * z + 2] = 0.5 * pair_x(rows_paired(buf2, (c, z), 0, 2), 4)
    msg_out[0, 0, 0:1] = packed_row(stack[...])
    msg_out[0, 0, 1:2] = far_c[:, 0:LANES]
    msg_out[0, 0, 2:3] = far_c[:, LANES : 2 * LANES]
    msg_out[0, 0, 3:4] = jnp.zeros((1, LANES), F32)
    message = msg_out[0]
    for g in range(1, msg_out.shape[0]):
        msg_out[g] = message
    landed(copies)


def spread_kernel(column, cells, near, rows):
    ny, _, nz, _ = cells.shape
    for k in range(3):
        for g in range(nz):
            rows[k, g : g + 1] = column[g, 0, k : k + 1]
        q = rows[k]
        for p in range(ny):
            cells[p, k] = q
    mine = lax.axis_index("gz")
    for d in (-1, 0, 1):
        p = jnp.clip(mine + d, 0, nz - 1)
        on = jnp.where((mine + d >= 0) & (mine + d < nz), 1.0, 0.0)
        for z in range(4):
            near[4 * d + 4 + z] = on * column[p, z + 1]


def real_lanes(rows):
    return lanes(rows) < 64


def flip(q):
    return pltpu.roll(q, 64, 1)


def as_factors(q):
    real, other = real_lanes(q.shape[0]), flip(q)
    return jnp.where(real, q, other), jnp.where(real, other, -q)


def product(t, q):
    return t[0] * q + flip(t[1] * q)


def inverse_factors(diag):
    real, other = real_lanes(diag.shape[0]), flip(diag)
    inv = relax / (diag * diag + other * other)
    return jnp.where(real, diag, other) * inv, jnp.where(real, -other, diag) * inv


def shifted_rows(q, k):
    edge = q.shape[0] - 1 if k > 0 else 0
    return jnp.where(row_ids(q.shape[0]) == edge, 0.0, ahead_y(q, k))


def near_level3(planes):
    n = planes[0].shape[0]
    lane = lanes(n)
    low_z, low_y, x = (lane & 32) == 0, (lane & 16) == 0, lane & 15
    turned = [swap_x(q, 16) for q in planes]
    out = []
    for i, q in enumerate(planes[1:-1]):
        qz = swap_x(q, 32)
        out.append(
            (
                jnp.where(low_y, turned[i + 1], turned[i + 2]),
                jnp.where(low_y, turned[i], turned[i + 1]),
                jnp.where(low_z, qz, shifted_rows(qz, 1)),
                jnp.where(low_z, shifted_rows(qz, -1), qz),
                jnp.where(x == 15, 0.0, ahead_x(q, 1)),
                jnp.where(x == 0, 0.0, ahead_x(q, -1)),
            )
        )
    return out


def slot_lanes(lane, slot):
    return (lane & 78) | ((slot & 4) << 3) | ((slot & 2) << 3) | (slot & 1)


def slot_of(lane):
    return ((lane >> 3) & 4) | ((lane >> 3) & 2) | (lane & 1)


def near_level4(groups):
    n = groups[0].shape[0]
    lane = lanes(n)
    slot, x = slot_of(lane), lane & 14
    nxt, prv = slot_lanes(lane, slot + 1), slot_lanes(lane, slot + 7)
    zero = jnp.zeros_like(groups[0])
    up = [jnp.take_along_axis(q, nxt, axis=1) for q in groups] + [zero]
    down = [zero] + [jnp.take_along_axis(q, prv, axis=1) for q in groups]
    return [
        (
            jnp.where(slot == 7, up[i + 1], up[i]),
            jnp.where(slot == 0, down[i], down[i + 1]),
            shifted_rows(q, 1),
            shifted_rows(q, -1),
            jnp.where(x == 14, 0.0, ahead_x(q, 2)),
            jnp.where(x == 0, 0.0, ahead_x(q, -2)),
        )
        for i, q in enumerate(groups)
    ]


def set_level(here, near, m, t, w, g, p):
    diag = m
    for i, other in enumerate(near):
        face = 0.5 * (here + other)
        diag = diag + face
        t[2 * i, p], t[2 * i + 1, p] = as_factors(face)
    w[0, p], w[1, p] = inverse_factors(diag)
    if g is not None:
        g[0, p], g[1, p] = as_factors(diag)


def gathered_inflow(near, t, p):
    a = sum(t[2 * i, p] * q for i, q in enumerate(near[1:], 1)) + t[0, p] * near[0]
    b = sum(t[2 * i + 1, p] * q for i, q in enumerate(near[1:], 1)) + t[1, p] * near[0]
    return a + flip(b)


def factors(ref, p):
    return ref[0, p], ref[1, p]


def folded(planes):
    lane = lanes(planes[0].shape[0])
    for bit in (1, 16, 32):
        low = (lane & bit) == 0
        planes = [
            jnp.where(low, a, b) + swap_x(jnp.where(low, b, a), bit) for a, b in zip(planes[0::2], planes[1::2])
        ]
    return planes[0]


BATCH = 8


def batches(n, body):
    def run(i, carry):
        body(pl.multiple_of(i * BATCH, BATCH))
        return carry

    lax.fori_loop(0, n // BATCH, run, 0)


def level4(f4, s4, m4, t4):
    real = real_lanes(s4[0].shape[0])
    start = []
    for k, near in enumerate(near_level4(s4)):
        faces = [0.5 * (s4[k] + other) for other in near]
        fa = inverse_factors(sum(faces[1:]) + faces[0] + m4[k])
        start.append(product(fa, f4[k]))
        for i, face in enumerate(faces):
            q = product(fa, face)
            other = flip(q)
            t4[2 * i, k] = jnp.where(real, q, other)
            t4[2 * i + 1, k] = jnp.where(real, -other, q)
    turned = [flip(q) for q in start]
    e, o = start, turned
    for sweep in range(COARSE_SWEEPS - 1):
        pairs = list(zip(near_level4(e), near_level4(o)))
        e_next, o_next = [], []
        for k, (ne, no) in enumerate(pairs):
            ab = [(t4[2 * i, k], t4[2 * i + 1, k]) for i in range(6)]
            x = [a * p + b * q for (a, b), p, q in zip(ab, ne, no)]
            y = [a * q - b * p for (a, b), p, q in zip(ab, ne, no)]
            e_next.append((keep * e[k] + start[k] + x[0]) + (x[1] + x[2]) + (x[3] + x[4]) + x[5])
            o_next.append((keep * o[k] + turned[k] + y[0]) + (y[1] + y[2]) + (y[3] + y[4]) + y[5])
        e, o = e_next, o_next
    return e


def coarse_solve(counts, cells, t3, w3, g3, t4, s3, va, vb, ea):
    nz, ny = counts
    groups = ny // 8
    zero = jnp.zeros((nz, LANES), F32)
    s3[0] = zero
    s3[ny + 1] = zero
    for ref in (va, vb):
        for p in (0, 1, 2, ny + 3, ny + 4, ny + 5):
            ref[p] = zero
    for p in (0, 1, ny + 2, ny + 3):
        for i in range(12):
            t3[i, p] = zero
        w3[0, p] = zero
        w3[1, p] = zero

    def load(p0):
        for i in range(BATCH):
            s3[p0 + i + 1] = cells[p0 + i, 1]

    batches(ny, load)

    def setup(p0):
        planes = [s3[p0 + i] for i in range(BATCH + 2)]
        for i, near in enumerate(near_level3(planes)):
            p = p0 + i
            set_level(planes[i + 1], near, cells[p, 2], t3, w3, g3, p + 2)
            va[p + 3] = product(factors(w3, p + 2), cells[p, 0])

    batches(ny, setup)
    s4 = [0.125 * folded([cells[8 * k + j, 1] for j in range(8)]) for k in range(groups)]
    m4 = [0.5 * folded([cells[8 * k + j, 2] for j in range(8)]) for k in range(groups)]

    def swept3(here, near, p):
        gain = cells[jnp.clip(p, 0, ny - 1), 0] + gathered_inflow(near, t3, p + 2)
        return keep * here + product(factors(w3, p + 2), gain)

    def pre(p0):
        planes = [va[p0 + i + 2] for i in range(BATCH + 2)]
        for i, near in enumerate(near_level3(planes)):
            p = p0 + i
            gain = cells[p, 0] + gathered_inflow(near, t3, p + 2)
            vb[p + 3] = keep * planes[i + 1] + product(factors(w3, p + 2), gain)

    batches(ny, pre)

    def restrict(p0):
        planes = [vb[p0 + i + 2] for i in range(BATCH + 2)]
        gains = []
        for i, near in enumerate(near_level3(planes)):
            p = p0 + i
            gain = cells[p, 0] + gathered_inflow(near, t3, p + 2)
            gains.append(gain - product(factors(g3, p + 2), planes[i + 1]))
        ea[p0 // BATCH] = 0.5 * folded(gains)

    batches(ny, restrict)
    for k, q in enumerate(level4([ea[k] for k in range(groups)], s4, m4, t4)):
        ea[k] = q

    mine = lax.axis_index("gy")
    lane = lanes(nz)
    planes = []
    for d in range(-3, 4):
        p = mine + d
        on = jnp.where((p >= 0) & (p < ny), 1.0, 0.0)
        q = jnp.clip(p, 0, ny - 1)
        corr = jnp.take_along_axis(ea[q // 8], slot_lanes(lane, jnp.full((nz, LANES), q % 8, jnp.int32)), axis=1)
        planes.append(vb[p + 3] + on * corr)
    for reach in (2, 1):
        planes = [
            swept3(here, near, mine + d)
            for d, here, near in zip(range(-reach, reach + 1), planes[1:-1], near_level3(planes))
        ]
    return planes


def up_kernel(counts, cells, cmid, cleft, cright, *rest):
    kept1, kept0, out, rest = rest[0], rest[1], rest[2], rest[3:]
    tz2, ty2, tx2, w2, v1, f1, tz1, ty1, tx1, w1, v0, f0, tz0, ty0, tx0, w0 = rest[:16]
    t3, w3, g3, t4, s3, va, vb, ea, near, a2, b2, f2, e1, a1, b1, e0, a0, b0, done, sem = rest[16:]
    copies = []
    for i, dst in enumerate(rest[:16]):
        src, dst = (
            (kept1.at[6 + i, :, 0:12, 0:16], dst) if i < 4
            else (kept1.at[i - 4], dst.at[:, KEPT1]) if i < 10
            else (kept0.at[i - 10], dst.at[:, KEPT0])
        )
        copies.append(pltpu.make_async_copy(src, dst, sem.at[i]))
    sent(copies)
    nz = counts[0]
    gz = lax.axis_index("gz")
    for d, q in enumerate(coarse_solve(counts, cells, t3, w3, g3, t4, s3, va, vb, ea)):
        near[d] = q

    lane4, zero4 = lanes(4), jnp.zeros((4, LANES), F32)

    def unpack(z):
        for ref in (a2, f2):
            for c in (0, 1):
                ref[c, z, 8:12] = zero4
        for lo, src in ((0, cmid), (4, cright), (12, cleft)):
            q = src[z]
            turned = {k: ahead_x(q, k) if k else q for k in range(-3, 4)}
            for k, (ref, c) in enumerate(((a2, 0), (a2, 1), (f2, 0), (f2, 1))):
                val = turned[k]
                for i in range(1, 4):
                    val = jnp.where((lane4 & 3) == i, turned[k - i], val)
                ref[c, z, lo : lo + 4] = val

    each(0, 12, unpack)
    r16, l16 = row_ids(16), lanes(16)
    cell = l16 // 8
    for dz in (-1, 0, 1):
        row = jnp.clip(gz + dz, 0, nz - 1)
        on = jnp.where((gz + dz >= 0) & (gz + dz < nz), 1.0, 0.0)
        before, own, after = (near[d, pl.ds(row, 1), :] * on for d in range(3))
        rows = jnp.where(r16 < 4, own, jnp.where(r16 < 8, after, jnp.where(r16 < 12, 0.0, before)))
        for c in (0, 1):
            for zz in (0, 1):
                corr = jnp.take_along_axis(rows, cell + 16 * ((r16 // 2) & 1) + (64 * c + 32 * zz), axis=1)
                for z in (4 * dz + 4 + 2 * zz, 4 * dz + 5 + 2 * zz):
                    a2[c, z] = a2[c, z] + corr

    landed(copies)
    each(1, 11, lambda z: put(b2, z, swept(z, 4, a2, f2, tz2, ty2, tx2, w2)))
    each(2, 10, lambda z: put(a2, z, swept(z, 4, b2, f2, tz2, ty2, tx2, w2)))

    def widen1(z):
        for c in (0, 1):
            q = a2[c, z]
            for k in (0, 1):
                e1.at[c, z][pl.ds(k, 8, stride=2), :] = q[0:8]
                e1.at[c, z][pl.ds(16 + k, 4, stride=2), :] = q[12:16]

    each(2, 10, widen1)
    def correct1(z):
        e = pair(e1, z)
        for k in (2 * z, 2 * z + 1):
            put(a1, k, add(pair(v1, k), e))

    each(3, 9, correct1)
    for k, z in ((5, 2), (18, 9)):
        put(a1, k, add(pair(v1, k), pair(e1, z)))
    each(6, 18, lambda z: put(b1, z, swept(z, 2, a1, f1, tz1, ty1, tx1, w1)))
    each(7, 17, lambda z: put(a1, z, swept(z, 2, b1, f1, tz1, ty1, tx1, w1)))

    def widen0(z):
        for c in (0, 1):
            q = a1[c, z]
            for k in (0, 1):
                e0.at[c, z][pl.ds(k, 8, stride=2), :] = q[0:8]
                e0.at[c, z][pl.ds(16 + k, 2, stride=2), :] = q[8:10]
                e0.at[c, z][pl.ds(20 + k, 2, stride=2), :] = q[22:24]

    each(7, 17, widen0)
    def correct0(z):
        e = pair(e0, z)
        for k in (2 * z - 12, 2 * z - 11):
            put(a0, k, add(pair(v0, k), e))

    each(7, 17, correct0)
    each(3, 21, lambda z: put(b0, z, swept(z, 1, a0, f0, tz0, ty0, tx0, w0)))

    def last(z):
        q = swept(z, 1, b0, f0, tz0, ty0, tx0, w0)
        done[0, z - 4] = q[0][0:16]
        done[1, z - 4] = q[1][0:16]

    copies = []
    for i in range(4):
        part = slice(4 * i, 4 * i + 4)
        for z in range(4):
            last(4 * i + z + 4)
        copies += sent([pltpu.make_async_copy(done.at[:, part], out.at[:, part], sem.at[16 + i])])
    landed(copies)


def run(kernel, name, args, outs, scratch, smem=(), far_in=(), far_out=(), copies=0, vmem=32 * 1024 * 1024):
    def specs(n, smem, far):
        spaces = [pltpu.SMEM if i in smem else pltpu.HBM if i in far else pltpu.VMEM for i in range(n)]
        return [pl.BlockSpec(memory_space=space) for space in spaces]

    return pl.pallas_call(
        kernel,
        name=name,
        out_shape=[jax.ShapeDtypeStruct(s, F32) for s in outs],
        in_specs=specs(len(args), smem, far_in),
        out_specs=specs(len(outs), (), far_out),
        scratch_shapes=[pltpu.VMEM(s, F32) if isinstance(s, tuple) else s for s in scratch]
        + ([pltpu.SemaphoreType.DMA((copies,))] if copies else []),
        compiler_params=pltpu.CompilerParams(vmem_limit_bytes=vmem),
    )(*args)


def traded(axis, top, bottom):
    n = lax.axis_size(axis)
    even = lax.axis_index(axis) % 2 == 0
    far = [(i, j) for k in range(2, n, 2) for i, j in ((k - 1, k), (k, k - 1))]
    close = [(i, i ^ 1) for i in range(n) if i ^ 1 < n]
    same = top is bottom
    to_far = top if same else jnp.where(even, bottom, top)
    to_close = top if same else jnp.where(even, top, bottom)
    from_far = lax.ppermute(to_far, axis, far)
    from_close = lax.ppermute(to_close, axis, close)
    return jnp.where(even, from_far, from_close), jnp.where(even, from_close, from_far)


def around(block, axis, dim, width):
    size = block.shape[dim]
    if width == size:
        return traded(axis, block, block)
    return traded(
        axis,
        lax.slice_in_dim(block, size - width, size, axis=dim),
        lax.slice_in_dim(block, 0, width, axis=dim),
    )


def window(block, dim, width):
    before, after = around(block, "gz", dim, width)
    mid = jnp.concatenate([before, block, after], axis=dim)
    left, right = around(mid, "gy", dim + 1, width)
    return mid, left, right


def body(source, labels, phase_table):
    nz, ny = lax.axis_size("gz"), lax.axis_size("gy")

    channel = lax.broadcasted_iota(jnp.int32, (3, *labels.shape), 0)
    padded = jnp.pad(source, ((0, 1), (0, 0), (0, 0), (0, 0)))
    base = lax.optimization_barrier(jnp.where(channel == 2, labels.astype(F32)[None], padded))
    zb, za = around(base, "gz", 1, 4)
    left, right = around(jnp.concatenate([zb, base, za], axis=1), "gy", 2, 4)

    near_c, far_c, values = run(
        coeff_kernel, "coefficients", (base, phase_table),
        [(2, 8, 8, LANES), (1, 2 * LANES), (PHASES, 4, 8, LANES)],
        [(4, 8, 16, LANES), (4, 8, 8, LANES), (4, 4, 4, LANES), (2, 8, LANES)], smem=(1,),
    )
    win, win2 = (2, 24, 24, LANES), (2, 12, 16, LANES)
    win0 = (2, KEPT0.stop - KEPT0.start, 24, LANES)
    win1 = (2, KEPT1.stop - KEPT1.start, 24, LANES)
    msg, state0 = run(
        lambda *refs: fine_kernel((16 * nz, 16 * ny), *refs), "fine_down",
        (base, zb, za, left, right, values, near_c),
        [(3, 8, 8, LANES), (20, *win0)],
        [win] * 6 + [(24, 24, LANES)] + [win] * 4 + [(2, 8, 24, LANES)],
        far_out=(1,), copies=6, vmem=MOST_VMEM,
    )
    msg, state1 = run(
        lambda *refs: middle_kernel(((8 * nz, 8 * ny), (4 * nz, 4 * ny)), *refs), "middle_down",
        (*window(msg, 1, 8), far_c),
        [(nz, *MESSAGE), (32, *win1)],
        [win] * 6 + [win2] * 4 + [win] * 4 + [(2, 12, 24, LANES)] + [win2] * 6 + [(2, 2, 16, LANES), (8, LANES)],
        far_out=(1,), copies=10, vmem=MOST_VMEM,
    )
    column = lax.all_to_all(msg, "gz", 0, 0)
    cells, cmid = run(
        spread_kernel, "spread", (column,), [(ny, 3, nz, LANES), (12, 4, LANES)], [(3, nz, LANES)],
    )
    cells = lax.all_to_all(cells, "gy", 0, 0)
    cwin = (cmid, *around(cmid, "gy", 1, 4))

    def whole(n, pad):
        return (n, ny + 2 * pad, nz, LANES)

    small = (ny // 8, nz, LANES)
    return run(
        lambda *refs: up_kernel((nz, ny), *refs), "coarse_and_up",
        (cells, *cwin, state1, state0),
        [(2, 16, 16, LANES)],
        [win2] * 4 + [win] * 12
        + [whole(12, 2), whole(2, 2), whole(2, 2), (12, *small)]
        + [whole(1, 1)[1:]] + [whole(1, 3)[1:]] * 2 + [small, (3, nz, LANES)]
        + [win2] * 3 + [(2, 12, 24, LANES), win, win, win, win, win, (2, 16, 16, LANES)],
        far_in=(4, 5), far_out=(0,), copies=20, vmem=MOST_VMEM,
    )[0]


def solution(mesh):
    in_specs = (P(None, "gz", "gy", None), P("gz", "gy", None), P())
    out_specs = P(None, "gz", "gy", None)
    return jax.shard_map(body, mesh=mesh, in_specs=in_specs, out_specs=out_specs, check_vma=False)
```

```python
import jax
import jax.numpy as jnp
from jax import lax
from jax.experimental import pallas as pl
from jax.experimental.pallas import tpu as pltpu
from jax.sharding import PartitionSpec as P

PHASES = 4
COARSE_SWEEPS = 8
LANES = 128
relax = 0.7
keep = 1.0 - relax
mass_scale = 0.01
F32 = jnp.float32
MESSAGE = (5, 4, LANES)
MOST_VMEM = 51 * 1024 * 1024


def lanes(rows):
    return lax.broadcasted_iota(jnp.int32, (rows, LANES), 1)


def row_ids(rows):
    return lax.broadcasted_iota(jnp.int32, (rows, LANES), 0)


def ahead_x(q, k):
    return pltpu.roll(q, (-k) % LANES, 1)


def ahead_y(q, k):
    return pltpu.roll(q, (-k) % q.shape[0], 0)


def pair_x(q, k):
    return q + swap_x(q, k)


def swap_x(q, k):
    return jnp.where((lanes(q.shape[0]) & k) == 0, ahead_x(q, k), ahead_x(q, -k))


def interleave(re, im):
    return jnp.where((lanes(re.shape[0]) & 1) == 0, re, im)


def separate(q):
    even = (lanes(q.shape[0]) & 1) == 0
    return jnp.where(even, q, ahead_x(q, -1)), jnp.where(even, ahead_x(q, 1), q)


def each(lo, hi, body, step=4):
    full = (hi - lo) // step

    def run(i, carry):
        for j in range(step):
            body(lo + i * step + j)
        return carry

    lax.fori_loop(0, full, run, 0)
    for z in range(lo + full * step, hi):
        body(z)


def sent(copies):
    for copy in copies:
        copy.start()
    return copies


def landed(copies):
    for copy in copies:
        copy.wait()


def times(t, q):
    return t[0] * q[0] - t[1] * q[1], t[0] * q[1] + t[1] * q[0]


def pair(ref, z):
    return ref[0, z], ref[1, z]


def put(ref, z, q):
    ref[0, z] = q[0]
    ref[1, z] = q[1]


def add(*terms):
    return sum(t[0] for t in terms[1:]) + terms[0][0], sum(t[1] for t in terms[1:]) + terms[0][1]


def both(fn, q, k):
    return fn(q[0], k), fn(q[1], k)


def inside(rows, wrap, z, first_z, first_y, size_z, size_y, dead=()):
    r = row_ids(rows)
    y = jnp.where(r >= wrap, r - rows, r) + first_y
    ok = (y >= 0) & (y < size_y)
    plane = jnp.full((rows, LANES), first_z + z, jnp.int32)
    ok = ok & (plane >= 0) & (plane < size_z)
    if dead:
        ok = ok & ((r < dead[0]) | (r >= dead[1]))
    return ok


def make_faces(z, shift, ok, s, m, tz, ty, tx, w, g=None):
    lane = lanes(s.shape[2])
    last = lane >= LANES - shift
    initial = lane < shift
    diag = []
    for c in (0, 1):
        here = s[c, z]
        up = 0.5 * (here + s[c, z + 1])
        down = 0.5 * (here + s[c, z - 1])
        side = 0.5 * (here + ahead_y(here, 1))
        right = 0.5 * (here + jnp.where(last, 0.0, ahead_x(here, shift)))
        left = 0.5 * (here + jnp.where(initial, 0.0, ahead_x(here, -shift)))
        tz[c, z] = up
        ty[c, z] = side
        tx[c, z] = jnp.where(last, 0.0, right)
        diag.append(m[c, z] + (up + down) + (side + ahead_y(side, -1)) + (right + left))
    inv = jnp.where(ok, relax / (diag[0] * diag[0] + diag[1] * diag[1]), 0.0)
    q = (diag[0] * inv, -(diag[1] * inv))
    put(w, z, q)
    if g is not None:
        put(g, z, diag)
    return q


def inflow(z, shift, v, tz, ty, tx):
    here = pair(v, z)
    side, right = pair(ty, z), pair(tx, z)
    return add(
        times(pair(tz, z), pair(v, z + 1)),
        times(pair(tz, z - 1), pair(v, z - 1)),
        times(side, both(ahead_y, here, 1)),
        both(ahead_y, times(side, here), -1),
        times(right, both(ahead_x, here, shift)),
        both(ahead_x, times(right, here), -shift),
    )


def swept(z, shift, v, f, tz, ty, tx, w):
    here = pair(v, z)
    step = times(pair(w, z), add(pair(f, z), inflow(z, shift, v, tz, ty, tx)))
    return keep * here[0] + step[0], keep * here[1] + step[1]


def residual(z, shift, v, f, tz, ty, tx, g):
    out = times(pair(g, z), pair(v, z))
    gain = add(pair(f, z), inflow(z, shift, v, tz, ty, tx))
    return gain[0] - out[0], gain[1] - out[1]


def rows_paired(buf, at, start, count):
    plane = buf.at[at]
    return plane[pl.ds(start, count, stride=2), :] + plane[pl.ds(start + 1, count, stride=2), :]


def packed_row(stack):
    lane, row = lanes(8), row_ids(8)
    cells = jnp.take_along_axis(stack, 8 * (lane % 16), axis=1)
    return jnp.sum(jnp.where(lane // 16 == row, cells, 0.0), axis=0, keepdims=True)


def lookup(lab, val):
    return [
        jnp.where(lab == 0, val[0][c], jnp.where(lab == 1, val[1][c], jnp.where(lab == 2, val[2][c], val[3][c])))
        for c in range(4)
    ]


def coeff_kernel(base, table, near_out, far_out, values_out, buf, c1, c2, stack):
    val = [[table[p, c] * F32(1.0 if c < 2 else mass_scale) for c in range(4)] for p in range(PHASES)]
    for p in range(PHASES):
        for c in range(4):
            values_out[p, c] = jnp.full((8, LANES), val[p][c], F32)
    for z in range(8):
        a, b = lookup(base[2, 2 * z], val), lookup(base[2, 2 * z + 1], val)
        for c in range(4):
            buf[c, z] = a[c] + b[c]
    for z in range(8):
        for c in range(4):
            c1[c, z] = pair_x(rows_paired(buf, (c, z), 0, 8), 1) * (0.125 if c < 2 else 0.5)
    for z in range(8):
        near_out[0, z] = interleave(c1[0, z], c1[1, z])
        near_out[1, z] = interleave(c1[2, z], c1[3, z])
    for c in range(4):
        scale = 0.125 if c < 2 else 0.5
        for z in range(4):
            buf[c, z, 0:8] = c1[c, 2 * z] + c1[c, 2 * z + 1]
        for z in range(4):
            c2[c, z] = pair_x(rows_paired(buf, (c, z), 0, 4), 2) * scale
        for z in range(2):
            buf[c, 4 + z, 0:4] = c2[c, 2 * z] + c2[c, 2 * z + 1]
        for z in range(2):
            stack[c // 2, (c % 2) * 4 + 2 * z : (c % 2) * 4 + 2 * z + 2] = (
                pair_x(rows_paired(buf, (c, 4 + z), 0, 2), 4) * scale
            )
    far_out[:, 0:LANES] = packed_row(stack[0])
    far_out[:, LANES : 2 * LANES] = packed_row(stack[1])


KEPT0 = slice(2, 22)
KEPT1 = slice(5, 19)


def fine_kernel(
    sizes, base, zb, za, left, right, values, near_c, msg_out, *rest
):
    keeps, v, f, tz, ty, tx, w, lab, s, m, g, first, buf, sem = rest
    first_z = lax.axis_index("gz") * 16 - 4
    first_y = lax.axis_index("gy") * 16

    def load(z, own, k):
        for c, dst in enumerate((f.at[0, z], f.at[1, z], lab.at[z])):
            dst[0:16] = own[c, k]
            dst[16:20] = right[c, z]
            dst[20:24] = left[c, z]
        ok = inside(24, 20, z, first_z, first_y, *sizes)
        val = [[values[p, c] for c in range(4)] for p in range(PHASES)]
        for r in (slice(0, 8), slice(8, 16), slice(16, 24)):
            got = lookup(lab[z, r], val)
            for c in (0, 1):
                s[c, z, r] = jnp.where(ok[r], got[c], 0.0)
                m[c, z, r] = got[2 + c]

    for z in range(4):
        load(z, zb, z)
        load(z + 20, za, z)
    each(0, 16, lambda z: load(z + 4, base, z))

    def faces(z):
        ok = inside(24, 20, z, first_z, first_y, *sizes)
        put(first, z, times(make_faces(z, 1, ok, s, m, tz, ty, tx, w, g), pair(f, z)))

    each(1, 23, faces)

    def kept(i, ref):
        return pltpu.make_async_copy(ref.at[:, KEPT0], keeps.at[i], sem.at[i])

    copies = sent([kept(i, ref) for i, ref in enumerate((v, f, tz, ty, tx, w)) if i])
    each(2, 22, lambda z: put(v, z, swept(z, 1, first, f, tz, ty, tx, w)))
    copies += sent([kept(0, v)])

    def restrict(z):
        a = residual(2 * z + 4, 1, v, f, tz, ty, tx, g)
        b = residual(2 * z + 5, 1, v, f, tz, ty, tx, g)
        put(buf, z, add(a, b))

    each(0, 8, restrict, 4)

    def finish(z):
        re, im = (0.5 * pair_x(rows_paired(buf, (c, z), 0, 8), 1) for c in (0, 1))
        msg_out[2, z] = interleave(re, im)
        msg_out[0, z] = near_c[0, z]
        msg_out[1, z] = near_c[1, z]

    each(0, 8, finish)
    landed(copies)


def middle_kernel(
    sizes, mid, left, right, far_c,
    msg_out, *rest
):
    keeps, rest = rest[0], rest[1:]
    v, f, tz, ty, tx, w, tz2, ty2, tx2, w2, s, m, g, first, buf, s2, m2, f2, g2, first2, v2, buf2, stack, sem = rest
    gz, gy = lax.axis_index("gz"), lax.axis_index("gy")

    def load(z):
        for lo, src in ((0, mid), (8, right), (16, left)):
            for i, ref in enumerate((s, m, f)):
                re, im = separate(src[i, z])
                ref[0, z, lo : lo + 8] = re
                ref[1, z, lo : lo + 8] = im

    each(0, 24, load)

    def faces(z):
        ok = inside(24, 16, z, gz * 8 - 8, gy * 8, *sizes[0])
        put(first, z, times(make_faces(z, 2, ok, s, m, tz, ty, tx, w, g), pair(f, z)))

    each(2, 22, faces)

    def kept(i, ref):
        return pltpu.make_async_copy(ref.at[:, KEPT1], keeps.at[i], sem.at[i])

    copies = sent([kept(i, ref) for i, ref in enumerate((v, f, tz, ty, tx, w)) if i])
    each(3, 21, lambda z: put(v, z, swept(z, 2, first, f, tz, ty, tx, w)))
    copies += sent([kept(0, v)])

    def coarser(dst, scale, z):
        for c in (0, 1):
            dst[c, z, 0:8] = scale * pair_x(rows_paired(buf, (c, z), 0, 8), 2)
            dst[c, z, 8:12] = jnp.zeros((4, LANES), F32)
            dst[c, z, 12:16] = scale * pair_x(rows_paired(buf, (c, z), 16, 4), 2)

    for src, dst, scale in ((s, s2, 0.125), (m, m2, 0.5)):
        each(0, 12, lambda z: put(buf, z, add(pair(src, 2 * z), pair(src, 2 * z + 1))))
        each(0, 12, lambda z: coarser(dst, scale, z))

    def restrict(z):
        put(buf, z, add(residual(2 * z, 2, v, f, tz, ty, tx, g), residual(2 * z + 1, 2, v, f, tz, ty, tx, g)))

    each(2, 10, restrict, 4)
    each(2, 10, lambda z: coarser(f2, 0.5, z))

    def faces2(z):
        ok = inside(16, 12, z, gz * 4 - 4, gy * 4, *sizes[1], dead=(8, 12))
        return make_faces(z, 4, ok, s2, m2, tz2, ty2, tx2, w2, g2)

    faces2(1)
    tz2[0, 0] = 0.5 * (s2[0, 0] + s2[0, 1])
    tz2[1, 0] = 0.5 * (s2[1, 0] + s2[1, 1])
    each(2, 10, lambda z: put(first2, z, times(faces2(z), pair(f2, z))))
    faces2(10)
    copies += sent([pltpu.make_async_copy(ref, keeps.at[6 + i, :, 0:12, 0:16], sem.at[6 + i]) for i, ref in enumerate((tz2, ty2, tx2, w2))])
    each(3, 9, lambda z: put(v2, z, swept(z, 4, first2, f2, tz2, ty2, tx2, w2)))
    which = lanes(4) & 3
    for z in range(4):
        a, b = pair(v2, z + 4), pair(f2, z + 4)
        msg_out[0, z + 1] = jnp.where(
            which < 2, jnp.where(which == 0, a[0][0:4], a[1][0:4]), jnp.where(which == 2, b[0][0:4], b[1][0:4])
        )
    for z in range(2):
        a = residual(2 * z + 4, 4, v2, f2, tz2, ty2, tx2, g2)
        b = residual(2 * z + 5, 4, v2, f2, tz2, ty2, tx2, g2)
        put(buf2, z, add(a, b))
    for z in range(2):
        for c in (0, 1):
            stack[4 * c + 2 * z : 4 * c + 2 * z + 2] = 0.5 * pair_x(rows_paired(buf2, (c, z), 0, 2), 4)
    msg_out[0, 0, 0:1] = packed_row(stack[...])
    msg_out[0, 0, 1:2] = far_c[:, 0:LANES]
    msg_out[0, 0, 2:3] = far_c[:, LANES : 2 * LANES]
    msg_out[0, 0, 3:4] = jnp.zeros((1, LANES), F32)
    message = msg_out[0]
    for g in range(1, msg_out.shape[0]):
        msg_out[g] = message
    landed(copies)


def spread_kernel(column, cells, near, rows):
    ny, _, nz, _ = cells.shape
    for k in range(3):
        for g in range(nz):
            rows[k, g : g + 1] = column[g, 0, k : k + 1]
        q = rows[k]
        for p in range(ny):
            cells[p, k] = q
    mine = lax.axis_index("gz")
    for d in (-1, 0, 1):
        p = jnp.clip(mine + d, 0, nz - 1)
        on = jnp.where((mine + d >= 0) & (mine + d < nz), 1.0, 0.0)
        for z in range(4):
            near[4 * d + 4 + z] = on * column[p, z + 1]


def real_lanes(rows):
    return lanes(rows) < 64


def flip(q):
    return pltpu.roll(q, 64, 1)


def as_factors(q):
    real, other = real_lanes(q.shape[0]), flip(q)
    return jnp.where(real, q, other), jnp.where(real, other, -q)


def product(t, q):
    return t[0] * q + flip(t[1] * q)


def inverse_factors(diag):
    real, other = real_lanes(diag.shape[0]), flip(diag)
    inv = relax / (diag * diag + other * other)
    return jnp.where(real, diag, other) * inv, jnp.where(real, -other, diag) * inv


def shifted_rows(q, k):
    edge = q.shape[0] - 1 if k > 0 else 0
    return jnp.where(row_ids(q.shape[0]) == edge, 0.0, ahead_y(q, k))


def near_level3(planes):
    n = planes[0].shape[0]
    lane = lanes(n)
    low_z, low_y, x = (lane & 32) == 0, (lane & 16) == 0, lane & 15
    turned = [swap_x(q, 16) for q in planes]
    out = []
    for i, q in enumerate(planes[1:-1]):
        qz = swap_x(q, 32)
        out.append(
            (
                jnp.where(low_y, turned[i + 1], turned[i + 2]),
                jnp.where(low_y, turned[i], turned[i + 1]),
                jnp.where(low_z, qz, shifted_rows(qz, 1)),
                jnp.where(low_z, shifted_rows(qz, -1), qz),
                jnp.where(x == 15, 0.0, ahead_x(q, 1)),
                jnp.where(x == 0, 0.0, ahead_x(q, -1)),
            )
        )
    return out


def slot_lanes(lane, slot):
    return (lane & 78) | ((slot & 4) << 3) | ((slot & 2) << 3) | (slot & 1)


def slot_of(lane):
    return ((lane >> 3) & 4) | ((lane >> 3) & 2) | (lane & 1)


def near_level4(groups):
    n = groups[0].shape[0]
    lane = lanes(n)
    slot, x = slot_of(lane), lane & 14
    nxt, prv = slot_lanes(lane, slot + 1), slot_lanes(lane, slot + 7)
    zero = jnp.zeros_like(groups[0])
    up = [jnp.take_along_axis(q, nxt, axis=1) for q in groups] + [zero]
    down = [zero] + [jnp.take_along_axis(q, prv, axis=1) for q in groups]
    return [
        (
            jnp.where(slot == 7, up[i + 1], up[i]),
            jnp.where(slot == 0, down[i], down[i + 1]),
            shifted_rows(q, 1),
            shifted_rows(q, -1),
            jnp.where(x == 14, 0.0, ahead_x(q, 2)),
            jnp.where(x == 0, 0.0, ahead_x(q, -2)),
        )
        for i, q in enumerate(groups)
    ]


def set_level(here, near, m, t, w, g, p):
    diag = m
    for i, other in enumerate(near):
        face = 0.5 * (here + other)
        diag = diag + face
        t[2 * i, p], t[2 * i + 1, p] = as_factors(face)
    w[0, p], w[1, p] = inverse_factors(diag)
    if g is not None:
        g[0, p], g[1, p] = as_factors(diag)


def gathered_inflow(near, t, p):
    a = sum(t[2 * i, p] * q for i, q in enumerate(near[1:], 1)) + t[0, p] * near[0]
    b = sum(t[2 * i + 1, p] * q for i, q in enumerate(near[1:], 1)) + t[1, p] * near[0]
    return a + flip(b)


def factors(ref, p):
    return ref[0, p], ref[1, p]


def folded(planes):
    lane = lanes(planes[0].shape[0])
    for bit in (1, 16, 32):
        low = (lane & bit) == 0
        planes = [
            jnp.where(low, a, b) + swap_x(jnp.where(low, b, a), bit) for a, b in zip(planes[0::2], planes[1::2])
        ]
    return planes[0]


BATCH = 8


def batches(n, body):
    def run(i, carry):
        body(pl.multiple_of(i * BATCH, BATCH))
        return carry

    lax.fori_loop(0, n // BATCH, run, 0)


def level4(f4, s4, m4, t4):
    real = real_lanes(s4[0].shape[0])
    start = []
    for k, near in enumerate(near_level4(s4)):
        faces = [0.5 * (s4[k] + other) for other in near]
        fa = inverse_factors(sum(faces[1:]) + faces[0] + m4[k])
        start.append(product(fa, f4[k]))
        for i, face in enumerate(faces):
            q = product(fa, face)
            other = flip(q)
            t4[2 * i, k] = jnp.where(real, q, other)
            t4[2 * i + 1, k] = jnp.where(real, -other, q)
    turned = [flip(q) for q in start]
    e, o = start, turned
    for sweep in range(COARSE_SWEEPS - 1):
        pairs = list(zip(near_level4(e), near_level4(o)))
        e_next, o_next = [], []
        for k, (ne, no) in enumerate(pairs):
            ab = [(t4[2 * i, k], t4[2 * i + 1, k]) for i in range(6)]
            x = [a * p + b * q for (a, b), p, q in zip(ab, ne, no)]
            y = [a * q - b * p for (a, b), p, q in zip(ab, ne, no)]
            e_next.append((keep * e[k] + start[k] + x[0]) + (x[1] + x[2]) + (x[3] + x[4]) + x[5])
            o_next.append((keep * o[k] + turned[k] + y[0]) + (y[1] + y[2]) + (y[3] + y[4]) + y[5])
        e, o = e_next, o_next
    return e


def coarse_solve(counts, cells, t3, w3, g3, t4, s3, va, vb, ea):
    nz, ny = counts
    groups = ny // 8
    zero = jnp.zeros((nz, LANES), F32)
    s3[0] = zero
    s3[ny + 1] = zero
    for ref in (va, vb):
        for p in (0, 1, 2, ny + 3, ny + 4, ny + 5):
            ref[p] = zero
    for p in (0, 1, ny + 2, ny + 3):
        for i in range(12):
            t3[i, p] = zero
        w3[0, p] = zero
        w3[1, p] = zero

    def load(p0):
        for i in range(BATCH):
            s3[p0 + i + 1] = cells[p0 + i, 1]

    batches(ny, load)

    def setup(p0):
        planes = [s3[p0 + i] for i in range(BATCH + 2)]
        for i, near in enumerate(near_level3(planes)):
            p = p0 + i
            set_level(planes[i + 1], near, cells[p, 2], t3, w3, g3, p + 2)
            va[p + 3] = product(factors(w3, p + 2), cells[p, 0])

    batches(ny, setup)
    s4 = [0.125 * folded([cells[8 * k + j, 1] for j in range(8)]) for k in range(groups)]
    m4 = [0.5 * folded([cells[8 * k + j, 2] for j in range(8)]) for k in range(groups)]

    def swept3(here, near, p):
        gain = cells[jnp.clip(p, 0, ny - 1), 0] + gathered_inflow(near, t3, p + 2)
        return keep * here + product(factors(w3, p + 2), gain)

    def pre(p0):
        planes = [va[p0 + i + 2] for i in range(BATCH + 2)]
        for i, near in enumerate(near_level3(planes)):
            p = p0 + i
            gain = cells[p, 0] + gathered_inflow(near, t3, p + 2)
            vb[p + 3] = keep * planes[i + 1] + product(factors(w3, p + 2), gain)

    batches(ny, pre)

    def restrict(p0):
        planes = [vb[p0 + i + 2] for i in range(BATCH + 2)]
        gains = []
        for i, near in enumerate(near_level3(planes)):
            p = p0 + i
            gain = cells[p, 0] + gathered_inflow(near, t3, p + 2)
            gains.append(gain - product(factors(g3, p + 2), planes[i + 1]))
        ea[p0 // BATCH] = 0.5 * folded(gains)

    batches(ny, restrict)
    for k, q in enumerate(level4([ea[k] for k in range(groups)], s4, m4, t4)):
        ea[k] = q

    mine = lax.axis_index("gy")
    lane = lanes(nz)
    planes = []
    for d in range(-3, 4):
        p = mine + d
        on = jnp.where((p >= 0) & (p < ny), 1.0, 0.0)
        q = jnp.clip(p, 0, ny - 1)
        corr = jnp.take_along_axis(ea[q // 8], slot_lanes(lane, jnp.full((nz, LANES), q % 8, jnp.int32)), axis=1)
        planes.append(vb[p + 3] + on * corr)
    for reach in (2, 1):
        planes = [
            swept3(here, near, mine + d)
            for d, here, near in zip(range(-reach, reach + 1), planes[1:-1], near_level3(planes))
        ]
    return planes


def up_kernel(counts, cells, cmid, cleft, cright, *rest):
    kept1, kept0, out, rest = rest[0], rest[1], rest[2], rest[3:]
    tz2, ty2, tx2, w2, v1, f1, tz1, ty1, tx1, w1, v0, f0, tz0, ty0, tx0, w0 = rest[:16]
    t3, w3, g3, t4, s3, va, vb, ea, near, a2, b2, f2, e1, a1, b1, e0, a0, b0, done, sem = rest[16:]
    copies = []
    for i, dst in enumerate(rest[:16]):
        src, dst = (
            (kept1.at[6 + i, :, 0:12, 0:16], dst) if i < 4
            else (kept1.at[i - 4], dst.at[:, KEPT1]) if i < 10
            else (kept0.at[i - 10], dst.at[:, KEPT0])
        )
        copies.append(pltpu.make_async_copy(src, dst, sem.at[i]))
    sent(copies)
    nz = counts[0]
    gz = lax.axis_index("gz")
    for d, q in enumerate(coarse_solve(counts, cells, t3, w3, g3, t4, s3, va, vb, ea)):
        near[d] = q

    lane4, zero4 = lanes(4), jnp.zeros((4, LANES), F32)

    def unpack(z):
        for ref in (a2, f2):
            for c in (0, 1):
                ref[c, z, 8:12] = zero4
        for lo, src in ((0, cmid), (4, cright), (12, cleft)):
            q = src[z]
            turned = {k: ahead_x(q, k) if k else q for k in range(-3, 4)}
            for k, (ref, c) in enumerate(((a2, 0), (a2, 1), (f2, 0), (f2, 1))):
                val = turned[k]
                for i in range(1, 4):
                    val = jnp.where((lane4 & 3) == i, turned[k - i], val)
                ref[c, z, lo : lo + 4] = val

    each(0, 12, unpack)
    r16, l16 = row_ids(16), lanes(16)
    cell = l16 // 8
    for dz in (-1, 0, 1):
        row = jnp.clip(gz + dz, 0, nz - 1)
        on = jnp.where((gz + dz >= 0) & (gz + dz < nz), 1.0, 0.0)
        before, own, after = (near[d, pl.ds(row, 1), :] * on for d in range(3))
        rows = jnp.where(r16 < 4, own, jnp.where(r16 < 8, after, jnp.where(r16 < 12, 0.0, before)))
        for c in (0, 1):
            for zz in (0, 1):
                corr = jnp.take_along_axis(rows, cell + 16 * ((r16 // 2) & 1) + (64 * c + 32 * zz), axis=1)
                for z in (4 * dz + 4 + 2 * zz, 4 * dz + 5 + 2 * zz):
                    a2[c, z] = a2[c, z] + corr

    landed(copies)
    each(1, 11, lambda z: put(b2, z, swept(z, 4, a2, f2, tz2, ty2, tx2, w2)))
    each(2, 10, lambda z: put(a2, z, swept(z, 4, b2, f2, tz2, ty2, tx2, w2)))

    def widen1(z):
        for c in (0, 1):
            q = a2[c, z]
            for k in (0, 1):
                e1.at[c, z][pl.ds(k, 8, stride=2), :] = q[0:8]
                e1.at[c, z][pl.ds(16 + k, 4, stride=2), :] = q[12:16]

    each(2, 10, widen1)
    def correct1(z):
        e = pair(e1, z)
        for k in (2 * z, 2 * z + 1):
            put(a1, k, add(pair(v1, k), e))

    each(3, 9, correct1)
    for k, z in ((5, 2), (18, 9)):
        put(a1, k, add(pair(v1, k), pair(e1, z)))
    each(6, 18, lambda z: put(b1, z, swept(z, 2, a1, f1, tz1, ty1, tx1, w1)))
    each(7, 17, lambda z: put(a1, z, swept(z, 2, b1, f1, tz1, ty1, tx1, w1)))

    def widen0(z):
        for c in (0, 1):
            q = a1[c, z]
            for k in (0, 1):
                e0.at[c, z][pl.ds(k, 8, stride=2), :] = q[0:8]
                e0.at[c, z][pl.ds(16 + k, 2, stride=2), :] = q[8:10]
                e0.at[c, z][pl.ds(20 + k, 2, stride=2), :] = q[22:24]

    each(7, 17, widen0)
    def correct0(z):
        e = pair(e0, z)
        for k in (2 * z - 12, 2 * z - 11):
            put(a0, k, add(pair(v0, k), e))

    each(7, 17, correct0)
    each(3, 21, lambda z: put(b0, z, swept(z, 1, a0, f0, tz0, ty0, tx0, w0)))

    def last(z):
        q = swept(z, 1, b0, f0, tz0, ty0, tx0, w0)
        done[0, z - 4] = q[0][0:16]
        done[1, z - 4] = q[1][0:16]

    copies = []
    for i in range(4):
        part = slice(4 * i, 4 * i + 4)
        for z in range(4):
            last(4 * i + z + 4)
        copies += sent([pltpu.make_async_copy(done.at[:, part], out.at[:, part], sem.at[16 + i])])
    landed(copies)


def run(kernel, name, args, outs, scratch, smem=(), far_in=(), far_out=(), copies=0, vmem=32 * 1024 * 1024):
    def specs(n, smem, far):
        spaces = [pltpu.SMEM if i in smem else pltpu.HBM if i in far else pltpu.VMEM for i in range(n)]
        return [pl.BlockSpec(memory_space=space) for space in spaces]

    return pl.pallas_call(
        kernel,
        name=name,
        out_shape=[jax.ShapeDtypeStruct(s, F32) for s in outs],
        in_specs=specs(len(args), smem, far_in),
        out_specs=specs(len(outs), (), far_out),
        scratch_shapes=[pltpu.VMEM(s, F32) if isinstance(s, tuple) else s for s in scratch]
        + ([pltpu.SemaphoreType.DMA((copies,))] if copies else []),
        compiler_params=pltpu.CompilerParams(vmem_limit_bytes=vmem),
    )(*args)


def traded(axis, top, bottom):
    n = lax.axis_size(axis)
    even = lax.axis_index(axis) % 2 == 0
    far = [(i, j) for k in range(2, n, 2) for i, j in ((k - 1, k), (k, k - 1))]
    close = [(i, i ^ 1) for i in range(n) if i ^ 1 < n]
    same = top is bottom
    to_far = top if same else jnp.where(even, bottom, top)
    to_close = top if same else jnp.where(even, top, bottom)
    from_close = lax.ppermute(to_close, axis, close)
    from_far = lax.ppermute(to_far, axis, far)
    if same:
        odd = jnp.logical_not(even)
        return jnp.where(odd, from_close, from_far), jnp.where(odd, from_far, from_close)
    return jnp.where(even, from_far, from_close), jnp.where(even, from_close, from_far)


def around(block, axis, dim, width):
    size = block.shape[dim]
    if width == size:
        return traded(axis, block, block)
    return traded(
        axis,
        lax.slice_in_dim(block, size - width, size, axis=dim),
        lax.slice_in_dim(block, 0, width, axis=dim),
    )


def window(block, dim, width):
    before, after = around(block, "gz", dim, width)
    mid = jnp.concatenate([before, block, after], axis=dim)
    left, right = around(mid, "gy", dim + 1, width)
    return mid, left, right


def body(source, labels, phase_table):
    nz, ny = lax.axis_size("gz"), lax.axis_size("gy")

    channel = lax.broadcasted_iota(jnp.int32, (3, *labels.shape), 0)
    padded = jnp.pad(source, ((0, 1), (0, 0), (0, 0), (0, 0)))
    base = lax.optimization_barrier(jnp.where(channel == 2, labels.astype(F32)[None], padded))
    zb, za = around(base, "gz", 1, 4)
    left, right = around(jnp.concatenate([zb, base, za], axis=1), "gy", 2, 4)

    near_c, far_c, values = run(
        coeff_kernel, "coefficients", (base, phase_table),
        [(2, 8, 8, LANES), (1, 2 * LANES), (PHASES, 4, 8, LANES)],
        [(4, 8, 16, LANES), (4, 8, 8, LANES), (4, 4, 4, LANES), (2, 8, LANES)], smem=(1,),
    )
    win, win2 = (2, 24, 24, LANES), (2, 12, 16, LANES)
    win0 = (2, KEPT0.stop - KEPT0.start, 24, LANES)
    win1 = (2, KEPT1.stop - KEPT1.start, 24, LANES)
    msg, state0 = run(
        lambda *refs: fine_kernel((16 * nz, 16 * ny), *refs), "fine_down",
        (base, zb, za, left, right, values, near_c),
        [(3, 8, 8, LANES), (20, *win0)],
        [win] * 6 + [(24, 24, LANES)] + [win] * 4 + [(2, 8, 24, LANES)],
        far_out=(1,), copies=6, vmem=MOST_VMEM,
    )
    msg, state1 = run(
        lambda *refs: middle_kernel(((8 * nz, 8 * ny), (4 * nz, 4 * ny)), *refs), "middle_down",
        (*window(msg, 1, 8), far_c),
        [(nz, *MESSAGE), (32, *win1)],
        [win] * 6 + [win2] * 4 + [win] * 4 + [(2, 12, 24, LANES)] + [win2] * 6 + [(2, 2, 16, LANES), (8, LANES)],
        far_out=(1,), copies=10, vmem=MOST_VMEM,
    )
    column = lax.all_to_all(msg, "gz", 0, 0)
    cells, cmid = run(
        spread_kernel, "spread", (column,), [(ny, 3, nz, LANES), (12, 4, LANES)], [(3, nz, LANES)],
    )
    cells = lax.all_to_all(cells, "gy", 0, 0)
    cwin = (cmid, *around(cmid, "gy", 1, 4))

    def whole(n, pad):
        return (n, ny + 2 * pad, nz, LANES)

    small = (ny // 8, nz, LANES)
    return run(
        lambda *refs: up_kernel((nz, ny), *refs), "coarse_and_up",
        (cells, *cwin, state1, state0),
        [(2, 16, 16, LANES)],
        [win2] * 4 + [win] * 12
        + [whole(12, 2), whole(2, 2), whole(2, 2), (12, *small)]
        + [whole(1, 1)[1:]] + [whole(1, 3)[1:]] * 2 + [small, (3, nz, LANES)]
        + [win2] * 3 + [(2, 12, 24, LANES), win, win, win, win, win, (2, 16, 16, LANES)],
        far_in=(4, 5), far_out=(0,), copies=20, vmem=MOST_VMEM,
    )[0]


def solution(mesh):
    in_specs = (P(None, "gz", "gy", None), P("gz", "gy", None), P())
    out_specs = P(None, "gz", "gy", None)
    return jax.shard_map(body, mesh=mesh, in_specs=in_specs, out_specs=out_specs, check_vma=False)
```
